128 devices in a mesh: wide: 16 (over x, z_lo, core), narrow: 8 (over y, z_hi).
Axes of the slice: x: 4, y: 4, z: 4 (z_hi: 2, z_lo: 2; z = z_hi * 2 + z_lo), core: 2. Of those that a mesh axis runs over, the one named last changes fastest.
Arguments:
- pair_rep: bfloat16 [256, 256, 128], P('wide', 'narrow'), may hold values from -6 to 6
- cotangent: bfloat16 [256, 256, 128], P('wide', 'narrow'), may hold values from -6 to 6
- norm_gain: float32 [128], replicated, may hold values from 0.1 to 1.9
- proj_weight: bfloat16 [128, 512], replicated, may hold values from -0.5 to 0.5
- bias_weight: bfloat16 [128, 4], replicated, may hold values from -0.5 to 0.5
- out_weight: bfloat16 [128, 128], replicated, may hold values from -0.5 to 0.5
- residue_mask: int32 [256], replicated, may hold values 0 or 1
Outputs:
- d_pair: bfloat16 [256, 256, 128], P('wide', 'narrow')
- grad_proj: float32 [128, 512], replicated
- grad_bias: float32 [128, 4], replicated
- grad_out: float32 [128, 128], replicated
- grad_gain: float32 [128], replicated
The draws below stay inside these ranges and needn't reach their ends.
All inputs are finite; a program needn't handle non-finite values.
Results may differ from the reference program's by a relative error of at most 0.019.
Values may be sent and summed in bfloat16 or wider, within the bound.
No kernel may reach another device: no remote copies, remote signals or barrier semaphores. Data moves between devices by JAX's collectives and lax.ppermute only.
A program may use at most 128 MiB of HBM per device.

```python
import jax
import jax.numpy as jnp
from jax import lax

CZ = 128
HEADS = 4
HEAD_DIM = 32
ROWS = 16
RESIDUES = 256
N_WIDE = 16


def place_ends(result, key, least, high):
    longest = result.shape.index(max(result.shape))
    spots = []
    for shift in (0, 1):
        where = [jax.random.randint(jax.random.fold_in(key, axis), (), 0, length) for axis, length in enumerate(result.shape)]
        where[longest] = (where[longest] + shift) % result.shape[longest]
        spots.append(tuple(where))
    return result.at[spots[0]].set(least).at[spots[1]].set(high)


def steps_of(rng, dims, shards, smallest, top_value):
    factor_of, own = 1.0, jax.random.fold_in(rng, 6)
    for axis_at, shards_of in shards:
        draws = jnp.exp(jax.random.uniform(jax.random.fold_in(own, axis_at), (shards_of,), jnp.float32, smallest / len(shards), top_value / len(shards)))
        factor_of = factor_of * jnp.repeat(draws, dims[axis_at] // shards_of).reshape([-1 if axis == axis_at else 1 for axis in range(len(dims))])
    return factor_of


def noise(own_key, extent, width, most, cuts=(), kind=jnp.bfloat16):
    drawn = jax.random.normal(own_key, extent, jnp.float32) * width
    if len(cuts) > 0:
        drawn = steps_of(own_key, extent, cuts, -0.22, 0.18) * drawn
    return jnp.clip(drawn, min=-most, max=most).astype(kind)


def setup_inputs(seed: int = 0) -> dict:
    splits = jax.random.split(jax.random.key(seed), 8)
    pair_rep = noise(splits[0], (RESIDUES, RESIDUES, CZ), 1.0, 6.0, ((0, 16), (1, 8)))
    cotangent = noise(splits[1], (RESIDUES, RESIDUES, CZ), 1.0, 6.0, ((0, 16), (1, 8)))
    norm_gain = jnp.clip(1.0 + 0.18 * jax.random.normal(splits[2], (CZ,), jnp.float32), 0.1, 1.9)
    proj_weight = noise(splits[3], (CZ, 4 * HEADS * HEAD_DIM), CZ ** -0.5, 0.5)
    bias_weight = noise(splits[4], (CZ, HEADS), CZ ** -0.5, 0.5)
    out_weight = noise(splits[5], (HEADS * HEAD_DIM, CZ), (HEADS * HEAD_DIM) ** -0.5, 0.5)
    residue_mask = place_ends((jax.random.randint(splits[6], (RESIDUES,), 0, 8) < 7).astype(jnp.int32), jax.random.fold_in(splits[6], 1), 0, 1)
    return dict(pair_rep=pair_rep, cotangent=cotangent, norm_gain=norm_gain, proj_weight=proj_weight, bias_weight=bias_weight, out_weight=out_weight, residue_mask=residue_mask)


NORM_EPSILON = 1e-05
MASK_FILL = 1000000000.0

def normalize(pair_rep, norm_gain):
    widened = pair_rep.astype(jnp.float32)
    centre = lax.optimization_barrier(jnp.mean(widened, axis=-1, keepdims=True))
    centered = widened - centre
    inverse = lax.rsqrt(lax.optimization_barrier(jnp.mean(centered * centered, axis=-1, keepdims=True)) + NORM_EPSILON)
    normal_hat = centered * inverse
    normed = (normal_hat * norm_gain).astype(jnp.bfloat16)
    return (normed, normal_hat, inverse)

def reference(pair_rep, cotangent, norm_gain, proj_weight, bias_weight, out_weight, residue_mask):
    head_width = HEADS * HEAD_DIM
    score_scale = HEAD_DIM ** (-0.5)
    normed, normal_hat, inverse = normalize(pair_rep, norm_gain)
    flat_normed = normed.reshape(RESIDUES * RESIDUES, CZ)
    projected = jnp.dot(flat_normed, proj_weight, preferred_element_type=jnp.float32)
    projected = projected.reshape(RESIDUES, RESIDUES, 4 * head_width)
    head_shape = (RESIDUES, RESIDUES, HEADS, HEAD_DIM)
    queries = projected[..., :head_width].astype(jnp.bfloat16).reshape(head_shape)
    key_rows = projected[..., head_width:2 * head_width].astype(jnp.bfloat16).reshape(head_shape)
    value_rows = projected[..., 2 * head_width:3 * head_width].astype(jnp.bfloat16).reshape(head_shape)
    gating = jax.nn.sigmoid(projected[..., 3 * head_width:])
    pair_bias = jnp.dot(flat_normed, bias_weight, preferred_element_type=jnp.float32).astype(jnp.bfloat16)
    pair_bias = pair_bias.reshape(RESIDUES, RESIDUES, HEADS)
    bias_by_query = jnp.transpose(pair_bias, (1, 2, 0)).astype(jnp.float32)
    masking = (residue_mask.astype(jnp.float32) - 1.0) * MASK_FILL
    out_grad = jnp.dot(cotangent.reshape(-1, CZ), out_weight.T, preferred_element_type=jnp.float32)
    out_grad = out_grad.reshape(RESIDUES, RESIDUES, head_width)

    def per_column(carried, pieces):
        col_query, col_key, col_value, col_gate, col_grad = pieces
        query32 = col_query.astype(jnp.float32)
        key32 = col_key.astype(jnp.float32)
        value32 = col_value.astype(jnp.float32)
        logits = jnp.einsum('ihd,khd->ihk', query32, key32) * score_scale
        logits = logits + bias_by_query + masking
        row_max = lax.optimization_barrier(jnp.max(logits, axis=-1))
        log_total = row_max + jnp.log(lax.optimization_barrier(jnp.sum(jnp.exp(logits - row_max[..., None]), axis=-1)))
        soft = jnp.exp(logits - log_total[..., None])
        soft_bf = soft.astype(jnp.bfloat16)
        attended = jnp.einsum('ihk,khd->ihd', soft_bf.astype(jnp.float32), value32)
        attended = attended.reshape(RESIDUES, head_width)
        gated = (col_gate * attended).astype(jnp.bfloat16)
        d_att = (col_grad * col_gate).astype(jnp.bfloat16)
        d_gate = col_grad * attended * col_gate * (1.0 - col_gate)
        d_att4 = d_att.astype(jnp.float32).reshape(RESIDUES, HEADS, HEAD_DIM)
        row_delta = lax.optimization_barrier(jnp.sum(d_att4 * attended.reshape(RESIDUES, HEADS, HEAD_DIM), axis=-1))
        d_soft = jnp.einsum('ihd,khd->ihk', d_att4, value32)
        d_logits = (soft * (d_soft - row_delta[..., None])).astype(jnp.bfloat16)
        d_logit32 = d_logits.astype(jnp.float32)
        d_query = jnp.einsum('ihk,khd->ihd', d_logit32, key32) * score_scale
        block_logits = d_logit32.reshape(N_WIDE, ROWS, HEADS, RESIDUES)
        block_query = query32.reshape(N_WIDE, ROWS, HEADS, HEAD_DIM)
        key_parts = (jnp.einsum('bihk,bihd->bkhd', block_logits, block_query) * score_scale).astype(jnp.bfloat16)
        d_key = lax.optimization_barrier(jnp.sum(key_parts.astype(jnp.float32), axis=0))
        block_soft = soft_bf.astype(jnp.float32).reshape(N_WIDE, ROWS, HEADS, RESIDUES)
        block_grad = d_att4.reshape(N_WIDE, ROWS, HEADS, HEAD_DIM)
        value_parts = jnp.einsum('bihk,bihd->bkhd', block_soft, block_grad).astype(jnp.bfloat16)
        d_value = lax.optimization_barrier(jnp.sum(value_parts.astype(jnp.float32), axis=0))
        results = (gated, d_query.reshape(RESIDUES, head_width), d_key.reshape(RESIDUES, head_width), d_value.reshape(RESIDUES, head_width), d_gate)
        return (carried + d_logit32, results)
    columns = (jnp.swapaxes(queries, 0, 1), jnp.swapaxes(key_rows, 0, 1), jnp.swapaxes(value_rows, 0, 1), jnp.swapaxes(gating, 0, 1), jnp.swapaxes(out_grad, 0, 1))
    start_bias = jnp.zeros((RESIDUES, HEADS, RESIDUES), jnp.float32)
    bias_sum, outputs = lax.scan(per_column, start_bias, columns)
    gated, d_query, d_key, d_value, d_gate = [jnp.swapaxes(item, 0, 1) for item in outputs]
    grads = jnp.concatenate([d_query.astype(jnp.bfloat16), d_key.astype(jnp.bfloat16), d_value.astype(jnp.bfloat16), d_gate.astype(jnp.bfloat16)], axis=-1)
    bias_grad = jnp.transpose(bias_sum, (2, 0, 1)).astype(jnp.bfloat16)
    flat_grads = grads.reshape(-1, 4 * head_width)
    flat_bias = bias_grad.reshape(-1, HEADS)
    d_normed = jnp.dot(flat_grads, proj_weight.T, preferred_element_type=jnp.float32)
    d_normed = d_normed + jnp.dot(flat_bias, bias_weight.T, preferred_element_type=jnp.float32)
    grad_proj = jnp.dot(flat_normed.T, flat_grads, preferred_element_type=jnp.float32)
    grad_bias = jnp.dot(flat_normed.T, flat_bias, preferred_element_type=jnp.float32)
    grad_out = jnp.dot(gated.reshape(-1, head_width).T, cotangent.reshape(-1, CZ), preferred_element_type=jnp.float32)
    flat_hat = normal_hat.reshape(-1, CZ)
    grad_gain = lax.optimization_barrier(jnp.sum(d_normed * flat_hat, axis=0))
    d_hat = d_normed * norm_gain
    d_pair = inverse.reshape(-1, 1) * (d_hat - lax.optimization_barrier(jnp.mean(d_hat, axis=-1, keepdims=True)) - flat_hat * lax.optimization_barrier(jnp.mean(d_hat * flat_hat, axis=-1, keepdims=True)))
    d_pair = d_pair.reshape(RESIDUES, RESIDUES, CZ).astype(jnp.bfloat16)
    return (d_pair, grad_proj, grad_bias, grad_out, grad_gain)
```

```python
import jax
import jax.numpy as jnp
from jax import lax
from jax.experimental import pallas as pl
from jax.experimental.pallas import tpu as pltpu
from jax.sharding import PartitionSpec as P

NORM_EPSILON = 1e-05
MASK_FILL = 1000000000.0
BF = jnp.bfloat16
F32 = jnp.float32
BOTH = ("wide", "narrow")

ROWS = 16
COLS = 32
TILE = ROWS * COLS
N_WIDE = 16
N_NARROW = 8
DEVICES = N_WIDE * N_NARROW
LENGTH = 256
CH = 128
HEADS = 4
DIM = 32
IN_ROWS = 40
MID_ROWS = 24
OUT_ROWS = 16

NT = (((1,), (1,)), ((), ()))
NN = (((1,), (0,)), ((), ()))
TN = (((0,), (0,)), ((), ()))


def mm(a, b, dims=NN):
    return lax.dot_general(a, b, dims, preferred_element_type=F32)


def normal(x):
    centered = x - jnp.mean(x, axis=-1, keepdims=True)
    inverse = lax.rsqrt(jnp.mean(centered * centered, axis=-1, keepdims=True) + NORM_EPSILON)
    return centered * inverse, inverse


def lane_group(shape):
    return lax.broadcasted_iota(jnp.int32, shape, 1) // COLS


def pre_kernel(pair_ref, cot_ref, gain_ref, wbt_ref, send_ref, normed_ref, xs, cs):
    hat, _ = normal(pair_ref[...].astype(F32).reshape(TILE, CH))
    normed = (hat * gain_ref[...]).astype(BF)
    normed_ref[...] = normed
    xs[...] = normed.astype(F32)
    cs[...] = cot_ref[...].astype(F32).reshape(TILE, CH)
    bias = mm(wbt_ref[...], normed, NT)
    turned = [pltpu.roll(bias[:, b * CH : (b + 1) * CH], 64, 1) for b in range(4)]
    for h in range(HEADS):
        rows = []
        for b in range(4):
            rows += [bias[h : h + 1, b * CH : (b + 1) * CH], turned[b][h : h + 1]]
        chunk = jnp.concatenate(rows, axis=0).astype(BF)
        for col in range(COLS):
            send_ref[h * COLS + col, 32:40, :] = chunk
    for col in range(COLS):
        x = xs[pl.ds(col, ROWS, stride=COLS), :].astype(BF)
        c = cs[pl.ds(col, ROWS, stride=COLS), :].astype(BF)
        for h in range(HEADS):
            send_ref[h * COLS + col, 0:16, :] = x
            send_ref[h * COLS + col, 16:32, :] = c


def attention_kernel(
    recv_ref, wall_ref, ow_ref, mask_ref, send_ref, bias_s, sum_s, tail_s, grad_s, gout_s
):
    me = lax.axis_index("wide") * N_NARROW + lax.axis_index("narrow")
    head = me // COLS
    scale = DIM**-0.5
    weight = wall_ref[head]
    out_w = ow_ref[pl.ds(pl.multiple_of(head * DIM, DIM), DIM), :]
    group = lane_group((CH, CH))
    for half in range(2):
        for kq in range(2):
            acc = jnp.zeros((CH, CH), F32)
            for q in range(4):
                got = recv_ref[:, half * 4 + q, 32:40, :].astype(F32).reshape(CH, CH)
                shift = (q - kq) * COLS % CH
                acc = jnp.where(group == q, pltpu.roll(got, shift, 1) if shift else got, acc)
            bias_s.at[half][pl.ds(kq, CH, stride=2), :] = acc
    mask = mask_ref[...]
    zero = jnp.zeros((DIM, CH), BF)
    eye = (
        lax.broadcasted_iota(jnp.int32, (LENGTH, LENGTH), 0)
        == lax.broadcasted_iota(jnp.int32, (LENGTH, LENGTH), 1)
    ).astype(BF)

    for n in range(N_NARROW):
        x = recv_ref[:, n, 0:16, :].reshape(LENGTH, CH)
        cot = recv_ref[:, n, 16:32, :].reshape(LENGTH, CH)
        proj_t = mm(weight, x, NT)
        kv = mm(x, weight[DIM : 3 * DIM], NT).astype(BF)
        k_t = proj_t[DIM : 2 * DIM].astype(BF)
        v_t = proj_t[2 * DIM : 3 * DIM].astype(BF)
        out_grad = mm(out_w, cot, NT)
        dq, dg, gated = [], [], []
        dk = dv = None
        for half in range(2):
            part = slice(half * CH, (half + 1) * CH)
            q_t = proj_t[0:DIM, part].astype(BF)
            gate = jax.nn.sigmoid(proj_t[3 * DIM :, part])
            og = out_grad[:, part]
            da_t = (og * gate).astype(BF)
            logits = mm(kv, jnp.concatenate([q_t, zero], axis=0)) * scale
            logits = logits + bias_s[half] + mask
            top = jnp.max(logits, axis=0, keepdims=True)
            e = jnp.exp(logits - top)
            soft = e * (1.0 / jnp.sum(e, axis=0, keepdims=True))
            soft_bf = soft.astype(BF)
            att = mm(v_t, soft_bf)
            delta = jnp.sum(da_t.astype(F32) * att, axis=0, keepdims=True)
            d_soft = mm(kv, jnp.concatenate([zero, da_t], axis=0))
            d_log = (soft * (d_soft - delta)).astype(BF)
            if n == 0:
                sum_s[half] = d_log.astype(F32)
            else:
                sum_s[half] += d_log.astype(F32)
            dq.append(mm(k_t, d_log) * scale)
            dk_half = mm(q_t, d_log, NT)
            dv_half = mm(da_t, soft_bf, NT)
            dk = dk_half if half == 0 else dk + dk_half
            dv = dv_half if half == 0 else dv + dv_half
            dg.append(og * att * gate * (1.0 - gate))
            gated.append((gate * att).astype(BF))
        dq = jnp.concatenate(dq, axis=1)
        dg = jnp.concatenate(dg, axis=1)
        gated = jnp.concatenate(gated, axis=1)
        grads_t = jnp.concatenate([dq, dk * scale, dv, dg], axis=0).astype(BF)
        part = mm(grads_t, x)
        out_part = mm(gated, cot)
        if n == 0:
            grad_s[...] = part
            gout_s[...] = out_part
        else:
            grad_s[...] += part
            gout_s[...] += out_part
        grads = mm(eye, grads_t, NT).astype(BF)
        send_ref[:, n, 0:16, :] = grads.reshape(N_WIDE, ROWS, CH)

    group = lane_group((64, CH))
    tail_s[...] = jnp.zeros_like(tail_s)
    for n in range(N_NARROW):
        half, q = n // 4, n % 4
        acc = jnp.zeros((64, CH), F32)
        for kq in range(4):
            got = sum_s.at[half][pl.ds(kq, 64, stride=4), :]
            shift = (kq - q) * COLS % CH
            acc = jnp.where(group == kq, pltpu.roll(got, shift, 1) if shift else got, acc)
        for w in range(N_WIDE):
            at = (w * N_NARROW + n) * 8
            tail_s[at : at + 4, :] = acc[w * 4 : (w + 1) * 4, :]
    tail_s[pl.ds(4, DEVICES, stride=8), :] = jnp.transpose(grad_s[...])
    out_part = gout_s[...]
    for r in range(4):
        tail_s[pl.ds(5 + 8 * r, DIM, stride=32), :] = out_part
    tail = tail_s[...].astype(BF).reshape(N_WIDE, N_NARROW, 8, CH)
    send_ref[:, :, 16:24, :] = tail


def reduce_kernel(recv_ref, normed_ref, send_ref, bias_ref):
    sums = [
        jnp.sum(recv_ref[h * COLS : (h + 1) * COLS, 16:24, :].astype(F32), axis=0)
        for h in range(HEADS)
    ]
    blocks = [
        jnp.concatenate([sums[h][b : b + 1] for h in range(HEADS)], axis=0) for b in range(4)
    ]
    bias = jnp.concatenate(blocks, axis=1).astype(BF)
    bias = jnp.concatenate([bias, jnp.zeros_like(bias)], axis=0)
    bias_ref[...] = bias
    grad_bias = mm(bias, normed_ref[...])
    own = jnp.concatenate([sums[h][4:5] for h in range(HEADS)], axis=0)
    group = lane_group((1, CH))
    rows = []
    for t in range(4):
        row = jnp.zeros((1, CH), F32)
        for h in range(HEADS):
            shift = (h - t) * COLS % CH
            got = own[h : h + 1]
            row = jnp.where(group == h, pltpu.roll(got, shift, 1) if shift else got, row)
        rows.append(row)
    rows += [sums[h][5:6] for h in range(HEADS)]
    rows.append(grad_bias)
    chunk = jnp.concatenate(rows, axis=0).astype(BF)
    send_ref[...] = jnp.broadcast_to(chunk[None], (DEVICES, OUT_ROWS, CH))


def pair_kernel(recv_ref, bias_ref, pair_ref, gain_ref, wall_ref, wbt_ref, out_ref, ds):
    total = jnp.zeros((TILE, CH), F32)
    for h in range(HEADS):
        g = recv_ref[h * COLS : (h + 1) * COLS, 0:16, :].reshape(TILE, CH)
        total = total + mm(g, wall_ref[h])
    ds[...] = total
    d_normed = jnp.concatenate([ds[pl.ds(r, COLS, stride=ROWS), :] for r in range(ROWS)], axis=0)
    d_normed = d_normed + mm(bias_ref[...], wbt_ref[...], TN)
    hat, inverse = normal(pair_ref[...].astype(F32).reshape(TILE, CH))
    d_hat = d_normed * gain_ref[...]
    d_pair = inverse * (
        d_hat
        - jnp.mean(d_hat, axis=-1, keepdims=True)
        - hat * jnp.mean(d_hat * hat, axis=-1, keepdims=True)
    )
    out_ref[...] = d_pair.astype(BF).reshape(ROWS, COLS, CH)


def final_kernel(
    recv_ref, pw_ref, wbt_ref, gain_ref, gp_ref, gb_ref, go_ref, gg_ref, vs
):
    vs[...] = recv_ref[...].astype(F32).reshape(DEVICES * OUT_ROWS, CH)
    dots = jnp.zeros((CH, CH), F32)
    for t in range(4):
        got = vs[pl.ds(t, CH, stride=OUT_ROWS), :]
        gp_ref[:, t * CH : (t + 1) * CH] = got
        dots = dots + got * pw_ref[:, t * CH : (t + 1) * CH].astype(F32)
    for h in range(HEADS):
        go_ref[h * DIM : (h + 1) * DIM, :] = vs[pl.ds(4 + h, DIM, stride=4 * OUT_ROWS), :]
    grad_bias = jnp.sum(recv_ref[:, 8:16, :].astype(F32), axis=0)
    gb_ref[...] = jnp.transpose(grad_bias)[:, :HEADS]
    dots_row = jnp.sum(jnp.transpose(dots), axis=0, keepdims=True)
    bias_row = jnp.sum(grad_bias * wbt_ref[...].astype(F32), axis=0, keepdims=True)
    gg_ref[...] = (dots_row + bias_row) / gain_ref[...]


def call(kernel, out_shape, scratch=(), cost=None):
    many = isinstance(out_shape, (list, tuple))
    spec = pl.BlockSpec(memory_space=pltpu.VMEM)
    return pl.pallas_call(
        kernel,
        out_shape=out_shape,
        out_specs=[spec] * len(out_shape) if many else spec,
        scratch_shapes=list(scratch),
        compiler_params=pltpu.CompilerParams(vmem_limit_bytes=32 * 1024 * 1024),
        cost_estimate=cost,
    )


def shape(*dims, dtype=BF):
    return jax.ShapeDtypeStruct(dims, dtype)


def exchange(x):
    return lax.all_to_all(x, BOTH, 0, 0, tiled=True)


def local(pair_rep, cotangent, norm_gain, proj_weight, bias_weight, out_weight, residue_mask):
    gain = norm_gain.reshape(1, CH)
    wbt = jnp.concatenate([bias_weight.T, jnp.zeros((HEADS, CH), BF)], axis=0)
    wall = proj_weight.reshape(CH, 4, HEADS, DIM).transpose(2, 1, 3, 0).reshape(HEADS, CH, CH)
    masking = (residue_mask.astype(F32) - 1.0) * MASK_FILL
    masking = jnp.broadcast_to(masking[:, None], (LENGTH, CH))
    tile_f32 = pltpu.VMEM((TILE, CH), F32)

    send, normed = call(
        pre_kernel, [shape(DEVICES, IN_ROWS, CH), shape(TILE, CH)], [tile_f32, tile_f32]
    )(pair_rep, cotangent, gain, wbt)
    recv = exchange(send)
    mid = call(
        attention_kernel,
        shape(N_WIDE, N_NARROW, MID_ROWS, CH),
        [
            pltpu.VMEM((2, LENGTH, CH), F32),
            pltpu.VMEM((2, LENGTH, CH), F32),
            pltpu.VMEM((DEVICES * 8, CH), F32),
            pltpu.VMEM((CH, CH), F32),
            pltpu.VMEM((DIM, CH), F32),
        ],
    )(recv.reshape(N_WIDE, N_NARROW, IN_ROWS, CH), wall, out_weight, masking)
    mid = exchange(mid.reshape(DEVICES, MID_ROWS, CH))
    send, bias = call(reduce_kernel, [shape(DEVICES, OUT_ROWS, CH), shape(8, TILE)])(mid, normed)
    last = exchange(send)
    d_pair = call(
        pair_kernel,
        shape(ROWS, COLS, CH),
        [tile_f32],
        pl.CostEstimate(flops=100_000_000, bytes_accessed=4_000_000, transcendentals=512),
    )(mid, bias, pair_rep, gain, wall, wbt)
    grad_proj, grad_bias, grad_out, grad_gain = call(
        final_kernel,
        [
            shape(CH, 4 * CH, dtype=F32),
            shape(CH, HEADS, dtype=F32),
            shape(CH, CH, dtype=F32),
            shape(1, CH, dtype=F32),
        ],
        [pltpu.VMEM((DEVICES * OUT_ROWS, CH), F32)],
    )(last, proj_weight, wbt, gain)
    return (d_pair, grad_proj, grad_bias, grad_out, grad_gain.reshape(CH))


def solution(mesh):
    in_specs = (P("wide", "narrow", None), P("wide", "narrow", None), P(), P(), P(), P(), P())
    out_specs = (P("wide", "narrow", None), P(), P(), P(), P())
    return jax.shard_map(local, mesh=mesh, in_specs=in_specs, out_specs=out_specs, check_vma=False)
```

```python
import jax
import jax.numpy as jnp
from jax import lax
from jax.experimental import pallas as pl
from jax.experimental.pallas import tpu as pltpu
from jax.sharding import Mesh, PartitionSpec as P

NORM_EPSILON = 1e-05
MASK_FILL = 1000000000.0
BF = jnp.bfloat16
F32 = jnp.float32
CHIPS = ("chip", "narrow")
BOTH = ("chip", "core", "narrow")

ROWS = 16
COLS = 32
TILE = ROWS * COLS
N_WIDE = 16
N_CHIP = 8
N_NARROW = 8
DEVICES = N_WIDE * N_NARROW
LENGTH = 256
CH = 128
HEADS = 4
DIM = 32
IN_ROWS = 40
TOGETHER = 4
MID_ROWS = 24
OUT_ROWS = 10

NT = (((1,), (1,)), ((), ()))
NN = (((1,), (0,)), ((), ()))
TN = (((0,), (0,)), ((), ()))


def mm(a, b, dims=NN):
    return lax.dot_general(a, b, dims, preferred_element_type=F32)


def normal(x):
    centered = x - jnp.mean(x, axis=-1, keepdims=True)
    inverse = lax.rsqrt(jnp.mean(centered * centered, axis=-1, keepdims=True) + NORM_EPSILON)
    return centered * inverse, inverse


def lane_group(shape):
    return lax.broadcasted_iota(jnp.int32, shape, 1) // COLS


def pre_kernel(
    pair_hbm, cot_hbm, gain_hbm, wbt_ref, send_ref, normed_ref, pair_v, cot_v, gain_v, xs, cs, sems
):
    copies = [
        pltpu.make_async_copy(src, dst, sems.at[i])
        for i, (src, dst) in enumerate(
            ((pair_hbm, pair_v), (gain_hbm, gain_v), (cot_hbm, cot_v))
        )
    ]
    for copy in copies:
        copy.start()
    copies[0].wait()
    hat, _ = normal(pair_v[...].astype(F32).reshape(TILE, CH))
    copies[1].wait()
    normed = (hat * gain_v[...]).astype(BF)
    normed_ref[...] = normed
    xs[...] = normed.astype(F32)
    bias = mm(wbt_ref[...], normed, NT)
    for pair in range(2):
        rows = [
            bias[h : h + 1, b * CH : (b + 1) * CH]
            for h in (2 * pair, 2 * pair + 1)
            for b in range(4)
        ]
        chunk = jnp.concatenate(rows, axis=0).astype(BF)
        for col in range(COLS):
            send_ref[pair * COLS + col, 32:40, :] = chunk
    copies[2].wait()
    cs[...] = cot_v[...].astype(F32).reshape(TILE, CH)
    for col in range(COLS):
        x = xs[pl.ds(col, ROWS, stride=COLS), :].astype(BF)
        c = cs[pl.ds(col, ROWS, stride=COLS), :].astype(BF)
        for pair in range(2):
            send_ref[pair * COLS + col, 0:16, :] = x
            send_ref[pair * COLS + col, 16:32, :] = c


def attention_kernel(
    own_ref, other_ref, wall_ref, ow_ref, mask_ref, send_ref, bias_s, sum_s, tail_s, grad_s, gout_s
):
    core = lax.axis_index("core")
    head = 2 * (lax.axis_index("chip") // 4) + core
    scale = DIM**-0.5
    weight = wall_ref[head]
    out_w = ow_ref[pl.ds(pl.multiple_of(head * DIM, DIM), DIM), :]
    zero = jnp.zeros((DIM, CH), BF)

    def rows(n, start, stop):
        own, other = own_ref[:, n, start:stop, :], other_ref[:, n, start:stop, :]
        low, high = jnp.where(core == 0, own, other), jnp.where(core == 0, other, own)
        return jnp.stack([low, high], axis=1)

    group = lane_group((64, CH))
    for half in range(2):
        got = []
        for q in range(4):
            both = rows(half * 4 + q, 32, 40).astype(F32).reshape(N_WIDE, 8, CH)
            got.append(jnp.where(core == 0, both[:, 0:4], both[:, 4:8]).reshape(64, CH))
        for kq in range(4):
            acc = jnp.zeros((64, CH), F32)
            for q in range(4):
                shift = (q - kq) * COLS % CH
                acc = jnp.where(group == q, pltpu.roll(got[q], shift, 1) if shift else got[q], acc)
            bias_s.at[half][pl.ds(kq, 64, stride=4), :] = acc

    class Unit:
        pass

    def project(n):
        u = Unit()
        u.n = n
        u.x = rows(n, 0, 16).reshape(LENGTH, CH)
        u.cot = rows(n, 16, 32).reshape(LENGTH, CH)
        projected = mm(weight, u.x, NT)
        u.kv = mm(u.x, weight[DIM : 3 * DIM], NT).astype(BF)
        u.q, u.k, u.v = [projected[DIM * t : DIM * (t + 1)].astype(BF) for t in range(3)]
        u.gate = jax.nn.sigmoid(projected[3 * DIM :])
        u.og = mm(out_w, u.cot, NT)
        u.da = (u.og * u.gate).astype(BF)
        return u

    def score(u, half):
        part = slice(half * CH, (half + 1) * CH)
        h = Unit()
        h.half, h.q, h.da, h.v, h.n = half, u.q[:, part], u.da[:, part], u.v, u.n
        right = jnp.concatenate(
            [
                jnp.concatenate([h.q, zero], axis=1),
                jnp.concatenate([zero, h.da], axis=1),
            ],
            axis=0,
        )
        both = mm(u.kv, right)
        h.logits, h.d_soft = both[:, :CH], both[:, CH:]
        return h

    def softmax(h):
        logits = h.logits * scale + bias_s[h.half] + mask_ref[...]
        top = jnp.max(logits, axis=0, keepdims=True)
        e = jnp.exp(logits - top)
        h.soft = e * (1.0 / jnp.sum(e, axis=0, keepdims=True))
        h.soft_bf = h.soft.astype(BF)

    def attend(h):
        h.att = mm(h.v, h.soft_bf)
        h.delta = jnp.sum(h.da.astype(F32) * h.att, axis=0, keepdims=True)

    def logit_grads(h):
        h.d_log = (h.soft * (h.d_soft - h.delta)).astype(BF)
        if h.n == 0:
            sum_s[h.half] = h.d_log.astype(F32)
        else:
            sum_s[h.half] += h.d_log.astype(F32)

    def gradients(u, halves):
        d_log = jnp.concatenate([h.d_log for h in halves], axis=1)
        soft_bf = jnp.concatenate([h.soft_bf for h in halves], axis=1)
        att = jnp.concatenate([h.att for h in halves], axis=1)
        dq = mm(u.k, d_log) * scale
        dk = mm(u.q, d_log, NT) * scale
        dv = mm(u.da, soft_bf, NT)
        dg = u.og * att * u.gate * (1.0 - u.gate)
        u.grads = jnp.concatenate([dq, dk, dv, dg], axis=0).astype(BF)
        u.gated = (u.gate * att).astype(BF)

    def emit(u):
        part = mm(u.grads, u.x)
        out_part = mm(u.gated, u.cot)
        if u.n == 0:
            grad_s[...] = part
            gout_s[...] = out_part
        else:
            grad_s[...] += part
            gout_s[...] += out_part
        turned = jnp.transpose(u.grads.astype(F32)).astype(BF)
        send_ref[:, u.n, 0:16, :] = turned.reshape(N_WIDE, ROWS, CH)

    for first in range(0, N_NARROW, TOGETHER):
        units = [project(n) for n in range(first, first + TOGETHER)]
        pieces = [[score(u, half) for half in range(2)] for u in units]
        flat = [h for halves in pieces for h in halves]
        for step in (softmax, attend, logit_grads):
            for h in flat:
                step(h)
        for u, halves in zip(units, pieces):
            gradients(u, halves)
        for u in units:
            emit(u)

    tail_s[...] = jnp.zeros_like(tail_s)
    for n in range(N_NARROW):
        half, q = n // 4, n % 4
        acc = jnp.zeros((64, CH), F32)
        for kq in range(4):
            got = sum_s.at[half][pl.ds(kq, 64, stride=4), :]
            shift = (kq - q) * COLS % CH
            acc = jnp.where(group == kq, pltpu.roll(got, shift, 1) if shift else got, acc)
        for w in range(N_WIDE):
            at = (w * N_NARROW + n) * 8
            tail_s[at : at + 4, :] = acc[w * 4 : (w + 1) * 4, :]
    tail_s[pl.ds(4, DEVICES, stride=8), :] = jnp.transpose(grad_s[...])
    out_part = gout_s[...]
    for r in range(4):
        tail_s[pl.ds(5 + 8 * r, DIM, stride=32), :] = out_part
    tail = tail_s[...].astype(BF).reshape(N_WIDE, N_NARROW, 8, CH)
    send_ref[:, :, 16:24, :] = tail


def of_head(recv_ref, h, start, stop):
    got = recv_ref[h // 2, :, h % 2, :, start:stop, :]
    return got.reshape(COLS, stop - start, CH)


def reduce_kernel(recv_ref, normed_ref, send_ref, bias_ref):
    sums = [jnp.sum(of_head(recv_ref, h, 16, 24).astype(F32), axis=0) for h in range(HEADS)]
    blocks = [
        jnp.concatenate([sums[h][b : b + 1] for h in range(HEADS)], axis=0) for b in range(4)
    ]
    bias = jnp.concatenate(blocks, axis=1)
    bias = jnp.concatenate([bias, jnp.zeros_like(bias)], axis=0).astype(BF)
    bias_ref[...] = bias
    grad_bias = mm(bias, normed_ref[...])[:HEADS]
    group = lane_group((1, CH))
    rows = []
    for t in range(4):
        row = jnp.zeros((1, CH), F32)
        for h in range(HEADS):
            shift = (h - t) * COLS % CH
            got = sums[h][4:5]
            row = jnp.where(group == h, pltpu.roll(got, shift, 1) if shift else got, row)
        rows.append(row)
    place = lax.rem(lax.axis_index("narrow"), 4)
    row = jnp.zeros((1, CH), F32)
    for h in range(HEADS):
        shift = lax.rem(h * COLS + CH - place * COLS, CH)
        row = jnp.where(group == h, pltpu.roll(sums[h][5:6], shift, 1), row)
    rows += [row, jnp.zeros((1, CH), F32), grad_bias]
    chunk = jnp.concatenate(rows, axis=0)
    block = jnp.concatenate([chunk] * 8, axis=0).astype(BF)
    for i in range(DEVICES // 8):
        send_ref[i * 80 : (i + 1) * 80, :] = block


def pair_kernel(recv_ref, bias_ref, pair_ref, gain_ref, wall_ref, wbt_ref, out_ref, ds):
    total = jnp.zeros((TILE, CH), F32)
    for h in range(HEADS):
        g = of_head(recv_ref, h, 0, 16).reshape(TILE, CH)
        total = total + mm(g, wall_ref[h])
    ds[...] = total
    d_normed = jnp.concatenate([ds[pl.ds(r, COLS, stride=ROWS), :] for r in range(ROWS)], axis=0)
    wbt = wbt_ref[...].astype(F32)
    wbt = jnp.concatenate([wbt, jnp.zeros_like(wbt)], axis=0).astype(BF)
    d_normed = d_normed + mm(bias_ref[...], wbt, TN)
    hat, inverse = normal(pair_ref[...].astype(F32).reshape(TILE, CH))
    d_hat = d_normed * gain_ref[...]
    d_pair = inverse * (
        d_hat
        - jnp.mean(d_hat, axis=-1, keepdims=True)
        - hat * jnp.mean(d_hat * hat, axis=-1, keepdims=True)
    )
    out_ref[...] = d_pair.astype(BF).reshape(ROWS, COLS, CH)


def final_kernel(recv_ref, pw_ref, wbt_ref, gain_ref, gp_ref, gb_ref, go_ref, gg_ref, vs):
    vs[...] = recv_ref[...].astype(F32)
    dots = jnp.zeros((CH, CH), F32)
    for t in range(4):
        got = vs[pl.ds(t, CH, stride=OUT_ROWS), :]
        gp_ref[:, t * CH : (t + 1) * CH] = got
        dots = dots + got * pw_ref[:, t * CH : (t + 1) * CH].astype(F32)
    group = lane_group((DIM, CH))
    quarters = [vs[pl.ds(OUT_ROWS * q + 4, DIM, stride=4 * OUT_ROWS), :] for q in range(4)]
    for h in range(HEADS):
        acc = jnp.zeros((DIM, CH), F32)
        for q in range(4):
            shift = (q - h) * COLS % CH
            got = pltpu.roll(quarters[q], shift, 1) if shift else quarters[q]
            acc = jnp.where(group == q, got, acc)
        go_ref[h * DIM : (h + 1) * DIM, :] = acc
    grad_bias = jnp.concatenate(
        [
            jnp.sum(vs[pl.ds(6 + h, DEVICES, stride=OUT_ROWS), :], axis=0, keepdims=True)
            for h in range(HEADS)
        ],
        axis=0,
    )
    gb_ref[...] = grad_bias
    dots_row = jnp.sum(jnp.transpose(dots), axis=0, keepdims=True)
    bias_row = jnp.sum(grad_bias * wbt_ref[...].astype(F32), axis=0, keepdims=True)
    gg_ref[...] = (dots_row + bias_row) / gain_ref[...]


def call(kernel, out_shape, scratch=(), cost=None, outside=0):
    many = isinstance(out_shape, (list, tuple))
    spec = pl.BlockSpec(memory_space=pltpu.VMEM)

    def run(*args):
        specs = [
            pl.BlockSpec(memory_space=pltpu.HBM) if i < outside else spec for i in range(len(args))
        ]
        return pl.pallas_call(
            kernel,
            out_shape=out_shape,
            in_specs=specs,
            out_specs=[spec] * len(out_shape) if many else spec,
            scratch_shapes=list(scratch),
            compiler_params=pltpu.CompilerParams(vmem_limit_bytes=32 * 1024 * 1024),
            cost_estimate=cost,
        )(*args)

    return run


def shape(*dims, dtype=BF):
    return jax.ShapeDtypeStruct(dims, dtype)


def local(pair_rep, cotangent, norm_gain, proj_weight, bias_weight, out_weight, residue_mask):
    gain = norm_gain.reshape(1, CH)
    wbt = bias_weight.T
    wall = proj_weight.reshape(CH, 4, HEADS, DIM).transpose(2, 1, 3, 0).reshape(HEADS, CH, CH)
    masking = (residue_mask.astype(F32) - 1.0) * MASK_FILL
    masking = jnp.broadcast_to(masking[:, None], (LENGTH, CH))
    tile_f32 = pltpu.VMEM((TILE, CH), F32)

    send, normed = call(
        pre_kernel,
        [shape(DEVICES // 2, IN_ROWS, CH), shape(TILE, CH)],
        [
            pltpu.VMEM((ROWS, COLS, CH), BF),
            pltpu.VMEM((ROWS, COLS, CH), BF),
            pltpu.VMEM((1, CH), F32),
            tile_f32,
            tile_f32,
            pltpu.SemaphoreType.DMA((3,)),
        ],
        outside=3,
    )(pair_rep, cotangent, gain, wbt)
    own = lax.all_to_all(send, CHIPS, 0, 0, tiled=True)
    other = lax.ppermute(own, "core", [(0, 1), (1, 0)])
    mid = call(
        attention_kernel,
        shape(N_WIDE, N_NARROW, MID_ROWS, CH),
        [
            pltpu.VMEM((2, LENGTH, CH), F32),
            pltpu.VMEM((2, LENGTH, CH), F32),
            pltpu.VMEM((DEVICES * 8, CH), F32),
            pltpu.VMEM((CH, CH), F32),
            pltpu.VMEM((DIM, CH), F32),
        ],
    )(
        own.reshape(N_CHIP, N_NARROW, IN_ROWS, CH),
        other.reshape(N_CHIP, N_NARROW, IN_ROWS, CH),
        wall,
        out_weight,
        masking,
    )
    mid = lax.all_to_all(mid.reshape(DEVICES, MID_ROWS, CH), BOTH, 0, 0, tiled=True)
    mid = mid.reshape(2, N_CHIP // 2, 2, N_NARROW, MID_ROWS, CH)
    send, bias = call(reduce_kernel, [shape(DEVICES * OUT_ROWS, CH), shape(8, TILE)])(mid, normed)
    last = lax.all_to_all(send.reshape(DEVICES, OUT_ROWS // 2, 2, CH), BOTH, 0, 0, tiled=True)
    d_pair = call(
        pair_kernel,
        shape(ROWS, COLS, CH),
        [tile_f32],
        pl.CostEstimate(flops=100_000_000, bytes_accessed=4_000_000, transcendentals=512),
    )(mid, bias, pair_rep, gain, wall, wbt)
    grad_proj, grad_bias, grad_out, grad_gain = call(
        final_kernel,
        [
            shape(CH, 4 * CH, dtype=F32),
            shape(HEADS, CH, dtype=F32),
            shape(CH, CH, dtype=F32),
            shape(1, CH, dtype=F32),
        ],
        [pltpu.VMEM((DEVICES * OUT_ROWS, CH), F32)],
    )(last.reshape(DEVICES * OUT_ROWS, CH), proj_weight, wbt, gain)
    return (d_pair, grad_proj, grad_bias.T, grad_out, grad_gain.reshape(CH))


def solution(mesh):
    cores = Mesh(mesh.devices.reshape(N_CHIP, 2, N_NARROW), BOTH)
    tile = P(("chip", "core"), "narrow", None)
    in_specs = (tile, tile, P(), P(), P(), P(), P())
    out_specs = (tile, P(), P(), P(), P())
    return jax.shard_map(local, mesh=cores, in_specs=in_specs, out_specs=out_specs, check_vma=False)
```

```python
import jax
import jax.numpy as jnp
from jax import lax
from jax.experimental import pallas as pl
from jax.experimental.pallas import tpu as pltpu
from jax.sharding import Mesh, PartitionSpec as P

NORM_EPSILON = 1e-05
MASK_FILL = 1000000000.0
BF = jnp.bfloat16
F32 = jnp.float32
CHIPS = ("chip", "narrow")
BOTH = ("chip", "core", "narrow")

ROWS = 16
COLS = 32
TILE = ROWS * COLS
N_WIDE = 16
N_CHIP = 8
N_NARROW = 8
DEVICES = N_WIDE * N_NARROW
LENGTH = 256
CH = 128
HEADS = 4
DIM = 32
IN_ROWS = 40
TOGETHER = 4
MID_ROWS = 24
OUT_ROWS = 10

NT = (((1,), (1,)), ((), ()))
NN = (((1,), (0,)), ((), ()))
TN = (((0,), (0,)), ((), ()))


def mm(a, b, dims=NN):
    return lax.dot_general(a, b, dims, preferred_element_type=F32)


def normal(x):
    centered = x - jnp.mean(x, axis=-1, keepdims=True)
    inverse = lax.rsqrt(jnp.mean(centered * centered, axis=-1, keepdims=True) + NORM_EPSILON)
    return centered * inverse, inverse


def lane_group(shape):
    return lax.broadcasted_iota(jnp.int32, shape, 1) // COLS


def pre_kernel(
    pair_hbm, cot_hbm, gain_hbm, wbt_ref, send_ref, normed_ref, pair_v, cot_v, gain_v, xs, cs, sems
):
    copies = [
        pltpu.make_async_copy(src, dst, sems.at[i])
        for i, (src, dst) in enumerate(
            ((pair_hbm, pair_v), (gain_hbm, gain_v), (cot_hbm, cot_v))
        )
    ]
    for copy in copies:
        copy.start()
    copies[0].wait()
    hat, _ = normal(pair_v[...].astype(F32).reshape(TILE, CH))
    copies[1].wait()
    normed = (hat * gain_v[...]).astype(BF)
    normed_ref[...] = normed
    xs[...] = normed.astype(F32)
    bias = mm(wbt_ref[...], normed, NT)
    for pair in range(2):
        rows = [
            bias[h : h + 1, b * CH : (b + 1) * CH]
            for h in (2 * pair, 2 * pair + 1)
            for b in range(4)
        ]
        chunk = jnp.concatenate(rows, axis=0).astype(BF)
        for col in range(COLS):
            send_ref[pair * COLS + col, 32:40, :] = chunk
    copies[2].wait()
    cs[...] = cot_v[...].astype(F32).reshape(TILE, CH)
    for col in range(COLS):
        x = xs[pl.ds(col, ROWS, stride=COLS), :].astype(BF)
        c = cs[pl.ds(col, ROWS, stride=COLS), :].astype(BF)
        for pair in range(2):
            send_ref[pair * COLS + col, 0:16, :] = x
            send_ref[pair * COLS + col, 16:32, :] = c


def attention_kernel(
    own_ref, other_ref, wall_ref, ow_ref, mask_ref, send_ref, bias_s, sum_s, tail_s, grad_s, gout_s
):
    core = lax.axis_index("core")
    head = 2 * (lax.axis_index("chip") // 4) + core
    scale = DIM**-0.5
    weight = wall_ref[head]
    out_w = ow_ref[pl.ds(pl.multiple_of(head * DIM, DIM), DIM), :]
    zero = jnp.zeros((DIM, CH), BF)

    def rows(n, start, stop):
        own, other = own_ref[:, n, start:stop, :], other_ref[:, n, start:stop, :]
        low, high = jnp.where(core == 0, own, other), jnp.where(core == 0, other, own)
        return jnp.stack([low, high], axis=1)

    group = lane_group((64, CH))
    for half in range(2):
        got = []
        for q in range(4):
            both = rows(half * 4 + q, 32, 40).astype(F32).reshape(N_WIDE, 8, CH)
            got.append(jnp.where(core == 0, both[:, 0:4], both[:, 4:8]).reshape(64, CH))
        for kq in range(4):
            acc = jnp.zeros((64, CH), F32)
            for q in range(4):
                shift = (q - kq) * COLS % CH
                acc = jnp.where(group == q, pltpu.roll(got[q], shift, 1) if shift else got[q], acc)
            bias_s.at[half][pl.ds(kq, 64, stride=4), :] = acc

    class Unit:
        pass

    def project(n):
        u = Unit()
        u.n = n
        u.x = rows(n, 0, 16).reshape(LENGTH, CH)
        u.cot = rows(n, 16, 32).reshape(LENGTH, CH)
        projected = mm(weight, u.x, NT)
        u.kv = mm(u.x, weight[DIM : 3 * DIM], NT).astype(BF)
        u.q, u.k, u.v = [projected[DIM * t : DIM * (t + 1)].astype(BF) for t in range(3)]
        u.gate = jax.nn.sigmoid(projected[3 * DIM :])
        u.og = mm(out_w, u.cot, NT)
        u.da = (u.og * u.gate).astype(BF)
        return u

    def score(u, half):
        part = slice(half * CH, (half + 1) * CH)
        h = Unit()
        h.half, h.q, h.da, h.v, h.n = half, u.q[:, part], u.da[:, part], u.v, u.n
        right = jnp.concatenate(
            [
                jnp.concatenate([h.q, zero], axis=1),
                jnp.concatenate([zero, h.da], axis=1),
            ],
            axis=0,
        )
        both = mm(u.kv, right)
        h.logits, h.d_soft = both[:, :CH], both[:, CH:]
        return h

    def softmax(h):
        logits = h.logits * scale + bias_s[h.half] + mask_ref[...]
        top = jnp.max(logits, axis=0, keepdims=True)
        e = jnp.exp(logits - top)
        h.soft = e * (1.0 / jnp.sum(e, axis=0, keepdims=True))
        h.soft_bf = h.soft.astype(BF)

    def attend(h):
        h.att = mm(h.v, h.soft_bf)
        h.delta = jnp.sum(h.da.astype(F32) * h.att, axis=0, keepdims=True)

    def logit_grads(h):
        h.d_log = (h.soft * (h.d_soft - h.delta)).astype(BF)
        if h.n == 0:
            sum_s[h.half] = h.d_log.astype(F32)
        else:
            sum_s[h.half] += h.d_log.astype(F32)

    def gradients(u, halves):
        d_log = jnp.concatenate([h.d_log for h in halves], axis=1)
        soft_bf = jnp.concatenate([h.soft_bf for h in halves], axis=1)
        att = jnp.concatenate([h.att for h in halves], axis=1)
        dq = mm(u.k, d_log) * scale
        dk = mm(u.q, d_log, NT) * scale
        dv = mm(u.da, soft_bf, NT)
        dg = u.og * att * u.gate * (1.0 - u.gate)
        u.grads = jnp.concatenate([dq, dk, dv, dg], axis=0).astype(BF)
        u.gated = (u.gate * att).astype(BF)

    def emit(u):
        part = mm(u.grads, u.x)
        out_part = mm(u.gated, u.cot)
        if u.n == 0:
            grad_s[...] = part
            gout_s[...] = out_part
        else:
            grad_s[...] += part
            gout_s[...] += out_part
        turned = jnp.transpose(u.grads.astype(F32)).astype(BF)
        send_ref[:, u.n, 0:16, :] = turned.reshape(N_WIDE, ROWS, CH)

    for first in range(0, N_NARROW, TOGETHER):
        units = [project(n) for n in range(first, first + TOGETHER)]
        pieces = [[score(u, half) for half in range(2)] for u in units]
        flat = [h for halves in pieces for h in halves]
        for step in (softmax, attend, logit_grads):
            for h in flat:
                step(h)
        for u, halves in zip(units, pieces):
            gradients(u, halves)
        for u in units:
            emit(u)

    tail_s[...] = jnp.zeros_like(tail_s)
    for n in range(N_NARROW):
        half, q = n // 4, n % 4
        acc = jnp.zeros((64, CH), F32)
        for kq in range(4):
            got = sum_s.at[half][pl.ds(kq, 64, stride=4), :]
            shift = (kq - q) * COLS % CH
            acc = jnp.where(group == kq, pltpu.roll(got, shift, 1) if shift else got, acc)
        for w in range(N_WIDE):
            at = (w * N_NARROW + n) * 8
            tail_s[at : at + 4, :] = acc[w * 4 : (w + 1) * 4, :]
    tail_s[pl.ds(4, DEVICES, stride=8), :] = jnp.transpose(grad_s[...])
    out_part = gout_s[...]
    for r in range(4):
        tail_s[pl.ds(5 + 8 * r, DIM, stride=32), :] = out_part
    tail = tail_s[...].astype(BF).reshape(N_WIDE, N_NARROW, 8, CH)
    send_ref[:, :, 16:24, :] = tail


def of_head(recv_ref, h, start, stop):
    got = recv_ref[h // 2, :, h % 2, :, start:stop, :]
    return got.reshape(COLS, stop - start, CH)


def reduce_kernel(recv_ref, normed_ref, send_ref, bias_ref):
    sums = [jnp.sum(of_head(recv_ref, h, 16, 24).astype(F32), axis=0) for h in range(HEADS)]
    blocks = [
        jnp.concatenate([sums[h][b : b + 1] for h in range(HEADS)], axis=0) for b in range(4)
    ]
    bias = jnp.concatenate(blocks, axis=1)
    bias = jnp.concatenate([bias, jnp.zeros_like(bias)], axis=0).astype(BF)
    bias_ref[...] = bias
    grad_bias = mm(bias, normed_ref[...])[:HEADS]
    group = lane_group((1, CH))
    rows = []
    for t in range(4):
        row = jnp.zeros((1, CH), F32)
        for h in range(HEADS):
            shift = (h - t) * COLS % CH
            got = sums[h][4:5]
            row = jnp.where(group == h, pltpu.roll(got, shift, 1) if shift else got, row)
        rows.append(row)
    place = lax.rem(lax.axis_index("narrow"), 4)
    row = jnp.zeros((1, CH), F32)
    for h in range(HEADS):
        shift = lax.rem(h * COLS + CH - place * COLS, CH)
        row = jnp.where(group == h, pltpu.roll(sums[h][5:6], shift, 1), row)
    rows += [row, jnp.zeros((1, CH), F32), grad_bias]
    chunk = jnp.concatenate(rows, axis=0)
    block = jnp.concatenate([chunk] * 8, axis=0).astype(BF)
    for i in range(DEVICES // 8):
        send_ref[i * 80 : (i + 1) * 80, :] = block


def pair_kernel(recv_ref, bias_ref, pair_ref, gain_ref, wall_ref, wbt_ref, out_ref, ds):
    total = jnp.zeros((TILE, CH), F32)
    for h in range(HEADS):
        g = of_head(recv_ref, h, 0, 16).reshape(TILE, CH)
        total = total + mm(g, wall_ref[h])
    ds[...] = total
    d_normed = jnp.concatenate([ds[pl.ds(r, COLS, stride=ROWS), :] for r in range(ROWS)], axis=0)
    wbt = wbt_ref[...].astype(F32)
    wbt = jnp.concatenate([wbt, jnp.zeros_like(wbt)], axis=0).astype(BF)
    d_normed = d_normed + mm(bias_ref[...], wbt, TN)
    hat, inverse = normal(pair_ref[...].astype(F32).reshape(TILE, CH))
    d_hat = d_normed * gain_ref[...]
    d_pair = inverse * (
        d_hat
        - jnp.mean(d_hat, axis=-1, keepdims=True)
        - hat * jnp.mean(d_hat * hat, axis=-1, keepdims=True)
    )
    out_ref[...] = d_pair.astype(BF).reshape(ROWS, COLS, CH)


def final_kernel(recv_ref, pw_ref, wbt_ref, gain_ref, gp_ref, gb_ref, go_ref, gg_ref, vs):
    vs[...] = recv_ref[...].astype(F32)
    dots = jnp.zeros((CH, CH), F32)
    for t in range(4):
        got = vs[pl.ds(t, CH, stride=OUT_ROWS), :]
        gp_ref[:, t * CH : (t + 1) * CH] = got
        dots = dots + got * pw_ref[:, t * CH : (t + 1) * CH].astype(F32)
    group = lane_group((DIM, CH))
    quarters = [vs[pl.ds(OUT_ROWS * q + 4, DIM, stride=4 * OUT_ROWS), :] for q in range(4)]
    for h in range(HEADS):
        acc = jnp.zeros((DIM, CH), F32)
        for q in range(4):
            shift = (q - h) * COLS % CH
            got = pltpu.roll(quarters[q], shift, 1) if shift else quarters[q]
            acc = jnp.where(group == q, got, acc)
        go_ref[h * DIM : (h + 1) * DIM, :] = acc
    grad_bias = jnp.concatenate(
        [
            jnp.sum(vs[pl.ds(6 + h, DEVICES, stride=OUT_ROWS), :], axis=0, keepdims=True)
            for h in range(HEADS)
        ],
        axis=0,
    )
    gb_ref[...] = grad_bias
    dots_row = jnp.sum(jnp.transpose(dots), axis=0, keepdims=True)
    bias_row = jnp.sum(grad_bias * wbt_ref[...].astype(F32), axis=0, keepdims=True)
    gg_ref[...] = (dots_row + bias_row) / gain_ref[...]


def call(kernel, out_shape, scratch=(), cost=None, outside=0, vmem=32):
    many = isinstance(out_shape, (list, tuple))
    spec = pl.BlockSpec(memory_space=pltpu.VMEM)

    def run(*args):
        specs = [
            pl.BlockSpec(memory_space=pltpu.HBM) if i < outside else spec for i in range(len(args))
        ]
        return pl.pallas_call(
            kernel,
            out_shape=out_shape,
            in_specs=specs,
            out_specs=[spec] * len(out_shape) if many else spec,
            scratch_shapes=list(scratch),
            compiler_params=pltpu.CompilerParams(vmem_limit_bytes=vmem * 1024 * 1024),
            cost_estimate=cost,
        )(*args)

    return run


def shape(*dims, dtype=BF):
    return jax.ShapeDtypeStruct(dims, dtype)


def local(pair_rep, cotangent, norm_gain, proj_weight, bias_weight, out_weight, residue_mask):
    gain = norm_gain.reshape(1, CH)
    wbt = bias_weight.T
    wall = proj_weight.reshape(CH, 4, HEADS, DIM).transpose(2, 1, 3, 0).reshape(HEADS, CH, CH)
    masking = (residue_mask.astype(F32) - 1.0) * MASK_FILL
    masking = jnp.broadcast_to(masking[:, None], (LENGTH, CH))
    tile_f32 = pltpu.VMEM((TILE, CH), F32)

    send, normed = call(
        pre_kernel,
        [shape(DEVICES // 2, IN_ROWS, CH), shape(TILE, CH)],
        [
            pltpu.VMEM((ROWS, COLS, CH), BF),
            pltpu.VMEM((ROWS, COLS, CH), BF),
            pltpu.VMEM((1, CH), F32),
            tile_f32,
            tile_f32,
            pltpu.SemaphoreType.DMA((3,)),
        ],
        outside=3,
        vmem=63,
    )(pair_rep, cotangent, gain, wbt)
    own = lax.all_to_all(send, CHIPS, 0, 0, tiled=True)
    other = lax.ppermute(own, "core", [(0, 1), (1, 0)])
    mid = call(
        attention_kernel,
        shape(N_WIDE, N_NARROW, MID_ROWS, CH),
        [
            pltpu.VMEM((2, LENGTH, CH), F32),
            pltpu.VMEM((2, LENGTH, CH), F32),
            pltpu.VMEM((DEVICES * 8, CH), F32),
            pltpu.VMEM((CH, CH), F32),
            pltpu.VMEM((DIM, CH), F32),
        ],
    )(
        own.reshape(N_CHIP, N_NARROW, IN_ROWS, CH),
        other.reshape(N_CHIP, N_NARROW, IN_ROWS, CH),
        wall,
        out_weight,
        masking,
    )
    mid = lax.all_to_all(mid.reshape(DEVICES, MID_ROWS, CH), BOTH, 0, 0, tiled=True)
    mid = mid.reshape(2, N_CHIP // 2, 2, N_NARROW, MID_ROWS, CH)
    send, bias = call(reduce_kernel, [shape(DEVICES * OUT_ROWS, CH), shape(8, TILE)])(mid, normed)
    last = lax.all_to_all(send.reshape(DEVICES, OUT_ROWS // 2, 2, CH), BOTH, 0, 0, tiled=True)
    d_pair = call(
        pair_kernel,
        shape(ROWS, COLS, CH),
        [tile_f32],
        pl.CostEstimate(flops=100_000_000, bytes_accessed=4_000_000, transcendentals=512),
    )(mid, bias, pair_rep, gain, wall, wbt)
    grad_proj, grad_bias, grad_out, grad_gain = call(
        final_kernel,
        [
            shape(CH, 4 * CH, dtype=F32),
            shape(HEADS, CH, dtype=F32),
            shape(CH, CH, dtype=F32),
            shape(1, CH, dtype=F32),
        ],
        [pltpu.VMEM((DEVICES * OUT_ROWS, CH), F32)],
    )(last.reshape(DEVICES * OUT_ROWS, CH), proj_weight, wbt, gain)
    return (d_pair, grad_proj, grad_bias.T, grad_out, grad_gain.reshape(CH))


def solution(mesh):
    cores = Mesh(mesh.devices.reshape(N_CHIP, 2, N_NARROW), BOTH)
    tile = P(("chip", "core"), "narrow", None)
    in_specs = (tile, tile, P(), P(), P(), P(), P())
    out_specs = (tile, P(), P(), P(), P())
    return jax.shard_map(local, mesh=cores, in_specs=in_specs, out_specs=out_specs, check_vma=False)
```

```python
import jax
import jax.numpy as jnp
from jax import lax
from jax.experimental import pallas as pl
from jax.experimental.pallas import tpu as pltpu
from jax.sharding import Mesh, PartitionSpec as P

NORM_EPSILON = 1e-05
MASK_FILL = 1000000000.0
BF = jnp.bfloat16
F32 = jnp.float32
CHIPS = ("chip", "narrow")
BOTH = ("chip", "core", "narrow")

ROWS = 16
COLS = 32
TILE = ROWS * COLS
N_WIDE = 16
N_CHIP = 8
N_NARROW = 8
DEVICES = N_WIDE * N_NARROW
LENGTH = 256
CH = 128
HEADS = 4
DIM = 32
IN_ROWS = 40
PARTS = 4
TOGETHER = 4
MID_ROWS = 24
SUM_ROWS = 32
OUT_ROWS = 10

NT = (((1,), (1,)), ((), ()))
NN = (((1,), (0,)), ((), ()))
TN = (((0,), (0,)), ((), ()))


def mm(a, b, dims=NN):
    return lax.dot_general(a, b, dims, preferred_element_type=F32)


def normal(x):
    centered = x - jnp.mean(x, axis=-1, keepdims=True)
    inverse = lax.rsqrt(jnp.mean(centered * centered, axis=-1, keepdims=True) + NORM_EPSILON)
    return centered * inverse, inverse


def lane_group(shape):
    return lax.broadcasted_iota(jnp.int32, shape, 1) // COLS


def pre_kernel(
    pair_hbm, cot_hbm, gain_hbm, wbt_hbm, send_hbm, normed_hbm,
    pair_v, cot_v, gain_v, wbt_v, send_v, normed_v, xs, cs, sems, out_sems,
):
    copies = [
        pltpu.make_async_copy(src, dst, sems.at[i])
        for i, (src, dst) in enumerate(
            ((pair_hbm, pair_v), (gain_hbm, gain_v), (wbt_hbm, wbt_v), (cot_hbm, cot_v))
        )
    ]
    for copy in copies:
        copy.start()
    copies[0].wait()
    hat, _ = normal(pair_v[...].astype(F32).reshape(TILE, CH))
    copies[1].wait()
    normed = (hat * gain_v[...]).astype(BF)
    normed_v[...] = normed
    outs = [pltpu.make_async_copy(normed_v, normed_hbm, out_sems.at[PARTS])]
    outs[0].start()
    xs[...] = normed.astype(F32)
    copies[2].wait()
    bias = mm(wbt_v[...], normed, NT)
    chunks = []
    for pair in range(2):
        rows = [
            bias[h : h + 1, b * CH : (b + 1) * CH]
            for h in (2 * pair, 2 * pair + 1)
            for b in range(4)
        ]
        chunks.append(jnp.concatenate(rows, axis=0).astype(BF))
    copies[3].wait()
    cs[...] = cot_v[...].astype(F32).reshape(TILE, CH)
    for part in range(PARTS):
        size = COLS // PARTS
        for col in range(part * size, (part + 1) * size):
            x = xs[pl.ds(col, ROWS, stride=COLS), :].astype(BF)
            c = cs[pl.ds(col, ROWS, stride=COLS), :].astype(BF)
            for pair in range(2):
                send_v[pair, col, 0:16, :] = x
                send_v[pair, col, 16:32, :] = c
                send_v[pair, col, 32:40, :] = chunks[pair]
        place = pl.ds(part * size, size)
        copy = pltpu.make_async_copy(
            send_v.at[:, place], send_hbm.at[:, place], out_sems.at[part]
        )
        copy.start()
        outs.append(copy)
    for copy in outs:
        copy.wait()


def attention_kernel(
    own_ref, other_ref, wall_ref, ow_ref, mask_ref, keep_ref, give_ref,
    bias_s, sum_s, tail_s, grad_s, gout_s,
):
    core = lax.axis_index("core")
    head = 2 * (lax.axis_index("chip") // 4) + core
    scale = DIM**-0.5
    weight = wall_ref[head]
    out_w = ow_ref[pl.ds(pl.multiple_of(head * DIM, DIM), DIM), :]
    zero = jnp.zeros((DIM, CH), BF)

    def rows(n, start, stop):
        own, other = own_ref[:, n, start:stop, :], other_ref[:, n, start:stop, :]
        low, high = jnp.where(core == 0, own, other), jnp.where(core == 0, other, own)
        return jnp.stack([low, high], axis=1)

    def put(value, n, start, stop):
        even, odd = value[:, 0], value[:, 1]
        keep_ref[:, n, start:stop, :] = jnp.where(core == 0, even, odd)
        give_ref[:, n, start:stop, :] = jnp.where(core == 0, odd, even)

    group = lane_group((64, CH))
    for half in range(2):
        got = []
        for q in range(4):
            both = rows(half * 4 + q, 32, 40).astype(F32).reshape(N_WIDE, 8, CH)
            got.append(jnp.where(core == 0, both[:, 0:4], both[:, 4:8]).reshape(64, CH))
        for kq in range(4):
            acc = jnp.zeros((64, CH), F32)
            for q in range(4):
                shift = (q - kq) * COLS % CH
                acc = jnp.where(group == q, pltpu.roll(got[q], shift, 1) if shift else got[q], acc)
            bias_s.at[half][pl.ds(kq, 64, stride=4), :] = acc

    class Unit:
        pass

    def project(n):
        u = Unit()
        u.n = n
        u.x = rows(n, 0, 16).reshape(LENGTH, CH)
        u.cot = rows(n, 16, 32).reshape(LENGTH, CH)
        projected = mm(weight, u.x, NT)
        u.kv = mm(u.x, weight[DIM : 3 * DIM], NT).astype(BF)
        u.q, u.k, u.v = [projected[DIM * t : DIM * (t + 1)].astype(BF) for t in range(3)]
        u.gate = jax.nn.sigmoid(projected[3 * DIM :])
        u.og = mm(out_w, u.cot, NT)
        u.da = (u.og * u.gate).astype(BF)
        return u

    def score(u, half):
        part = slice(half * CH, (half + 1) * CH)
        h = Unit()
        h.half, h.q, h.da, h.v, h.n = half, u.q[:, part], u.da[:, part], u.v, u.n
        right = jnp.concatenate(
            [
                jnp.concatenate([h.q, zero], axis=1),
                jnp.concatenate([zero, h.da], axis=1),
            ],
            axis=0,
        )
        both = mm(u.kv, right)
        h.logits, h.d_soft = both[:, :CH], both[:, CH:]
        return h

    def softmax(h):
        logits = h.logits * scale + bias_s[h.half] + mask_ref[...]
        top = jnp.max(logits, axis=0, keepdims=True)
        e = jnp.exp(logits - top)
        h.soft = e * (1.0 / jnp.sum(e, axis=0, keepdims=True))
        h.soft_bf = h.soft.astype(BF)

    def attend(h):
        h.att = mm(h.v, h.soft_bf)
        h.delta = jnp.sum(h.da.astype(F32) * h.att, axis=0, keepdims=True)

    def logit_grads(h):
        h.d_log = (h.soft * (h.d_soft - h.delta)).astype(BF)
        if h.n == 0:
            sum_s[h.half] = h.d_log.astype(F32)
        else:
            sum_s[h.half] += h.d_log.astype(F32)

    def gradients(u, halves):
        d_log = jnp.concatenate([h.d_log for h in halves], axis=1)
        soft_bf = jnp.concatenate([h.soft_bf for h in halves], axis=1)
        att = jnp.concatenate([h.att for h in halves], axis=1)
        dq = mm(u.k, d_log) * scale
        dk = mm(u.q, d_log, NT) * scale
        dv = mm(u.da, soft_bf, NT)
        dg = u.og * att * u.gate * (1.0 - u.gate)
        u.grads = jnp.concatenate([dq, dk, dv, dg], axis=0).astype(BF)
        u.gated = (u.gate * att).astype(BF)

    def emit(u):
        part = mm(u.grads, u.x)
        out_part = mm(u.gated, u.cot)
        if u.n == 0:
            grad_s[...] = part
            gout_s[...] = out_part
        else:
            grad_s[...] += part
            gout_s[...] += out_part
        d_normed = mm(u.grads, weight, TN).astype(BF)
        put(d_normed.reshape(N_CHIP, 2, ROWS, CH), u.n, 0, 16)

    for first in range(0, N_NARROW, TOGETHER):
        units = [project(n) for n in range(first, first + TOGETHER)]
        pieces = [[score(u, half) for half in range(2)] for u in units]
        flat = [h for halves in pieces for h in halves]
        for step in (softmax, attend, logit_grads):
            for h in flat:
                step(h)
        for u, halves in zip(units, pieces):
            gradients(u, halves)
        for u in units:
            emit(u)

    tail_s[...] = jnp.zeros_like(tail_s)
    for n in range(N_NARROW):
        half, q = n // 4, n % 4
        acc = jnp.zeros((64, CH), F32)
        for kq in range(4):
            got = sum_s.at[half][pl.ds(kq, 64, stride=4), :]
            shift = (kq - q) * COLS % CH
            acc = jnp.where(group == kq, pltpu.roll(got, shift, 1) if shift else got, acc)
        for w in range(N_WIDE):
            at = (w * N_NARROW + n) * 8
            tail_s[at : at + 4, :] = acc[w * 4 : (w + 1) * 4, :]
    tail_s[pl.ds(4, DEVICES, stride=8), :] = jnp.transpose(grad_s[...])
    out_part = gout_s[...]
    for r in range(4):
        tail_s[pl.ds(5 + 8 * r, DIM, stride=32), :] = out_part
    tail = tail_s[...].astype(BF).reshape(N_CHIP, 2, N_NARROW, 8, CH)
    put(tail, slice(None), 16, 24)


def join_kernel(keep_ref, got_ref, send_ref):
    core = lax.axis_index("core")
    total = keep_ref[:, 0:16, :].astype(F32) + got_ref[:, 0:16, :].astype(F32)
    send_ref[:, 0:16, :] = total.astype(BF)
    keep, got = keep_ref[:, 16:24, :], got_ref[:, 16:24, :]
    send_ref[:, 16:24, :] = jnp.where(core == 0, keep, got)
    send_ref[:, 24:32, :] = jnp.where(core == 0, got, keep)


def reduce_kernel(recv_ref, normed_ref, send_ref, bias_ref):
    sums = [
        jnp.sum(
            recv_ref[h // 2, :, 16 + 8 * (h % 2) : 24 + 8 * (h % 2), :].astype(F32), axis=0
        )
        for h in range(HEADS)
    ]
    blocks = [
        jnp.concatenate([sums[h][b : b + 1] for h in range(HEADS)], axis=0) for b in range(4)
    ]
    bias = jnp.concatenate(blocks, axis=1)
    bias = jnp.concatenate([bias, jnp.zeros_like(bias)], axis=0).astype(BF)
    bias_ref[...] = bias
    grad_bias = mm(bias, normed_ref[...])[:HEADS]
    group = lane_group((1, CH))
    rows = []
    for t in range(4):
        row = jnp.zeros((1, CH), F32)
        for h in range(HEADS):
            shift = (h - t) * COLS % CH
            got = sums[h][4:5]
            row = jnp.where(group == h, pltpu.roll(got, shift, 1) if shift else got, row)
        rows.append(row)
    place = lax.rem(lax.axis_index("narrow"), 4)
    row = jnp.zeros((1, CH), F32)
    for h in range(HEADS):
        shift = lax.rem(h * COLS + CH - place * COLS, CH)
        row = jnp.where(group == h, pltpu.roll(sums[h][5:6], shift, 1), row)
    rows += [row, jnp.zeros((1, CH), F32), grad_bias]
    chunk = jnp.concatenate(rows, axis=0)
    block = jnp.concatenate([chunk] * 8, axis=0).astype(BF)
    for i in range(DEVICES // 8):
        send_ref[i * 80 : (i + 1) * 80, :] = block


def pair_kernel(recv_ref, bias_ref, pair_ref, gain_ref, wbt_ref, out_ref, ds):
    total = recv_ref[0, :, 0:16, :].astype(F32) + recv_ref[1, :, 0:16, :].astype(F32)
    ds[...] = total.reshape(TILE, CH)
    d_normed = jnp.concatenate([ds[pl.ds(r, COLS, stride=ROWS), :] for r in range(ROWS)], axis=0)
    wbt = wbt_ref[...].astype(F32)
    wbt = jnp.concatenate([wbt, jnp.zeros_like(wbt)], axis=0).astype(BF)
    d_normed = d_normed + mm(bias_ref[...], wbt, TN)
    hat, inverse = normal(pair_ref[...].astype(F32).reshape(TILE, CH))
    d_hat = d_normed * gain_ref[...]
    d_pair = inverse * (
        d_hat
        - jnp.mean(d_hat, axis=-1, keepdims=True)
        - hat * jnp.mean(d_hat * hat, axis=-1, keepdims=True)
    )
    out_ref[...] = d_pair.astype(BF).reshape(ROWS, COLS, CH)


def final_kernel(recv_ref, pw_ref, wbt_ref, gain_ref, gp_ref, gb_ref, go_ref, gg_ref, vs):
    vs[...] = recv_ref[...].astype(F32)
    dots = jnp.zeros((CH, CH), F32)
    for t in range(4):
        got = vs[pl.ds(t, CH, stride=OUT_ROWS), :]
        gp_ref[:, t * CH : (t + 1) * CH] = got
        dots = dots + got * pw_ref[:, t * CH : (t + 1) * CH].astype(F32)
    group = lane_group((DIM, CH))
    quarters = [vs[pl.ds(OUT_ROWS * q + 4, DIM, stride=4 * OUT_ROWS), :] for q in range(4)]
    for h in range(HEADS):
        acc = jnp.zeros((DIM, CH), F32)
        for q in range(4):
            shift = (q - h) * COLS % CH
            got = pltpu.roll(quarters[q], shift, 1) if shift else quarters[q]
            acc = jnp.where(group == q, got, acc)
        go_ref[h * DIM : (h + 1) * DIM, :] = acc
    grad_bias = jnp.concatenate(
        [
            jnp.sum(vs[pl.ds(6 + h, DEVICES, stride=OUT_ROWS), :], axis=0, keepdims=True)
            for h in range(HEADS)
        ],
        axis=0,
    )
    gb_ref[...] = grad_bias
    dots_row = jnp.sum(jnp.transpose(dots), axis=0, keepdims=True)
    bias_row = jnp.sum(grad_bias * wbt_ref[...].astype(F32), axis=0, keepdims=True)
    gg_ref[...] = (dots_row + bias_row) / gain_ref[...]


def call(kernel, out_shape, scratch=(), cost=None, hbm=False, vmem=32):
    many = isinstance(out_shape, (list, tuple))
    spec = pl.BlockSpec(memory_space=pltpu.HBM if hbm else pltpu.VMEM)

    def run(*args):
        return pl.pallas_call(
            kernel,
            out_shape=out_shape,
            in_specs=[spec] * len(args),
            out_specs=[spec] * len(out_shape) if many else spec,
            scratch_shapes=list(scratch),
            compiler_params=pltpu.CompilerParams(vmem_limit_bytes=vmem * 1024 * 1024),
            cost_estimate=cost,
        )(*args)

    return run


def shape(*dims, dtype=BF):
    return jax.ShapeDtypeStruct(dims, dtype)


def exchange(x, axes, tile):
    count, rows, lanes = x.shape
    x = x.reshape(count, rows // tile, tile, lanes)
    return lax.all_to_all(x, axes, 0, 0, tiled=True).reshape(count, rows, lanes)


def swap(x):
    return lax.ppermute(x, "core", [(0, 1), (1, 0)])


def local(pair_rep, cotangent, norm_gain, proj_weight, bias_weight, out_weight, residue_mask):
    gain = norm_gain.reshape(1, CH)
    wbt = bias_weight.T
    wall = proj_weight.reshape(CH, 4, HEADS, DIM).transpose(2, 1, 3, 0).reshape(HEADS, CH, CH)
    masking = (residue_mask.astype(F32) - 1.0) * MASK_FILL
    masking = jnp.broadcast_to(masking[:, None], (LENGTH, CH))
    tile_f32 = pltpu.VMEM((TILE, CH), F32)
    half = DEVICES // 2

    send, normed = call(
        pre_kernel,
        [shape(2, COLS, IN_ROWS, CH), shape(TILE, CH)],
        [
            pltpu.VMEM((ROWS, COLS, CH), BF),
            pltpu.VMEM((ROWS, COLS, CH), BF),
            pltpu.VMEM((1, CH), F32),
            pltpu.VMEM((HEADS, CH), BF),
            pltpu.VMEM((2, COLS, IN_ROWS, CH), BF),
            pltpu.VMEM((TILE, CH), BF),
            tile_f32,
            tile_f32,
            pltpu.SemaphoreType.DMA((4,)),
            pltpu.SemaphoreType.DMA((PARTS + 1,)),
        ],
        hbm=True,
        vmem=63,
    )(pair_rep, cotangent, gain, wbt)
    own = exchange(send.reshape(half, IN_ROWS, CH), CHIPS, 4)
    other = swap(own)
    keep, give = call(
        attention_kernel,
        [shape(N_CHIP, N_NARROW, MID_ROWS, CH)] * 2,
        [
            pltpu.VMEM((2, LENGTH, CH), F32),
            pltpu.VMEM((2, LENGTH, CH), F32),
            pltpu.VMEM((DEVICES * 8, CH), F32),
            pltpu.VMEM((CH, CH), F32),
            pltpu.VMEM((DIM, CH), F32),
        ],
    )(
        own.reshape(N_CHIP, N_NARROW, IN_ROWS, CH),
        other.reshape(N_CHIP, N_NARROW, IN_ROWS, CH),
        wall,
        out_weight,
        masking,
    )
    got = swap(give)
    mid = call(join_kernel, shape(half, SUM_ROWS, CH))(
        keep.reshape(half, MID_ROWS, CH), got.reshape(half, MID_ROWS, CH)
    )
    mid = exchange(mid, CHIPS, 8).reshape(2, COLS, SUM_ROWS, CH)
    send, bias = call(reduce_kernel, [shape(DEVICES * OUT_ROWS, CH), shape(8, TILE)])(mid, normed)
    last = exchange(send.reshape(DEVICES, OUT_ROWS, CH), BOTH, 2)
    d_pair = call(
        pair_kernel,
        shape(ROWS, COLS, CH),
        [tile_f32],
        pl.CostEstimate(flops=100_000_000, bytes_accessed=4_000_000, transcendentals=512),
    )(mid, bias, pair_rep, gain, wbt)
    grad_proj, grad_bias, grad_out, grad_gain = call(
        final_kernel,
        [
            shape(CH, 4 * CH, dtype=F32),
            shape(HEADS, CH, dtype=F32),
            shape(CH, CH, dtype=F32),
            shape(1, CH, dtype=F32),
        ],
        [pltpu.VMEM((DEVICES * OUT_ROWS, CH), F32)],
    )(last.reshape(DEVICES * OUT_ROWS, CH), proj_weight, wbt, gain)
    return (d_pair, grad_proj, grad_bias.T, grad_out, grad_gain.reshape(CH))


def solution(mesh):
    cores = Mesh(mesh.devices.reshape(N_CHIP, 2, N_NARROW), BOTH)
    tile = P(("chip", "core"), "narrow", None)
    in_specs = (tile, tile, P(), P(), P(), P(), P())
    out_specs = (tile, P(), P(), P(), P())
    return jax.shard_map(local, mesh=cores, in_specs=in_specs, out_specs=out_specs, check_vma=False)
```

```python
import jax
import jax.numpy as jnp
from jax import lax
from jax.experimental import pallas as pl
from jax.experimental.pallas import tpu as pltpu
from jax.sharding import Mesh, PartitionSpec as P

NORM_EPSILON = 1e-05
MASK_FILL = 1000000000.0
BF = jnp.bfloat16
F32 = jnp.float32
CHIPS = ("chip", "narrow")
BOTH = ("chip", "core", "narrow")

ROWS = 16
COLS = 32
TILE = ROWS * COLS
N_WIDE = 16
N_CHIP = 8
N_NARROW = 8
DEVICES = N_WIDE * N_NARROW
LENGTH = 256
CH = 128
HEADS = 4
DIM = 32
HALF = 8
IN_ROWS = 32
PARTS = 4
TOGETHER = 8
MID_ROWS = 24
SUM_ROWS = 32
OUT_ROWS = 10

NT = (((1,), (1,)), ((), ()))
NN = (((1,), (0,)), ((), ()))
TN = (((0,), (0,)), ((), ()))


def mm(a, b, dims=NN):
    return lax.dot_general(a, b, dims, preferred_element_type=F32)


def normal(x):
    centered = x - jnp.mean(x, axis=-1, keepdims=True)
    inverse = lax.rsqrt(jnp.mean(centered * centered, axis=-1, keepdims=True) + NORM_EPSILON)
    return centered * inverse, inverse


def lane_group(shape, size=DIM):
    return lax.broadcasted_iota(jnp.int32, shape, 1) // size


def turn(x, lanes):
    lanes %= CH
    return pltpu.roll(x, lanes, 1) if lanes else x


def pre_kernel(
    pair_hbm, cot_hbm, gain_hbm, wbt_hbm, send_hbm, normed_hbm,
    pair_v, cot_v, gain_v, wbt_v, send_v, normed_v, xs, cs, sems, out_sems,
):
    copies = [
        pltpu.make_async_copy(src, dst, sems.at[i])
        for i, (src, dst) in enumerate(
            ((pair_hbm, pair_v), (gain_hbm, gain_v), (wbt_hbm, wbt_v), (cot_hbm, cot_v))
        )
    ]
    for copy in copies:
        copy.start()
    copies[0].wait()
    hat, _ = normal(pair_v[...].astype(F32).reshape(TILE, CH))
    copies[1].wait()
    normed = (hat * gain_v[...]).astype(BF).astype(F32)
    xs[...] = normed
    groups = normed.reshape(TILE // (2 * HALF), 2, HALF, CH)
    halves = [groups[:, s].reshape(TILE // 2, CH) for s in range(2)]
    split = jnp.concatenate(halves, axis=0).astype(BF)
    normed_v[...] = split
    outs = [pltpu.make_async_copy(normed_v, normed_hbm, out_sems.at[PARTS])]
    outs[0].start()
    copies[2].wait()
    bias = mm(wbt_v[...], split, NT)
    chunks = [
        jnp.concatenate(
            [
                bias[h : h + 1, (2 * s + kb) * CH : (2 * s + kb + 1) * CH]
                for h in range(HEADS)
                for kb in range(2)
            ],
            axis=0,
        )
        for s in range(2)
    ]
    copies[3].wait()
    cs[...] = cot_v[...].astype(F32).reshape(TILE, CH)
    for part in range(PARTS):
        size = COLS // PARTS
        for col in range(part * size, (part + 1) * size):
            x = xs[pl.ds(col, ROWS, stride=COLS), :].astype(BF)
            c = cs[pl.ds(col, ROWS, stride=COLS), :]
            for s in range(2):
                send_v[s, col, 0:16, :] = x
                rest = jnp.concatenate([c[s * HALF : (s + 1) * HALF], chunks[s]], axis=0)
                send_v[s, col, 16:32, :] = rest.astype(BF)
        place = pl.ds(part * size, size)
        copy = pltpu.make_async_copy(
            send_v.at[:, place], send_hbm.at[:, place], out_sems.at[part]
        )
        copy.start()
        outs.append(copy)
    for copy in outs:
        copy.wait()


def attention_kernel(
    own_ref, other_ref, wall_ref, ow_ref, mask_ref, keep_ref, give_ref,
    bias_s, sum_s, tail_s, kv_s, qg_s, gout_s,
):
    core = lax.axis_index("core")
    side = lax.axis_index("chip") // 4
    scale = DIM**-0.5
    two = [wall_ref[2 * core + hh] for hh in range(2)]
    w_kv = jnp.concatenate([w[DIM : 3 * DIM] for w in two], axis=0)
    w_qg = jnp.concatenate([w[:DIM] for w in two] + [w[3 * DIM :] for w in two], axis=0)
    out_w = ow_ref[pl.ds(pl.multiple_of(core * 2 * DIM, 2 * DIM), 2 * DIM), :]
    zero = jnp.zeros((DIM, CH), BF)

    def rows(n, start):
        own, other = [ref[:, n, start : start + HALF, :] for ref in (own_ref, other_ref)]
        low, high = jnp.where(core == 0, own, other), jnp.where(core == 0, other, own)
        return jnp.stack([low, high], axis=1).astype(F32).reshape(N_WIDE * HALF, CH)

    group = lane_group((N_WIDE, CH), 16)
    for n in range(N_NARROW):
        tail_s[n * CH : (n + 1) * CH, :] = rows(n, 24)
    for hh in range(2):
        for kb in range(2):
            got = []
            for n in range(N_NARROW):
                at = n * CH + 2 * hh + kb
                first = tail_s[pl.ds(at, N_WIDE, stride=8), :]
                second = tail_s[pl.ds(at + 4, N_WIDE, stride=8), :]
                got.append(jnp.where(core == 0, first, second))
            for kq in range(HALF):
                acc = got[0]
                acc = turn(acc, -kq * 16)
                for n in range(1, N_NARROW):
                    acc = jnp.where(group == n, turn(got[n], (n - kq) * 16), acc)
                bias_s.at[hh][pl.ds(kb * CH + kq, N_WIDE, stride=HALF), :] = acc

    class Unit:
        pass

    def project(n):
        u = Unit()
        u.n = n
        parts = [rows(n, 0).astype(BF), rows(n, HALF).astype(BF)]
        u.x = jnp.concatenate(parts, axis=0)
        u.x_own = jnp.where(side == 0, parts[0], parts[1])
        u.cot = rows(n, 16).astype(BF)
        u.kv = mm(u.x, w_kv, NT).astype(BF)
        kv_t = mm(w_kv, u.x, NT).astype(BF)
        qg = mm(w_qg, u.x_own, NT)
        og = mm(out_w, u.cot, NT)
        u.pieces = []
        for hh in range(2):
            h = Unit()
            h.n, h.hh, h.kv = n, hh, u.kv
            h.q = qg[hh * DIM : (hh + 1) * DIM].astype(BF)
            h.gate = jax.nn.sigmoid(qg[(2 + hh) * DIM : (3 + hh) * DIM])
            h.og = og[hh * DIM : (hh + 1) * DIM]
            h.da = (h.og * h.gate).astype(BF)
            h.k, h.v = [kv_t[(2 * hh + t) * DIM : (2 * hh + t + 1) * DIM] for t in range(2)]
            u.pieces.append(h)
        return u

    def score(h):
        top = [jnp.concatenate(pair, axis=1) for pair in ((h.q, zero), (zero, h.da))]
        rest = [jnp.concatenate([zero, zero], axis=1)] * 2
        right = jnp.concatenate(top + rest if h.hh == 0 else rest + top, axis=0)
        both = mm(h.kv, right)
        h.logits, h.d_soft = both[:, :CH], both[:, CH:]

    def softmax(h):
        logits = h.logits * scale + bias_s[h.hh] + mask_ref[...]
        top = jnp.max(logits, axis=0, keepdims=True)
        e = jnp.exp(logits - top)
        h.soft = e * (1.0 / jnp.sum(e, axis=0, keepdims=True))
        h.soft_bf = h.soft.astype(BF)

    def attend(h):
        h.att = mm(h.v, h.soft_bf)
        h.delta = jnp.sum(h.da.astype(F32) * h.att, axis=0, keepdims=True)

    def logit_grads(h):
        h.d_log = (h.soft * (h.d_soft - h.delta)).astype(BF)
        if h.n == 0:
            sum_s[h.hh] = h.d_log.astype(F32)
        else:
            sum_s[h.hh] += h.d_log.astype(F32)

    def gradients(h):
        h.dq = mm(h.k, h.d_log) * scale
        h.dk = mm(h.q, h.d_log, NT) * scale
        h.dv = mm(h.da, h.soft_bf, NT)
        h.dg = h.og * h.att * h.gate * (1.0 - h.gate)
        h.gated = (h.gate * h.att).astype(BF)

    def emit(u):
        one, other = u.pieces
        kv_grads = jnp.concatenate([one.dk, one.dv, other.dk, other.dv], axis=0).astype(BF)
        qg_grads = jnp.concatenate([one.dq, other.dq, one.dg, other.dg], axis=0).astype(BF)
        gated = jnp.concatenate([one.gated, other.gated], axis=0)
        sums = (mm(kv_grads, u.x), mm(qg_grads, u.x_own), mm(gated, u.cot))
        for ref, part in zip((kv_s, qg_s, gout_s), sums):
            if u.n == 0:
                ref[...] = part
            else:
                ref[...] += part
        d_normed = mm(kv_grads, w_kv, TN)
        d_own = mm(qg_grads, w_qg, TN)
        both = [
            (d_normed[i * CH : (i + 1) * CH] + jnp.where(side == i, d_own, 0.0)).reshape(
                N_CHIP, 2, HALF, CH
            )
            for i in range(2)
        ]
        put(jnp.concatenate(both, axis=2).astype(BF), u.n, 0, 16)

    def put(value, n, start, stop):
        even, odd = value[:, 0], value[:, 1]
        keep_ref[:, n, start:stop, :] = jnp.where(core == 0, even, odd)
        give_ref[:, n, start:stop, :] = jnp.where(core == 0, odd, even)

    for first in range(0, N_NARROW, TOGETHER):
        units = [project(n) for n in range(first, first + TOGETHER)]
        flat = [h for u in units for h in u.pieces]
        for step in (score, softmax, attend, logit_grads, gradients):
            for h in flat:
                step(h)
        for u in units:
            emit(u)

    for hh in range(2):
        for kb in range(2):
            got = [
                sum_s.at[hh][pl.ds(kb * CH + kq, N_WIDE, stride=HALF), :] for kq in range(HALF)
            ]
            for n in range(N_NARROW):
                acc = turn(got[0], -n * 16)
                for kq in range(1, HALF):
                    acc = jnp.where(group == kq, turn(got[kq], (kq - n) * 16), acc)
                tail_s[pl.ds(n * 8 + 2 * hh + kb, N_WIDE, stride=64), :] = acc
    tail_s[pl.ds(4, DEVICES, stride=8), :] = jnp.transpose(kv_s[...])
    tail_s[pl.ds(5, DEVICES, stride=8), :] = jnp.transpose(qg_s[...])
    for hh in range(2):
        out_part = gout_s[hh * DIM : (hh + 1) * DIM, :]
        for r in range(4):
            tail_s[pl.ds(6 + hh + 8 * r, DIM, stride=32), :] = out_part
    tail = tail_s[...].astype(BF).reshape(N_CHIP, 2, N_NARROW, 8, CH)
    put(tail, slice(None), 16, 24)


def join_kernel(keep_ref, got_ref, send_ref):
    core = lax.axis_index("core")
    total = keep_ref[:, 0:16, :].astype(F32) + got_ref[:, 0:16, :].astype(F32)
    send_ref[:, 0:16, :] = total.astype(BF)
    keep, got = keep_ref[:, 16:24, :], got_ref[:, 16:24, :]
    send_ref[:, 16:24, :] = jnp.where(core == 0, keep, got)
    send_ref[:, 24:32, :] = jnp.where(core == 0, got, keep)


def reduce_kernel(recv_ref, normed_ref, send_ref, bias_ref):
    sums = [
        [
            jnp.sum(recv_ref[s, :, 16 + 8 * c : 24 + 8 * c, :].astype(F32), axis=0)
            for c in range(2)
        ]
        for s in range(2)
    ]
    blocks = []
    for s in range(2):
        for kb in range(2):
            parts = [sums[s][h // 2][h % 2 * 2 + kb :][:1] for h in range(HEADS)]
            blocks.append(jnp.concatenate(parts, axis=0))
    bias = jnp.concatenate(blocks, axis=1)
    bias = jnp.concatenate([bias, jnp.zeros_like(bias)], axis=0).astype(BF)
    bias_ref[...] = bias
    grad_bias = mm(bias, normed_ref[...])[:HEADS]
    total = [sums[0][c] + sums[1][c] for c in range(2)]
    group = lane_group((1, CH))
    rows = []
    for t in range(4):
        row = jnp.zeros((1, CH), F32)
        for h in range(HEADS):
            own = total[h // 2]
            got, place = {
                0: (own[5:6], h % 2),
                1: (own[4:5], h % 2 * 2),
                2: (own[4:5], h % 2 * 2 + 1),
                3: (own[5:6], 2 + h % 2),
            }[t]
            row = jnp.where(group == h, turn(got, (h - place) * DIM), row)
        rows.append(row)
    place = lax.rem(lax.axis_index("narrow"), 4)
    row = jnp.zeros((1, CH), F32)
    for h in range(HEADS):
        shift = lax.rem(h * DIM + CH - place * DIM, CH)
        got = total[h // 2][6 + h % 2 :][:1]
        row = jnp.where(group == h, pltpu.roll(got, shift, 1), row)
    rows += [row, jnp.zeros((1, CH), F32), grad_bias]
    chunk = jnp.concatenate(rows, axis=0)
    block = jnp.concatenate([chunk] * 8, axis=0).astype(BF)
    for i in range(DEVICES // 8):
        send_ref[i * 80 : (i + 1) * 80, :] = block


def pair_kernel(recv_ref, bias_ref, pair_ref, gain_ref, wbt_ref, out_ref, ds):
    total = recv_ref[0, :, 0:16, :].astype(F32) + recv_ref[1, :, 0:16, :].astype(F32)
    ds[...] = total.reshape(TILE, CH)
    d_normed = jnp.concatenate([ds[pl.ds(r, COLS, stride=ROWS), :] for r in range(ROWS)], axis=0)
    wbt = wbt_ref[...].astype(F32)
    wbt = jnp.concatenate([wbt, jnp.zeros_like(wbt)], axis=0).astype(BF)
    split = mm(bias_ref[...], wbt, TN).reshape(2, TILE // (2 * HALF), HALF, CH)
    d_normed = d_normed + jnp.stack([split[0], split[1]], axis=1).reshape(TILE, CH)
    hat, inverse = normal(pair_ref[...].astype(F32).reshape(TILE, CH))
    d_hat = d_normed * gain_ref[...]
    d_pair = inverse * (
        d_hat
        - jnp.mean(d_hat, axis=-1, keepdims=True)
        - hat * jnp.mean(d_hat * hat, axis=-1, keepdims=True)
    )
    out_ref[...] = d_pair.astype(BF).reshape(ROWS, COLS, CH)


def final_kernel(recv_ref, pw_ref, wbt_ref, gain_ref, gp_ref, gb_ref, go_ref, gg_ref, vs):
    vs[...] = recv_ref[...].astype(F32)
    dots = jnp.zeros((CH, CH), F32)
    for t in range(4):
        got = vs[pl.ds(t, CH, stride=OUT_ROWS), :]
        gp_ref[:, t * CH : (t + 1) * CH] = got
        dots = dots + got * pw_ref[:, t * CH : (t + 1) * CH].astype(F32)
    group = lane_group((DIM, CH))
    quarters = [vs[pl.ds(OUT_ROWS * q + 4, DIM, stride=4 * OUT_ROWS), :] for q in range(4)]
    for h in range(HEADS):
        acc = jnp.zeros((DIM, CH), F32)
        for q in range(4):
            shift = (q - h) * COLS % CH
            got = pltpu.roll(quarters[q], shift, 1) if shift else quarters[q]
            acc = jnp.where(group == q, got, acc)
        go_ref[h * DIM : (h + 1) * DIM, :] = acc
    grad_bias = jnp.concatenate(
        [
            jnp.sum(vs[pl.ds(6 + h, DEVICES, stride=OUT_ROWS), :], axis=0, keepdims=True)
            for h in range(HEADS)
        ],
        axis=0,
    )
    gb_ref[...] = grad_bias
    dots_row = jnp.sum(jnp.transpose(dots), axis=0, keepdims=True)
    bias_row = jnp.sum(grad_bias * wbt_ref[...].astype(F32), axis=0, keepdims=True)
    gg_ref[...] = (dots_row + bias_row) / gain_ref[...]


def call(kernel, out_shape, scratch=(), cost=None, hbm=False, vmem=32):
    many = isinstance(out_shape, (list, tuple))
    spec = pl.BlockSpec(memory_space=pltpu.HBM if hbm else pltpu.VMEM)

    def run(*args):
        return pl.pallas_call(
            kernel,
            out_shape=out_shape,
            in_specs=[spec] * len(args),
            out_specs=[spec] * len(out_shape) if many else spec,
            scratch_shapes=list(scratch),
            compiler_params=pltpu.CompilerParams(vmem_limit_bytes=vmem * 1024 * 1024),
            cost_estimate=cost,
        )(*args)

    return run


def shape(*dims, dtype=BF):
    return jax.ShapeDtypeStruct(dims, dtype)


def exchange(x, axes, tile):
    count, rows, lanes = x.shape
    x = x.reshape(count, rows // tile, tile, lanes)
    return lax.all_to_all(x, axes, 0, 0, tiled=True).reshape(count, rows, lanes)


def swap(x):
    return lax.ppermute(x, "core", [(0, 1), (1, 0)])


def local(pair_rep, cotangent, norm_gain, proj_weight, bias_weight, out_weight, residue_mask):
    gain = norm_gain.reshape(1, CH)
    wbt = bias_weight.T
    wall = proj_weight.reshape(CH, 4, HEADS, DIM).transpose(2, 1, 3, 0).reshape(HEADS, CH, CH)
    masking = (residue_mask.astype(F32) - 1.0) * MASK_FILL
    masking = masking.reshape(N_WIDE, 2, HALF).transpose(1, 0, 2).reshape(LENGTH)
    masking = jnp.broadcast_to(masking[:, None], (LENGTH, CH))
    tile_f32 = pltpu.VMEM((TILE, CH), F32)
    half = DEVICES // 2

    send, normed = call(
        pre_kernel,
        [shape(2, COLS, IN_ROWS, CH), shape(TILE, CH)],
        [
            pltpu.VMEM((ROWS, COLS, CH), BF),
            pltpu.VMEM((ROWS, COLS, CH), BF),
            pltpu.VMEM((1, CH), F32),
            pltpu.VMEM((HEADS, CH), BF),
            pltpu.VMEM((2, COLS, IN_ROWS, CH), BF),
            pltpu.VMEM((TILE, CH), BF),
            tile_f32,
            tile_f32,
            pltpu.SemaphoreType.DMA((4,)),
            pltpu.SemaphoreType.DMA((PARTS + 1,)),
        ],
        hbm=True,
        vmem=63,
    )(pair_rep, cotangent, gain, wbt)
    own = exchange(send.reshape(half, IN_ROWS, CH), CHIPS, 4)
    other = swap(own)
    keep, give = call(
        attention_kernel,
        [shape(N_CHIP, N_NARROW, MID_ROWS, CH)] * 2,
        [
            pltpu.VMEM((2, LENGTH, CH), F32),
            pltpu.VMEM((2, LENGTH, CH), F32),
            pltpu.VMEM((DEVICES * 8, CH), F32),
            pltpu.VMEM((CH, CH), F32),
            pltpu.VMEM((CH, CH), F32),
            pltpu.VMEM((2 * DIM, CH), F32),
        ],
    )(
        own.reshape(N_CHIP, N_NARROW, IN_ROWS, CH),
        other.reshape(N_CHIP, N_NARROW, IN_ROWS, CH),
        wall,
        out_weight,
        masking,
    )
    got = swap(give)
    mid = call(join_kernel, shape(half, SUM_ROWS, CH))(
        keep.reshape(half, MID_ROWS, CH), got.reshape(half, MID_ROWS, CH)
    )
    mid = exchange(mid, CHIPS, 8).reshape(2, COLS, SUM_ROWS, CH)
    send, bias = call(reduce_kernel, [shape(DEVICES * OUT_ROWS, CH), shape(8, TILE)])(mid, normed)
    last = exchange(send.reshape(DEVICES, OUT_ROWS, CH), BOTH, 2)
    d_pair = call(
        pair_kernel,
        shape(ROWS, COLS, CH),
        [tile_f32],
        pl.CostEstimate(flops=100_000_000, bytes_accessed=4_000_000, transcendentals=512),
    )(mid, bias, pair_rep, gain, wbt)
    grad_proj, grad_bias, grad_out, grad_gain = call(
        final_kernel,
        [
            shape(CH, 4 * CH, dtype=F32),
            shape(HEADS, CH, dtype=F32),
            shape(CH, CH, dtype=F32),
            shape(1, CH, dtype=F32),
        ],
        [pltpu.VMEM((DEVICES * OUT_ROWS, CH), F32)],
    )(last.reshape(DEVICES * OUT_ROWS, CH), proj_weight, wbt, gain)
    return (d_pair, grad_proj, grad_bias.T, grad_out, grad_gain.reshape(CH))


def solution(mesh):
    cores = Mesh(mesh.devices.reshape(N_CHIP, 2, N_NARROW), BOTH)
    tile = P(("chip", "core"), "narrow", None)
    in_specs = (tile, tile, P(), P(), P(), P(), P())
    out_specs = (tile, P(), P(), P(), P())
    return jax.shard_map(local, mesh=cores, in_specs=in_specs, out_specs=out_specs, check_vma=False)
```

```python
import jax
import jax.numpy as jnp
from jax import lax
from jax.experimental import pallas as pl
from jax.experimental.pallas import tpu as pltpu
from jax.sharding import Mesh, PartitionSpec as P

NORM_EPSILON = 1e-05
MASK_FILL = 1000000000.0
BF = jnp.bfloat16
F32 = jnp.float32
CHIPS = ("chip", "narrow")
BOTH = ("chip", "core", "narrow")

ROWS = 16
COLS = 32
TILE = ROWS * COLS
N_WIDE = 16
N_CHIP = 8
N_NARROW = 8
DEVICES = N_WIDE * N_NARROW
LENGTH = 256
CH = 128
HEADS = 4
DIM = 32
HALF = 8
IN_ROWS = 32
TOGETHER = 8
MID_ROWS = 24
SUM_ROWS = 32
OUT_ROWS = 10

NT = (((1,), (1,)), ((), ()))
NN = (((1,), (0,)), ((), ()))
TN = (((0,), (0,)), ((), ()))


def mm(a, b, dims=NN):
    return lax.dot_general(a, b, dims, preferred_element_type=F32)


def normal(x):
    centered = x - jnp.mean(x, axis=-1, keepdims=True)
    inverse = lax.rsqrt(jnp.mean(centered * centered, axis=-1, keepdims=True) + NORM_EPSILON)
    return centered * inverse, inverse


def lane_group(shape, size=DIM):
    return lax.broadcasted_iota(jnp.int32, shape, 1) // size


def turn(x, lanes):
    lanes %= CH
    return pltpu.roll(x, lanes, 1) if lanes else x


def pre_kernel(
    pair_hbm, cot_hbm, gain_hbm, wbt_hbm, send_ref, normed_ref,
    pair_v, cot_v, gain_v, wbt_v, xs, cs, sems,
):
    copies = [
        pltpu.make_async_copy(src, dst, sems.at[i])
        for i, (src, dst) in enumerate(
            ((pair_hbm, pair_v), (gain_hbm, gain_v), (wbt_hbm, wbt_v), (cot_hbm, cot_v))
        )
    ]
    for copy in copies:
        copy.start()
    copies[0].wait()
    hat, _ = normal(pair_v[...].astype(F32).reshape(TILE, CH))
    copies[1].wait()
    normed = (hat * gain_v[...]).astype(BF).astype(F32)
    xs[...] = normed
    groups = normed.reshape(TILE // (2 * HALF), 2, HALF, CH)
    halves = [groups[:, s].reshape(TILE // 2, CH) for s in range(2)]
    split = jnp.concatenate(halves, axis=0).astype(BF)
    normed_ref[...] = split
    copies[2].wait()
    bias = mm(wbt_v[...], split, NT)
    chunks = [
        jnp.concatenate(
            [
                bias[h : h + 1, (2 * s + kb) * CH : (2 * s + kb + 1) * CH]
                for h in range(HEADS)
                for kb in range(2)
            ],
            axis=0,
        )
        for s in range(2)
    ]
    copies[3].wait()
    cs[...] = cot_v[...].astype(F32).reshape(TILE, CH)
    for col in range(COLS):
        x = xs[pl.ds(col, ROWS, stride=COLS), :].astype(BF)
        c = cs[pl.ds(col, ROWS, stride=COLS), :]
        for s in range(2):
            send_ref[s, col, 0:16, :] = x
            rest = jnp.concatenate([c[s * HALF : (s + 1) * HALF], chunks[s]], axis=0)
            send_ref[s, col, 16:32, :] = rest.astype(BF)


def attention_kernel(
    own_ref, other_ref, wall_ref, ow_ref, mask_ref, keep_ref, give_ref,
    bias_s, sum_s, tail_s, kv_s, qg_s, gout_s,
):
    core = lax.axis_index("core")
    side = lax.axis_index("chip") // 4
    scale = DIM**-0.5
    two = [wall_ref[2 * core + hh] for hh in range(2)]
    w_kv = jnp.concatenate([w[DIM : 3 * DIM] for w in two], axis=0)
    w_qg = jnp.concatenate([w[:DIM] for w in two] + [w[3 * DIM :] for w in two], axis=0)
    out_w = ow_ref[pl.ds(pl.multiple_of(core * 2 * DIM, 2 * DIM), 2 * DIM), :]
    zero = jnp.zeros((DIM, CH), BF)

    def rows(n, start):
        own, other = [ref[:, n, start : start + ROWS, :] for ref in (own_ref, other_ref)]
        low, high = jnp.where(core == 0, own, other), jnp.where(core == 0, other, own)
        both = jnp.stack([low, high], axis=1).astype(F32).reshape(N_WIDE, 2, HALF, CH)
        return [both[:, i].reshape(N_WIDE * HALF, CH) for i in range(2)]

    group = lane_group((N_WIDE, CH), 16)
    for n in range(N_NARROW):
        tail_s[n * CH : (n + 1) * CH, :] = rows(n, 16)[1]
    for hh in range(2):
        for kb in range(2):
            got = []
            for n in range(N_NARROW):
                at = n * CH + 2 * hh + kb
                first = tail_s[pl.ds(at, N_WIDE, stride=8), :]
                second = tail_s[pl.ds(at + 4, N_WIDE, stride=8), :]
                got.append(jnp.where(core == 0, first, second))
            for kq in range(HALF):
                acc = got[0]
                acc = turn(acc, -kq * 16)
                for n in range(1, N_NARROW):
                    acc = jnp.where(group == n, turn(got[n], (n - kq) * 16), acc)
                bias_s.at[hh][pl.ds(kb * CH + kq, N_WIDE, stride=HALF), :] = acc

    class Unit:
        pass

    def project(n):
        u = Unit()
        u.n = n
        parts = [part.astype(BF) for part in rows(n, 0)]
        u.x = jnp.concatenate(parts, axis=0)
        u.x_own = jnp.where(side == 0, parts[0], parts[1])
        u.cot = rows(n, 16)[0].astype(BF)
        kv_t = mm(w_kv, u.x, NT).astype(BF)
        qg = mm(w_qg, u.x_own, NT)
        og = mm(out_w, u.cot, NT)
        u.pieces = []
        for hh in range(2):
            h = Unit()
            h.n, h.hh = n, hh
            h.kv = mm(u.x, w_kv[2 * hh * DIM : (2 * hh + 2) * DIM], NT).astype(BF)
            h.q = qg[hh * DIM : (hh + 1) * DIM].astype(BF)
            h.gate = jax.nn.sigmoid(qg[(2 + hh) * DIM : (3 + hh) * DIM])
            h.og = og[hh * DIM : (hh + 1) * DIM]
            h.da = (h.og * h.gate).astype(BF)
            h.k, h.v = [kv_t[(2 * hh + t) * DIM : (2 * hh + t + 1) * DIM] for t in range(2)]
            u.pieces.append(h)
        return u

    def score(h):
        right = jnp.concatenate(
            [jnp.concatenate(pair, axis=1) for pair in ((h.q, zero), (zero, h.da))], axis=0
        )
        both = mm(h.kv, right)
        h.logits, h.d_soft = both[:, :CH], both[:, CH:]

    def softmax(h):
        logits = h.logits * scale + bias_s[h.hh] + mask_ref[...]
        top = jnp.max(logits, axis=0, keepdims=True)
        e = jnp.exp(logits - top)
        h.soft = e * (1.0 / jnp.sum(e, axis=0, keepdims=True))
        h.soft_bf = h.soft.astype(BF)

    def attend(h):
        h.att = mm(h.v, h.soft_bf)
        h.delta = jnp.sum(h.da.astype(F32) * h.att, axis=0, keepdims=True)

    def logit_grads(h):
        h.d_log = (h.soft * (h.d_soft - h.delta)).astype(BF)
        if h.n == 0:
            sum_s[h.hh] = h.d_log.astype(F32)
        else:
            sum_s[h.hh] += h.d_log.astype(F32)

    def gradients(h):
        h.dq = mm(h.k, h.d_log) * scale
        h.dk = mm(h.q, h.d_log, NT) * scale
        h.dv = mm(h.da, h.soft_bf, NT)
        h.dg = h.og * h.att * h.gate * (1.0 - h.gate)
        h.gated = (h.gate * h.att).astype(BF)

    def emit(u):
        one, other = u.pieces
        kv_grads = jnp.concatenate([one.dk, one.dv, other.dk, other.dv], axis=0).astype(BF)
        qg_grads = jnp.concatenate([one.dq, other.dq, one.dg, other.dg], axis=0).astype(BF)
        gated = jnp.concatenate([one.gated, other.gated], axis=0)
        sums = (mm(kv_grads, u.x), mm(qg_grads, u.x_own), mm(gated, u.cot))
        for ref, part in zip((kv_s, qg_s, gout_s), sums):
            if u.n == 0:
                ref[...] = part
            else:
                ref[...] += part
        d_normed = mm(kv_grads, w_kv, TN)
        d_own = mm(qg_grads, w_qg, TN)
        both = [
            (d_normed[i * CH : (i + 1) * CH] + jnp.where(side == i, d_own, 0.0)).reshape(
                N_CHIP, 2, HALF, CH
            )
            for i in range(2)
        ]
        put(jnp.concatenate(both, axis=2).astype(BF), u.n, 0, 16)

    def put(value, n, start, stop):
        even, odd = value[:, 0], value[:, 1]
        keep_ref[:, n, start:stop, :] = jnp.where(core == 0, even, odd)
        give_ref[:, n, start:stop, :] = jnp.where(core == 0, odd, even)

    for first in range(0, N_NARROW, TOGETHER):
        units = [project(n) for n in range(first, first + TOGETHER)]
        flat = [h for u in units for h in u.pieces]
        for step in (score, softmax, attend, logit_grads, gradients):
            for h in flat:
                step(h)
        for u in units:
            emit(u)

    for hh in range(2):
        for kb in range(2):
            got = [
                sum_s.at[hh][pl.ds(kb * CH + kq, N_WIDE, stride=HALF), :] for kq in range(HALF)
            ]
            for n in range(N_NARROW):
                acc = turn(got[0], -n * 16)
                for kq in range(1, HALF):
                    acc = jnp.where(group == kq, turn(got[kq], (kq - n) * 16), acc)
                tail_s[pl.ds(n * 8 + 2 * hh + kb, N_WIDE, stride=64), :] = acc
    tail_s[pl.ds(4, DEVICES, stride=8), :] = jnp.transpose(kv_s[...])
    tail_s[pl.ds(5, DEVICES, stride=8), :] = jnp.transpose(qg_s[...])
    for hh in range(2):
        out_part = gout_s[hh * DIM : (hh + 1) * DIM, :]
        for r in range(4):
            tail_s[pl.ds(6 + hh + 8 * r, DIM, stride=32), :] = out_part
    tail = tail_s[...].astype(BF).reshape(N_CHIP, 2, N_NARROW, 8, CH)
    put(tail, slice(None), 16, 24)


def join_kernel(keep_ref, got_ref, send_ref):
    core = lax.axis_index("core")
    total = keep_ref[:, 0:16, :].astype(F32) + got_ref[:, 0:16, :].astype(F32)
    send_ref[:, 0:16, :] = total.astype(BF)
    keep, got = keep_ref[:, 16:24, :], got_ref[:, 16:24, :]
    send_ref[:, 16:24, :] = jnp.where(core == 0, keep, got)
    send_ref[:, 24:32, :] = jnp.where(core == 0, got, keep)


def reduce_kernel(recv_ref, normed_ref, send_ref, bias_ref):
    sums = [
        [
            jnp.sum(recv_ref[s, :, 16 + 8 * c : 24 + 8 * c, :].astype(F32), axis=0)
            for c in range(2)
        ]
        for s in range(2)
    ]
    blocks = []
    for s in range(2):
        for kb in range(2):
            parts = [sums[s][h // 2][h % 2 * 2 + kb :][:1] for h in range(HEADS)]
            blocks.append(jnp.concatenate(parts, axis=0))
    bias = jnp.concatenate(blocks, axis=1)
    bias = jnp.concatenate([bias, jnp.zeros_like(bias)], axis=0).astype(BF)
    bias_ref[...] = bias
    grad_bias = mm(bias, normed_ref[...])[:HEADS]
    total = [sums[0][c] + sums[1][c] for c in range(2)]
    group = lane_group((1, CH))
    rows = []
    for t in range(4):
        row = jnp.zeros((1, CH), F32)
        for h in range(HEADS):
            own = total[h // 2]
            got, place = {
                0: (own[5:6], h % 2),
                1: (own[4:5], h % 2 * 2),
                2: (own[4:5], h % 2 * 2 + 1),
                3: (own[5:6], 2 + h % 2),
            }[t]
            row = jnp.where(group == h, turn(got, (h - place) * DIM), row)
        rows.append(row)
    place = lax.rem(lax.axis_index("narrow"), 4)
    row = jnp.zeros((1, CH), F32)
    for h in range(HEADS):
        shift = lax.rem(h * DIM + CH - place * DIM, CH)
        got = total[h // 2][6 + h % 2 :][:1]
        row = jnp.where(group == h, pltpu.roll(got, shift, 1), row)
    rows += [row, jnp.zeros((1, CH), F32), grad_bias]
    chunk = jnp.concatenate(rows, axis=0)
    block = jnp.concatenate([chunk] * 8, axis=0).astype(BF)
    for i in range(DEVICES // 8):
        send_ref[i * 80 : (i + 1) * 80, :] = block


def pair_kernel(recv_ref, bias_ref, pair_ref, gain_ref, wbt_ref, out_ref, ds):
    total = recv_ref[0, :, 0:16, :].astype(F32) + recv_ref[1, :, 0:16, :].astype(F32)
    ds[...] = total.reshape(TILE, CH)
    d_normed = jnp.concatenate([ds[pl.ds(r, COLS, stride=ROWS), :] for r in range(ROWS)], axis=0)
    wbt = wbt_ref[...].astype(F32)
    wbt = jnp.concatenate([wbt, jnp.zeros_like(wbt)], axis=0).astype(BF)
    split = mm(bias_ref[...], wbt, TN).reshape(2, TILE // (2 * HALF), HALF, CH)
    d_normed = d_normed + jnp.stack([split[0], split[1]], axis=1).reshape(TILE, CH)
    hat, inverse = normal(pair_ref[...].astype(F32).reshape(TILE, CH))
    d_hat = d_normed * gain_ref[...]
    d_pair = inverse * (
        d_hat
        - jnp.mean(d_hat, axis=-1, keepdims=True)
        - hat * jnp.mean(d_hat * hat, axis=-1, keepdims=True)
    )
    out_ref[...] = d_pair.astype(BF).reshape(ROWS, COLS, CH)


def final_kernel(recv_ref, pw_ref, wbt_ref, gain_ref, gp_ref, gb_ref, go_ref, gg_ref, vs):
    vs[...] = recv_ref[...].astype(F32)
    dots = jnp.zeros((CH, CH), F32)
    for t in range(4):
        got = vs[pl.ds(t, CH, stride=OUT_ROWS), :]
        gp_ref[:, t * CH : (t + 1) * CH] = got
        dots = dots + got * pw_ref[:, t * CH : (t + 1) * CH].astype(F32)
    group = lane_group((DIM, CH))
    quarters = [vs[pl.ds(OUT_ROWS * q + 4, DIM, stride=4 * OUT_ROWS), :] for q in range(4)]
    for h in range(HEADS):
        acc = jnp.zeros((DIM, CH), F32)
        for q in range(4):
            shift = (q - h) * COLS % CH
            got = pltpu.roll(quarters[q], shift, 1) if shift else quarters[q]
            acc = jnp.where(group == q, got, acc)
        go_ref[h * DIM : (h + 1) * DIM, :] = acc
    grad_bias = jnp.concatenate(
        [
            jnp.sum(vs[pl.ds(6 + h, DEVICES, stride=OUT_ROWS), :], axis=0, keepdims=True)
            for h in range(HEADS)
        ],
        axis=0,
    )
    gb_ref[...] = grad_bias
    dots_row = jnp.sum(jnp.transpose(dots), axis=0, keepdims=True)
    bias_row = jnp.sum(grad_bias * wbt_ref[...].astype(F32), axis=0, keepdims=True)
    gg_ref[...] = (dots_row + bias_row) / gain_ref[...]


def call(kernel, out_shape, scratch=(), cost=None, hbm=False):
    many = isinstance(out_shape, (list, tuple))
    spec = pl.BlockSpec(memory_space=pltpu.VMEM)
    in_spec = pl.BlockSpec(memory_space=pltpu.HBM) if hbm else spec

    def run(*args):
        return pl.pallas_call(
            kernel,
            out_shape=out_shape,
            in_specs=[in_spec] * len(args),
            out_specs=[spec] * len(out_shape) if many else spec,
            scratch_shapes=list(scratch),
            compiler_params=pltpu.CompilerParams(vmem_limit_bytes=32 * 1024 * 1024),
            cost_estimate=cost,
        )(*args)

    return run


def shape(*dims, dtype=BF):
    return jax.ShapeDtypeStruct(dims, dtype)


def exchange(x, axes, tile):
    count, rows, lanes = x.shape
    x = x.reshape(count, rows // tile, tile, lanes)
    return lax.all_to_all(x, axes, 0, 0, tiled=True).reshape(count, rows, lanes)


def swap(x):
    return lax.ppermute(x, "core", [(0, 1), (1, 0)])


def local(pair_rep, cotangent, norm_gain, proj_weight, bias_weight, out_weight, residue_mask):
    gain = norm_gain.reshape(1, CH)
    wbt = bias_weight.T
    wall = proj_weight.reshape(CH, 4, HEADS, DIM).transpose(2, 1, 3, 0).reshape(HEADS, CH, CH)
    masking = (residue_mask.astype(F32) - 1.0) * MASK_FILL
    masking = masking.reshape(N_WIDE, 2, HALF).transpose(1, 0, 2).reshape(LENGTH)
    masking = jnp.broadcast_to(masking[:, None], (LENGTH, CH))
    tile_f32 = pltpu.VMEM((TILE, CH), F32)
    half = DEVICES // 2

    send, normed = call(
        pre_kernel,
        [pltpu.VMEM((2, COLS, IN_ROWS, CH), BF), pltpu.VMEM((TILE, CH), BF)],
        [
            pltpu.VMEM((ROWS, COLS, CH), BF),
            pltpu.VMEM((ROWS, COLS, CH), BF),
            pltpu.VMEM((1, CH), F32),
            pltpu.VMEM((HEADS, CH), BF),
            tile_f32,
            tile_f32,
            pltpu.SemaphoreType.DMA((4,)),
        ],
        hbm=True,
    )(*[pltpu.with_memory_space_constraint(a, pltpu.HBM) for a in (pair_rep, cotangent, gain, wbt)])
    own = exchange(send.reshape(half, IN_ROWS, CH), CHIPS, 4)
    other = swap(own)
    keep, give = call(
        attention_kernel,
        [pltpu.VMEM((N_CHIP, N_NARROW, MID_ROWS, CH), BF)] * 2,
        [
            pltpu.VMEM((2, LENGTH, CH), F32),
            pltpu.VMEM((2, LENGTH, CH), F32),
            pltpu.VMEM((DEVICES * 8, CH), F32),
            pltpu.VMEM((CH, CH), F32),
            pltpu.VMEM((CH, CH), F32),
            pltpu.VMEM((2 * DIM, CH), F32),
        ],
    )(
        own.reshape(N_CHIP, N_NARROW, IN_ROWS, CH),
        other.reshape(N_CHIP, N_NARROW, IN_ROWS, CH),
        wall,
        out_weight,
        masking,
    )
    got = swap(give)
    mid = call(join_kernel, pltpu.VMEM((half, SUM_ROWS, CH), BF))(
        keep.reshape(half, MID_ROWS, CH), got.reshape(half, MID_ROWS, CH)
    )
    mid = exchange(mid, CHIPS, 8).reshape(2, COLS, SUM_ROWS, CH)
    send, bias = call(reduce_kernel, [pltpu.VMEM((DEVICES * OUT_ROWS, CH), BF), pltpu.VMEM((8, TILE), BF)])(mid, normed)
    last = exchange(send.reshape(DEVICES, OUT_ROWS, CH), BOTH, 2)
    d_pair = call(
        pair_kernel,
        shape(ROWS, COLS, CH),
        [tile_f32],
        pl.CostEstimate(flops=100_000_000, bytes_accessed=4_000_000, transcendentals=512),
    )(mid, bias, pair_rep, gain, wbt)
    grad_proj, grad_bias, grad_out, grad_gain = call(
        final_kernel,
        [
            shape(CH, 4 * CH, dtype=F32),
            shape(HEADS, CH, dtype=F32),
            shape(CH, CH, dtype=F32),
            shape(1, CH, dtype=F32),
        ],
        [pltpu.VMEM((DEVICES * OUT_ROWS, CH), F32)],
    )(last.reshape(DEVICES * OUT_ROWS, CH), proj_weight, wbt, gain)
    return (d_pair, grad_proj, grad_bias.T, grad_out, grad_gain.reshape(CH))


def solution(mesh):
    cores = Mesh(mesh.devices.reshape(N_CHIP, 2, N_NARROW), BOTH)
    tile = P(("chip", "core"), "narrow", None)
    in_specs = (tile, tile, P(), P(), P(), P(), P())
    out_specs = (tile, P(), P(), P(), P())
    return jax.shard_map(local, mesh=cores, in_specs=in_specs, out_specs=out_specs, check_vma=False)
```

```python
import jax
import jax.numpy as jnp
from jax import lax
from jax.experimental import pallas as pl
from jax.experimental.pallas import tpu as pltpu
from jax.sharding import Mesh, PartitionSpec as P

NORM_EPSILON = 1e-05
MASK_FILL = 1000000000.0
BF = jnp.bfloat16
F32 = jnp.float32
CHIPS = ("chip", "narrow")
BOTH = ("chip", "core", "narrow")

ROWS = 16
COLS = 32
TILE = ROWS * COLS
N_WIDE = 16
N_CHIP = 8
N_NARROW = 8
DEVICES = N_WIDE * N_NARROW
LENGTH = 256
CH = 128
HEADS = 4
DIM = 32
HALF = 8
IN_ROWS = 32
TOGETHER = 8
MID_ROWS = 24
SUM_ROWS = 32
OUT_ROWS = 10

NT = (((1,), (1,)), ((), ()))
NN = (((1,), (0,)), ((), ()))
TN = (((0,), (0,)), ((), ()))


def mm(a, b, dims=NN):
    return lax.dot_general(a, b, dims, preferred_element_type=F32)


def normal(x):
    centered = x - jnp.mean(x, axis=-1, keepdims=True)
    inverse = lax.rsqrt(jnp.mean(centered * centered, axis=-1, keepdims=True) + NORM_EPSILON)
    return centered * inverse, inverse


def lane_group(shape, size=DIM):
    return lax.broadcasted_iota(jnp.int32, shape, 1) // size


def turn(x, lanes):
    lanes %= CH
    return pltpu.roll(x, lanes, 1) if lanes else x


def pre_kernel(
    pair_hbm, cot_hbm, gain_hbm, wbt_hbm, send_ref, normed_ref, pair_v, gain_v, wbt_v,
    cot_v, xs, cs, sems,
):
    copies = [
        pltpu.make_async_copy(src, dst, sems.at[i])
        for i, (src, dst) in enumerate(
            ((pair_hbm, pair_v), (gain_hbm, gain_v), (wbt_hbm, wbt_v), (cot_hbm, cot_v))
        )
    ]
    for copy in copies:
        copy.start()
    for copy in copies:
        copy.wait()
    cs[...] = cot_v[...].astype(F32).reshape(TILE, CH)
    hat, _ = normal(pair_v[...].astype(F32).reshape(TILE, CH))
    normed = (hat * gain_v[...]).astype(BF).astype(F32)
    xs[...] = normed
    groups = normed.reshape(TILE // (2 * HALF), 2, HALF, CH)
    halves = [groups[:, s].reshape(TILE // 2, CH) for s in range(2)]
    split = jnp.concatenate(halves, axis=0).astype(BF)
    normed_ref[...] = split
    bias = mm(wbt_v[...], split, NT)
    chunks = [
        jnp.concatenate(
            [
                bias[h : h + 1, (2 * s + kb) * CH : (2 * s + kb + 1) * CH]
                for h in range(HEADS)
                for kb in range(2)
            ],
            axis=0,
        )
        for s in range(2)
    ]
    for col in range(COLS):
        x = xs[pl.ds(col, ROWS, stride=COLS), :].astype(BF)
        c = cs[pl.ds(col, ROWS, stride=COLS), :]
        for s in range(2):
            send_ref[s, col, 0:16, :] = x
            rest = jnp.concatenate([c[s * HALF : (s + 1) * HALF], chunks[s]], axis=0)
            send_ref[s, col, 16:32, :] = rest.astype(BF)


def attention_kernel(
    own_ref, other_ref, wall_ref, ow_ref, mask_ref, keep_ref, give_ref,
    bias_s, sum_s, tail_s, kv_s, qg_s, gout_s,
):
    core = lax.axis_index("core")
    side = lax.axis_index("chip") // 4
    scale = DIM**-0.5
    two = [wall_ref[2 * core + hh] for hh in range(2)]
    w_kv = jnp.concatenate([w[DIM : 3 * DIM] for w in two], axis=0)
    w_qg = jnp.concatenate([w[:DIM] for w in two] + [w[3 * DIM :] for w in two], axis=0)
    out_w = ow_ref[pl.ds(pl.multiple_of(core * 2 * DIM, 2 * DIM), 2 * DIM), :]
    zero = jnp.zeros((DIM, CH), BF)

    def rows(n, start):
        own, other = [ref[:, n, start : start + ROWS, :] for ref in (own_ref, other_ref)]
        low, high = jnp.where(core == 0, own, other), jnp.where(core == 0, other, own)
        both = jnp.stack([low, high], axis=1).astype(F32).reshape(N_WIDE, 2, HALF, CH)
        return [both[:, i].reshape(N_WIDE * HALF, CH) for i in range(2)]

    group = lane_group((N_WIDE, CH), 16)
    for n in range(N_NARROW):
        tail_s[n * CH : (n + 1) * CH, :] = rows(n, 16)[1]
    for hh in range(2):
        for kb in range(2):
            got = []
            for n in range(N_NARROW):
                at = n * CH + 2 * hh + kb
                first = tail_s[pl.ds(at, N_WIDE, stride=8), :]
                second = tail_s[pl.ds(at + 4, N_WIDE, stride=8), :]
                got.append(jnp.where(core == 0, first, second))
            for kq in range(HALF):
                acc = got[0]
                acc = turn(acc, -kq * 16)
                for n in range(1, N_NARROW):
                    acc = jnp.where(group == n, turn(got[n], (n - kq) * 16), acc)
                bias_s.at[hh][pl.ds(kb * CH + kq, N_WIDE, stride=HALF), :] = acc

    class Unit:
        pass

    def project(n):
        u = Unit()
        u.n = n
        parts = [part.astype(BF) for part in rows(n, 0)]
        u.x = jnp.concatenate(parts, axis=0)
        u.x_own = jnp.where(side == 0, parts[0], parts[1])
        u.cot = rows(n, 16)[0].astype(BF)
        kv_t = mm(w_kv, u.x, NT).astype(BF)
        qg = mm(w_qg, u.x_own, NT)
        og = mm(out_w, u.cot, NT)
        u.pieces = []
        for hh in range(2):
            h = Unit()
            h.n, h.hh = n, hh
            h.kv = mm(u.x, w_kv[2 * hh * DIM : (2 * hh + 2) * DIM], NT).astype(BF)
            h.q = qg[hh * DIM : (hh + 1) * DIM].astype(BF)
            h.gate = jax.nn.sigmoid(qg[(2 + hh) * DIM : (3 + hh) * DIM])
            h.og = og[hh * DIM : (hh + 1) * DIM]
            h.da = (h.og * h.gate).astype(BF)
            h.k, h.v = [kv_t[(2 * hh + t) * DIM : (2 * hh + t + 1) * DIM] for t in range(2)]
            u.pieces.append(h)
        return u

    def score(h):
        right = jnp.concatenate(
            [jnp.concatenate(pair, axis=1) for pair in ((h.q, zero), (zero, h.da))], axis=0
        )
        both = mm(h.kv, right)
        h.logits, h.d_soft = both[:, :CH], both[:, CH:]

    def softmax(h):
        logits = h.logits * scale + bias_s[h.hh] + mask_ref[...]
        top = jnp.max(logits, axis=0, keepdims=True)
        e = jnp.exp(logits - top)
        h.soft = e * (1.0 / jnp.sum(e, axis=0, keepdims=True))
        h.soft_bf = h.soft.astype(BF)

    def attend(h):
        h.att = mm(h.v, h.soft_bf)
        h.delta = jnp.sum(h.da.astype(F32) * h.att, axis=0, keepdims=True)

    def logit_grads(h):
        h.d_log = (h.soft * (h.d_soft - h.delta)).astype(BF)
        if h.n == 0:
            sum_s[h.hh] = h.d_log.astype(F32)
        else:
            sum_s[h.hh] += h.d_log.astype(F32)

    def gradients(h):
        h.dq = mm(h.k, h.d_log) * scale
        h.dk = mm(h.q, h.d_log, NT) * scale
        h.dv = mm(h.da, h.soft_bf, NT)
        h.dg = h.og * h.att * h.gate * (1.0 - h.gate)
        h.gated = (h.gate * h.att).astype(BF)

    def emit(u):
        one, other = u.pieces
        kv_grads = jnp.concatenate([one.dk, one.dv, other.dk, other.dv], axis=0).astype(BF)
        qg_grads = jnp.concatenate([one.dq, other.dq, one.dg, other.dg], axis=0).astype(BF)
        gated = jnp.concatenate([one.gated, other.gated], axis=0)
        sums = (mm(kv_grads, u.x), mm(qg_grads, u.x_own), mm(gated, u.cot))
        for ref, part in zip((kv_s, qg_s, gout_s), sums):
            if u.n == 0:
                ref[...] = part
            else:
                ref[...] += part
        d_normed = mm(kv_grads, w_kv, TN)
        d_own = mm(qg_grads, w_qg, TN)
        both = [
            (d_normed[i * CH : (i + 1) * CH] + jnp.where(side == i, d_own, 0.0)).reshape(
                N_CHIP, 2, HALF, CH
            )
            for i in range(2)
        ]
        put(jnp.concatenate(both, axis=2).astype(BF), u.n, 0, 16)

    def put(value, n, start, stop):
        even, odd = value[:, 0], value[:, 1]
        keep_ref[:, n, start:stop, :] = jnp.where(core == 0, even, odd)
        give_ref[:, n, start:stop, :] = jnp.where(core == 0, odd, even)

    for first in range(0, N_NARROW, TOGETHER):
        units = [project(n) for n in range(first, first + TOGETHER)]
        flat = [h for u in units for h in u.pieces]
        for step in (score, softmax, attend, logit_grads, gradients):
            for h in flat:
                step(h)
        for u in units:
            emit(u)

    for hh in range(2):
        for kb in range(2):
            got = [
                sum_s.at[hh][pl.ds(kb * CH + kq, N_WIDE, stride=HALF), :] for kq in range(HALF)
            ]
            for n in range(N_NARROW):
                acc = turn(got[0], -n * 16)
                for kq in range(1, HALF):
                    acc = jnp.where(group == kq, turn(got[kq], (kq - n) * 16), acc)
                tail_s[pl.ds(n * 8 + 2 * hh + kb, N_WIDE, stride=64), :] = acc
    tail_s[pl.ds(4, DEVICES, stride=8), :] = jnp.transpose(kv_s[...])
    tail_s[pl.ds(5, DEVICES, stride=8), :] = jnp.transpose(qg_s[...])
    for hh in range(2):
        out_part = gout_s[hh * DIM : (hh + 1) * DIM, :]
        for r in range(4):
            tail_s[pl.ds(6 + hh + 8 * r, DIM, stride=32), :] = out_part
    tail = tail_s[...].astype(BF).reshape(N_CHIP, 2, N_NARROW, 8, CH)
    put(tail, slice(None), 16, 24)


def join_kernel(keep_ref, got_ref, send_ref):
    core = lax.axis_index("core")
    total = keep_ref[:, 0:16, :].astype(F32) + got_ref[:, 0:16, :].astype(F32)
    send_ref[:, 0:16, :] = total.astype(BF)
    keep, got = keep_ref[:, 16:24, :], got_ref[:, 16:24, :]
    send_ref[:, 16:24, :] = jnp.where(core == 0, keep, got)
    send_ref[:, 24:32, :] = jnp.where(core == 0, got, keep)


def reduce_kernel(recv_ref, normed_ref, send_ref, bias_ref):
    sums = [
        [
            jnp.sum(recv_ref[s, :, 16 + 8 * c : 24 + 8 * c, :].astype(F32), axis=0)
            for c in range(2)
        ]
        for s in range(2)
    ]
    blocks = []
    for s in range(2):
        for kb in range(2):
            parts = [sums[s][h // 2][h % 2 * 2 + kb :][:1] for h in range(HEADS)]
            blocks.append(jnp.concatenate(parts, axis=0))
    bias = jnp.concatenate(blocks, axis=1)
    bias = jnp.concatenate([bias, jnp.zeros_like(bias)], axis=0).astype(BF)
    bias_ref[...] = bias
    grad_bias = mm(bias, normed_ref[...])[:HEADS]
    total = [sums[0][c] + sums[1][c] for c in range(2)]
    group = lane_group((1, CH))
    rows = []
    for t in range(4):
        row = jnp.zeros((1, CH), F32)
        for h in range(HEADS):
            own = total[h // 2]
            got, place = {
                0: (own[5:6], h % 2),
                1: (own[4:5], h % 2 * 2),
                2: (own[4:5], h % 2 * 2 + 1),
                3: (own[5:6], 2 + h % 2),
            }[t]
            row = jnp.where(group == h, turn(got, (h - place) * DIM), row)
        rows.append(row)
    place = lax.rem(lax.axis_index("narrow"), 4)
    row = jnp.zeros((1, CH), F32)
    for h in range(HEADS):
        shift = lax.rem(h * DIM + CH - place * DIM, CH)
        got = total[h // 2][6 + h % 2 :][:1]
        row = jnp.where(group == h, pltpu.roll(got, shift, 1), row)
    rows += [row, jnp.zeros((1, CH), F32), grad_bias]
    chunk = jnp.concatenate(rows, axis=0)
    block = jnp.concatenate([chunk] * 8, axis=0).astype(BF)
    for i in range(DEVICES // 8):
        send_ref[i * 80 : (i + 1) * 80, :] = block


def pair_grads(recv_ref, bias_ref, pair_ref, gain_ref, wbt_ref, out_ref, ds):
    total = recv_ref[0, :, 0:16, :].astype(F32) + recv_ref[1, :, 0:16, :].astype(F32)
    ds[...] = total.reshape(TILE, CH)
    d_normed = jnp.concatenate([ds[pl.ds(r, COLS, stride=ROWS), :] for r in range(ROWS)], axis=0)
    wbt = wbt_ref[...].astype(F32)
    wbt = jnp.concatenate([wbt, jnp.zeros_like(wbt)], axis=0).astype(BF)
    split = mm(bias_ref[...], wbt, TN).reshape(2, TILE // (2 * HALF), HALF, CH)
    d_normed = d_normed + jnp.stack([split[0], split[1]], axis=1).reshape(TILE, CH)
    hat, inverse = normal(pair_ref[...].astype(F32).reshape(TILE, CH))
    d_hat = d_normed * gain_ref[...]
    d_pair = inverse * (
        d_hat
        - jnp.mean(d_hat, axis=-1, keepdims=True)
        - hat * jnp.mean(d_hat * hat, axis=-1, keepdims=True)
    )
    out_ref[...] = d_pair.astype(BF).reshape(ROWS, COLS, CH)


def final_kernel(
    recv_ref, mid_ref, bias_ref, pair_ref, pw_ref, wbt_ref, gain_ref,
    out_ref, gp_ref, gb_ref, go_ref, gg_ref, vs, ds,
):
    pair_grads(mid_ref, bias_ref, pair_ref, gain_ref, wbt_ref, out_ref, ds)
    vs[...] = recv_ref[...].astype(F32)
    dots = jnp.zeros((CH, CH), F32)
    for t in range(4):
        got = vs[pl.ds(t, CH, stride=OUT_ROWS), :]
        gp_ref[:, t * CH : (t + 1) * CH] = got
        dots = dots + got * pw_ref[:, t * CH : (t + 1) * CH].astype(F32)
    group = lane_group((DIM, CH))
    quarters = [vs[pl.ds(OUT_ROWS * q + 4, DIM, stride=4 * OUT_ROWS), :] for q in range(4)]
    for h in range(HEADS):
        acc = jnp.zeros((DIM, CH), F32)
        for q in range(4):
            shift = (q - h) * COLS % CH
            got = pltpu.roll(quarters[q], shift, 1) if shift else quarters[q]
            acc = jnp.where(group == q, got, acc)
        go_ref[h * DIM : (h + 1) * DIM, :] = acc
    grad_bias = jnp.concatenate(
        [
            jnp.sum(vs[pl.ds(6 + h, DEVICES, stride=OUT_ROWS), :], axis=0, keepdims=True)
            for h in range(HEADS)
        ],
        axis=0,
    )
    gb_ref[...] = grad_bias
    dots_row = jnp.sum(jnp.transpose(dots), axis=0, keepdims=True)
    bias_row = jnp.sum(grad_bias * wbt_ref[...].astype(F32), axis=0, keepdims=True)
    gg_ref[...] = (dots_row + bias_row) / gain_ref[...]


def call(kernel, out_shape, scratch=(), cost=None, hbm=False):
    many = isinstance(out_shape, (list, tuple))
    spec = pl.BlockSpec(memory_space=pltpu.VMEM)
    in_spec = pl.BlockSpec(memory_space=pltpu.HBM) if hbm else spec

    def run(*args):
        return pl.pallas_call(
            kernel,
            out_shape=out_shape,
            in_specs=[in_spec] * len(args),
            out_specs=[spec] * len(out_shape) if many else spec,
            scratch_shapes=list(scratch),
            compiler_params=pltpu.CompilerParams(vmem_limit_bytes=32 * 1024 * 1024),
            cost_estimate=cost,
        )(*args)

    return run


def shape(*dims, dtype=BF):
    return jax.ShapeDtypeStruct(dims, dtype)


def exchange(x, axes, tile):
    count, rows, lanes = x.shape
    x = x.reshape(count, rows // tile, tile, lanes)
    return lax.all_to_all(x, axes, 0, 0, tiled=True).reshape(count, rows, lanes)


def swap(x):
    return lax.ppermute(x, "core", [(0, 1), (1, 0)])


def local(pair_rep, cotangent, norm_gain, proj_weight, bias_weight, out_weight, residue_mask):
    gain = norm_gain.reshape(1, CH)
    wbt = bias_weight.T
    wall = proj_weight.reshape(CH, 4, HEADS, DIM).transpose(2, 1, 3, 0).reshape(HEADS, CH, CH)
    masking = (residue_mask.astype(F32) - 1.0) * MASK_FILL
    masking = masking.reshape(N_WIDE, 2, HALF).transpose(1, 0, 2).reshape(LENGTH)
    masking = jnp.broadcast_to(masking[:, None], (LENGTH, CH))
    tile_f32 = pltpu.VMEM((TILE, CH), F32)
    half = DEVICES // 2

    send, normed, pair_here, gain, wbt = call(
        pre_kernel,
        [
            pltpu.VMEM((2, COLS, IN_ROWS, CH), BF),
            pltpu.VMEM((TILE, CH), BF),
            pltpu.VMEM((ROWS, COLS, CH), BF),
            pltpu.VMEM((1, CH), F32),
            pltpu.VMEM((HEADS, CH), BF),
        ],
        [
            pltpu.VMEM((ROWS, COLS, CH), BF),
            tile_f32,
            tile_f32,
            pltpu.SemaphoreType.DMA((4,)),
        ],
        hbm=True,
    )(*[pltpu.with_memory_space_constraint(a, pltpu.HBM) for a in (pair_rep, cotangent, gain, wbt)])
    own = exchange(send.reshape(half, IN_ROWS, CH), CHIPS, 4)
    other = swap(own)
    keep, give = call(
        attention_kernel,
        [pltpu.VMEM((N_CHIP, N_NARROW, MID_ROWS, CH), BF)] * 2,
        [
            pltpu.VMEM((2, LENGTH, CH), F32),
            pltpu.VMEM((2, LENGTH, CH), F32),
            pltpu.VMEM((DEVICES * 8, CH), F32),
            pltpu.VMEM((CH, CH), F32),
            pltpu.VMEM((CH, CH), F32),
            pltpu.VMEM((2 * DIM, CH), F32),
        ],
    )(
        own.reshape(N_CHIP, N_NARROW, IN_ROWS, CH),
        other.reshape(N_CHIP, N_NARROW, IN_ROWS, CH),
        wall,
        out_weight,
        masking,
    )
    got = swap(give)
    mid = call(join_kernel, pltpu.VMEM((half, SUM_ROWS, CH), BF))(
        keep.reshape(half, MID_ROWS, CH), got.reshape(half, MID_ROWS, CH)
    )
    mid = exchange(mid, CHIPS, 8).reshape(2, COLS, SUM_ROWS, CH)
    send, bias = call(reduce_kernel, [pltpu.VMEM((DEVICES * OUT_ROWS, CH), BF), pltpu.VMEM((8, TILE), BF)])(mid, normed)
    last = exchange(send.reshape(DEVICES, OUT_ROWS, CH), BOTH, 2)
    d_pair, grad_proj, grad_bias, grad_out, grad_gain = call(
        final_kernel,
        [
            shape(ROWS, COLS, CH),
            shape(CH, 4 * CH, dtype=F32),
            shape(HEADS, CH, dtype=F32),
            shape(CH, CH, dtype=F32),
            shape(1, CH, dtype=F32),
        ],
        [pltpu.VMEM((DEVICES * OUT_ROWS, CH), F32), tile_f32],
    )(last.reshape(DEVICES * OUT_ROWS, CH), mid, bias, pair_here, proj_weight, wbt, gain)
    return (d_pair, grad_proj, grad_bias.T, grad_out, grad_gain.reshape(CH))


def solution(mesh):
    cores = Mesh(mesh.devices.reshape(N_CHIP, 2, N_NARROW), BOTH)
    tile = P(("chip", "core"), "narrow", None)
    in_specs = (tile, tile, P(), P(), P(), P(), P())
    out_specs = (tile, P(), P(), P(), P())
    return jax.shard_map(local, mesh=cores, in_specs=in_specs, out_specs=out_specs, check_vma=False)
```

```python
import jax
import jax.numpy as jnp
from jax import lax
from jax.experimental import pallas as pl
from jax.experimental.pallas import tpu as pltpu
from jax.sharding import Mesh, PartitionSpec as P

NORM_EPSILON = 1e-05
MASK_FILL = 1000000000.0
BF = jnp.bfloat16
F32 = jnp.float32
CHIPS = ("chip", "narrow")
BOTH = ("chip", "core", "narrow")

ROWS = 16
COLS = 32
TILE = ROWS * COLS
N_WIDE = 16
N_CHIP = 8
N_NARROW = 8
DEVICES = N_WIDE * N_NARROW
LENGTH = 256
CH = 128
HEADS = 4
DIM = 32
HALF = 8
IN_ROWS = 32
TOGETHER = 8
MID_ROWS = 24
SUM_ROWS = 32
OUT_ROWS = 10

NT = (((1,), (1,)), ((), ()))
NN = (((1,), (0,)), ((), ()))
TN = (((0,), (0,)), ((), ()))


def mm(a, b, dims=NN):
    return lax.dot_general(a, b, dims, preferred_element_type=F32)


def normal(x):
    centered = x - jnp.mean(x, axis=-1, keepdims=True)
    inverse = lax.rsqrt(jnp.mean(centered * centered, axis=-1, keepdims=True) + NORM_EPSILON)
    return centered * inverse, inverse


def lane_group(shape, size=DIM):
    return lax.broadcasted_iota(jnp.int32, shape, 1) // size


def turn(x, lanes):
    lanes %= CH
    return pltpu.roll(x, lanes, 1) if lanes else x


def pre_kernel(
    pair_hbm, cot_hbm, gain_ref, wbt_ref, send_ref, normed_ref, pair_v, gain_v, wbt_v,
    cot_v, xs, cs, sems,
):
    copies = [
        pltpu.make_async_copy(src, dst, sems.at[i])
        for i, (src, dst) in enumerate(
            ((pair_hbm, pair_v), (cot_hbm, cot_v))
        )
    ]
    for copy in copies:
        copy.start()
    gain_v[...] = gain_ref[...]
    wbt_v[...] = wbt_ref[...]
    for copy in copies:
        copy.wait()
    cs[...] = cot_v[...].astype(F32).reshape(TILE, CH)
    hat, _ = normal(pair_v[...].astype(F32).reshape(TILE, CH))
    normed = (hat * gain_ref[...]).astype(BF).astype(F32)
    xs[...] = normed
    groups = normed.reshape(TILE // (2 * HALF), 2, HALF, CH)
    halves = [groups[:, s].reshape(TILE // 2, CH) for s in range(2)]
    split = jnp.concatenate(halves, axis=0).astype(BF)
    normed_ref[...] = split
    bias = mm(wbt_ref[...], split, NT)
    chunks = [
        jnp.concatenate(
            [
                bias[h : h + 1, (2 * s + kb) * CH : (2 * s + kb + 1) * CH]
                for h in range(HEADS)
                for kb in range(2)
            ],
            axis=0,
        )
        for s in range(2)
    ]
    for col in range(COLS):
        x = xs[pl.ds(col, ROWS, stride=COLS), :].astype(BF)
        c = cs[pl.ds(col, ROWS, stride=COLS), :]
        for s in range(2):
            send_ref[s, col, 0:16, :] = x
            rest = jnp.concatenate([c[s * HALF : (s + 1) * HALF], chunks[s]], axis=0)
            send_ref[s, col, 16:32, :] = rest.astype(BF)


def attention_kernel(
    own_ref, other_ref, wall_ref, ow_ref, mask_ref, keep_ref, give_ref,
    bias_s, sum_s, tail_s, kv_s, qg_s, gout_s,
):
    core = lax.axis_index("core")
    side = lax.axis_index("chip") // 4
    scale = DIM**-0.5
    two = [wall_ref[2 * core + hh] for hh in range(2)]
    w_kv = jnp.concatenate([w[DIM : 3 * DIM] for w in two], axis=0)
    w_qg = jnp.concatenate([w[:DIM] for w in two] + [w[3 * DIM :] for w in two], axis=0)
    out_w = ow_ref[pl.ds(pl.multiple_of(core * 2 * DIM, 2 * DIM), 2 * DIM), :]
    zero = jnp.zeros((DIM, CH), BF)

    def rows(n, start):
        own, other = [ref[:, n, start : start + ROWS, :] for ref in (own_ref, other_ref)]
        low, high = jnp.where(core == 0, own, other), jnp.where(core == 0, other, own)
        both = jnp.stack([low, high], axis=1).astype(F32).reshape(N_WIDE, 2, HALF, CH)
        return [both[:, i].reshape(N_WIDE * HALF, CH) for i in range(2)]

    group = lane_group((N_WIDE, CH), 16)
    for n in range(N_NARROW):
        tail_s[n * CH : (n + 1) * CH, :] = rows(n, 16)[1]
    for hh in range(2):
        for kb in range(2):
            got = []
            for n in range(N_NARROW):
                at = n * CH + 2 * hh + kb
                first = tail_s[pl.ds(at, N_WIDE, stride=8), :]
                second = tail_s[pl.ds(at + 4, N_WIDE, stride=8), :]
                got.append(jnp.where(core == 0, first, second))
            for kq in range(HALF):
                acc = got[0]
                acc = turn(acc, -kq * 16)
                for n in range(1, N_NARROW):
                    acc = jnp.where(group == n, turn(got[n], (n - kq) * 16), acc)
                bias_s.at[hh][pl.ds(kb * CH + kq, N_WIDE, stride=HALF), :] = acc

    class Unit:
        pass

    def project(n):
        u = Unit()
        u.n = n
        parts = [part.astype(BF) for part in rows(n, 0)]
        u.x = jnp.concatenate(parts, axis=0)
        u.x_own = jnp.where(side == 0, parts[0], parts[1])
        u.cot = rows(n, 16)[0].astype(BF)
        kv_t = mm(w_kv, u.x, NT).astype(BF)
        qg = mm(w_qg, u.x_own, NT)
        og = mm(out_w, u.cot, NT)
        u.pieces = []
        for hh in range(2):
            h = Unit()
            h.n, h.hh = n, hh
            h.kv = mm(u.x, w_kv[2 * hh * DIM : (2 * hh + 2) * DIM], NT).astype(BF)
            h.q = qg[hh * DIM : (hh + 1) * DIM].astype(BF)
            h.gate = jax.nn.sigmoid(qg[(2 + hh) * DIM : (3 + hh) * DIM])
            h.og = og[hh * DIM : (hh + 1) * DIM]
            h.da = (h.og * h.gate).astype(BF)
            h.k, h.v = [kv_t[(2 * hh + t) * DIM : (2 * hh + t + 1) * DIM] for t in range(2)]
            u.pieces.append(h)
        return u

    def score(h):
        right = jnp.concatenate(
            [jnp.concatenate(pair, axis=1) for pair in ((h.q, zero), (zero, h.da))], axis=0
        )
        both = mm(h.kv, right)
        h.logits, h.d_soft = both[:, :CH], both[:, CH:]

    def softmax(h):
        logits = h.logits * scale + bias_s[h.hh] + mask_ref[...]
        top = jnp.max(logits, axis=0, keepdims=True)
        e = jnp.exp(logits - top)
        h.soft = e * (1.0 / jnp.sum(e, axis=0, keepdims=True))
        h.soft_bf = h.soft.astype(BF)

    def attend(h):
        h.att = mm(h.v, h.soft_bf)
        h.delta = jnp.sum(h.da.astype(F32) * h.att, axis=0, keepdims=True)

    def logit_grads(h):
        h.d_log = (h.soft * (h.d_soft - h.delta)).astype(BF)
        if h.n == 0:
            sum_s[h.hh] = h.d_log.astype(F32)
        else:
            sum_s[h.hh] += h.d_log.astype(F32)

    def gradients(h):
        h.dq = mm(h.k, h.d_log) * scale
        h.dk = mm(h.q, h.d_log, NT) * scale
        h.dv = mm(h.da, h.soft_bf, NT)
        h.dg = h.og * h.att * h.gate * (1.0 - h.gate)
        h.gated = (h.gate * h.att).astype(BF)

    def emit(u):
        one, other = u.pieces
        kv_grads = jnp.concatenate([one.dk, one.dv, other.dk, other.dv], axis=0).astype(BF)
        qg_grads = jnp.concatenate([one.dq, other.dq, one.dg, other.dg], axis=0).astype(BF)
        gated = jnp.concatenate([one.gated, other.gated], axis=0)
        sums = (mm(kv_grads, u.x), mm(qg_grads, u.x_own), mm(gated, u.cot))
        for ref, part in zip((kv_s, qg_s, gout_s), sums):
            if u.n == 0:
                ref[...] = part
            else:
                ref[...] += part
        d_normed = mm(kv_grads, w_kv, TN)
        d_own = mm(qg_grads, w_qg, TN)
        both = [
            (d_normed[i * CH : (i + 1) * CH] + jnp.where(side == i, d_own, 0.0)).reshape(
                N_CHIP, 2, HALF, CH
            )
            for i in range(2)
        ]
        put(jnp.concatenate(both, axis=2).astype(BF), u.n, 0, 16)

    def put(value, n, start, stop):
        even, odd = value[:, 0], value[:, 1]
        keep_ref[:, n, start:stop, :] = jnp.where(core == 0, even, odd)
        give_ref[:, n, start:stop, :] = jnp.where(core == 0, odd, even)

    for first in range(0, N_NARROW, TOGETHER):
        units = [project(n) for n in range(first, first + TOGETHER)]
        flat = [h for u in units for h in u.pieces]
        for step in (score, softmax, attend, logit_grads, gradients):
            for h in flat:
                step(h)
        for u in units:
            emit(u)

    for hh in range(2):
        for kb in range(2):
            got = [
                sum_s.at[hh][pl.ds(kb * CH + kq, N_WIDE, stride=HALF), :] for kq in range(HALF)
            ]
            for n in range(N_NARROW):
                acc = turn(got[0], -n * 16)
                for kq in range(1, HALF):
                    acc = jnp.where(group == kq, turn(got[kq], (kq - n) * 16), acc)
                tail_s[pl.ds(n * 8 + 2 * hh + kb, N_WIDE, stride=64), :] = acc
    tail_s[pl.ds(4, DEVICES, stride=8), :] = jnp.transpose(kv_s[...])
    tail_s[pl.ds(5, DEVICES, stride=8), :] = jnp.transpose(qg_s[...])
    for hh in range(2):
        out_part = gout_s[hh * DIM : (hh + 1) * DIM, :]
        for r in range(4):
            tail_s[pl.ds(6 + hh + 8 * r, DIM, stride=32), :] = out_part
    tail = tail_s[...].astype(BF).reshape(N_CHIP, 2, N_NARROW, 8, CH)
    put(tail, slice(None), 16, 24)


def join_kernel(keep_ref, got_ref, send_ref):
    core = lax.axis_index("core")
    total = keep_ref[:, 0:16, :].astype(F32) + got_ref[:, 0:16, :].astype(F32)
    send_ref[:, 0:16, :] = total.astype(BF)
    keep, got = keep_ref[:, 16:24, :], got_ref[:, 16:24, :]
    send_ref[:, 16:24, :] = jnp.where(core == 0, keep, got)
    send_ref[:, 24:32, :] = jnp.where(core == 0, got, keep)


def reduce_kernel(recv_ref, normed_ref, send_ref, bias_ref):
    sums = [
        [
            jnp.sum(recv_ref[s, :, 16 + 8 * c : 24 + 8 * c, :].astype(F32), axis=0)
            for c in range(2)
        ]
        for s in range(2)
    ]
    blocks = []
    for s in range(2):
        for kb in range(2):
            parts = [sums[s][h // 2][h % 2 * 2 + kb :][:1] for h in range(HEADS)]
            blocks.append(jnp.concatenate(parts, axis=0))
    bias = jnp.concatenate(blocks, axis=1)
    bias = jnp.concatenate([bias, jnp.zeros_like(bias)], axis=0).astype(BF)
    bias_ref[...] = bias
    grad_bias = mm(bias, normed_ref[...])[:HEADS]
    total = [sums[0][c] + sums[1][c] for c in range(2)]
    group = lane_group((1, CH))
    rows = []
    for t in range(4):
        row = jnp.zeros((1, CH), F32)
        for h in range(HEADS):
            own = total[h // 2]
            got, place = {
                0: (own[5:6], h % 2),
                1: (own[4:5], h % 2 * 2),
                2: (own[4:5], h % 2 * 2 + 1),
                3: (own[5:6], 2 + h % 2),
            }[t]
            row = jnp.where(group == h, turn(got, (h - place) * DIM), row)
        rows.append(row)
    place = lax.rem(lax.axis_index("narrow"), 4)
    row = jnp.zeros((1, CH), F32)
    for h in range(HEADS):
        shift = lax.rem(h * DIM + CH - place * DIM, CH)
        got = total[h // 2][6 + h % 2 :][:1]
        row = jnp.where(group == h, pltpu.roll(got, shift, 1), row)
    rows += [row, jnp.zeros((1, CH), F32), grad_bias]
    chunk = jnp.concatenate(rows, axis=0)
    block = jnp.concatenate([chunk] * 8, axis=0).astype(BF)
    for i in range(DEVICES // 8):
        send_ref[i * 80 : (i + 1) * 80, :] = block


def pair_grads(recv_ref, bias_ref, pair_ref, gain_ref, wbt_ref, out_ref, ds):
    total = recv_ref[0, :, 0:16, :].astype(F32) + recv_ref[1, :, 0:16, :].astype(F32)
    ds[...] = total.reshape(TILE, CH)
    d_normed = jnp.concatenate([ds[pl.ds(r, COLS, stride=ROWS), :] for r in range(ROWS)], axis=0)
    wbt = wbt_ref[...].astype(F32)
    wbt = jnp.concatenate([wbt, jnp.zeros_like(wbt)], axis=0).astype(BF)
    split = mm(bias_ref[...], wbt, TN).reshape(2, TILE // (2 * HALF), HALF, CH)
    d_normed = d_normed + jnp.stack([split[0], split[1]], axis=1).reshape(TILE, CH)
    hat, inverse = normal(pair_ref[...].astype(F32).reshape(TILE, CH))
    d_hat = d_normed * gain_ref[...]
    d_pair = inverse * (
        d_hat
        - jnp.mean(d_hat, axis=-1, keepdims=True)
        - hat * jnp.mean(d_hat * hat, axis=-1, keepdims=True)
    )
    out_ref[...] = d_pair.astype(BF).reshape(ROWS, COLS, CH)


def final_kernel(
    recv_ref, mid_ref, bias_ref, pair_ref, pw_ref, wbt_ref, gain_ref,
    out_ref, gp_ref, gb_ref, go_ref, gg_ref, vs, ds,
):
    pair_grads(mid_ref, bias_ref, pair_ref, gain_ref, wbt_ref, out_ref, ds)
    vs[...] = recv_ref[...].astype(F32)
    dots = jnp.zeros((CH, CH), F32)
    for t in range(4):
        got = vs[pl.ds(t, CH, stride=OUT_ROWS), :]
        gp_ref[:, t * CH : (t + 1) * CH] = got
        dots = dots + got * pw_ref[:, t * CH : (t + 1) * CH].astype(F32)
    group = lane_group((DIM, CH))
    quarters = [vs[pl.ds(OUT_ROWS * q + 4, DIM, stride=4 * OUT_ROWS), :] for q in range(4)]
    for h in range(HEADS):
        acc = jnp.zeros((DIM, CH), F32)
        for q in range(4):
            shift = (q - h) * COLS % CH
            got = pltpu.roll(quarters[q], shift, 1) if shift else quarters[q]
            acc = jnp.where(group == q, got, acc)
        go_ref[h * DIM : (h + 1) * DIM, :] = acc
    grad_bias = jnp.concatenate(
        [
            jnp.sum(vs[pl.ds(6 + h, DEVICES, stride=OUT_ROWS), :], axis=0, keepdims=True)
            for h in range(HEADS)
        ],
        axis=0,
    )
    gb_ref[...] = grad_bias
    dots_row = jnp.sum(jnp.transpose(dots), axis=0, keepdims=True)
    bias_row = jnp.sum(grad_bias * wbt_ref[...].astype(F32), axis=0, keepdims=True)
    gg_ref[...] = (dots_row + bias_row) / gain_ref[...]


def call(kernel, out_shape, scratch=(), cost=None, hbm=0):
    many = isinstance(out_shape, (list, tuple))
    spec = pl.BlockSpec(memory_space=pltpu.VMEM)
    outside = pl.BlockSpec(memory_space=pltpu.HBM)

    def run(*args):
        return pl.pallas_call(
            kernel,
            out_shape=out_shape,
            in_specs=[outside] * hbm + [spec] * (len(args) - hbm),
            out_specs=[spec] * len(out_shape) if many else spec,
            scratch_shapes=list(scratch),
            compiler_params=pltpu.CompilerParams(vmem_limit_bytes=32 * 1024 * 1024),
            cost_estimate=cost,
        )(*args)

    return run


def shape(*dims, dtype=BF):
    return jax.ShapeDtypeStruct(dims, dtype)


def exchange(x, axes, tile):
    count, rows, lanes = x.shape
    x = x.reshape(count, rows // tile, tile, lanes)
    return lax.all_to_all(x, axes, 0, 0, tiled=True).reshape(count, rows, lanes)


def swap(x):
    return lax.ppermute(x, "core", [(0, 1), (1, 0)])


def local(pair_rep, cotangent, norm_gain, proj_weight, bias_weight, out_weight, residue_mask):
    gain = norm_gain.reshape(1, CH)
    wbt = bias_weight.T
    wall = proj_weight.reshape(CH, 4, HEADS, DIM).transpose(2, 1, 3, 0).reshape(HEADS, CH, CH)
    masking = (residue_mask.astype(F32) - 1.0) * MASK_FILL
    masking = masking.reshape(N_WIDE, 2, HALF).transpose(1, 0, 2).reshape(LENGTH)
    masking = jnp.broadcast_to(masking[:, None], (LENGTH, CH))
    tile_f32 = pltpu.VMEM((TILE, CH), F32)
    half = DEVICES // 2

    send, normed, pair_here, gain, wbt = call(
        pre_kernel,
        [
            pltpu.VMEM((2, COLS, IN_ROWS, CH), BF),
            pltpu.VMEM((TILE, CH), BF),
            pltpu.VMEM((ROWS, COLS, CH), BF),
            pltpu.VMEM((1, CH), F32),
            pltpu.VMEM((HEADS, CH), BF),
        ],
        [
            pltpu.VMEM((ROWS, COLS, CH), BF),
            tile_f32,
            tile_f32,
            pltpu.SemaphoreType.DMA((2,)),
        ],
        hbm=2,
    )(*[pltpu.with_memory_space_constraint(a, pltpu.HBM) for a in (pair_rep, cotangent)], gain, wbt)
    own = exchange(send.reshape(half, IN_ROWS, CH), CHIPS, 4)
    other = swap(own)
    keep, give = call(
        attention_kernel,
        [pltpu.VMEM((N_CHIP, N_NARROW, MID_ROWS, CH), BF)] * 2,
        [
            pltpu.VMEM((2, LENGTH, CH), F32),
            pltpu.VMEM((2, LENGTH, CH), F32),
            pltpu.VMEM((DEVICES * 8, CH), F32),
            pltpu.VMEM((CH, CH), F32),
            pltpu.VMEM((CH, CH), F32),
            pltpu.VMEM((2 * DIM, CH), F32),
        ],
    )(
        own.reshape(N_CHIP, N_NARROW, IN_ROWS, CH),
        other.reshape(N_CHIP, N_NARROW, IN_ROWS, CH),
        wall,
        out_weight,
        masking,
    )
    got = swap(give)
    mid = call(join_kernel, pltpu.VMEM((half, SUM_ROWS, CH), BF))(
        keep.reshape(half, MID_ROWS, CH), got.reshape(half, MID_ROWS, CH)
    )
    mid = exchange(mid, CHIPS, 8).reshape(2, COLS, SUM_ROWS, CH)
    send, bias = call(reduce_kernel, [pltpu.VMEM((DEVICES * OUT_ROWS, CH), BF), pltpu.VMEM((8, TILE), BF)])(mid, normed)
    last = exchange(send.reshape(DEVICES, OUT_ROWS, CH), BOTH, 2)
    d_pair, grad_proj, grad_bias, grad_out, grad_gain = call(
        final_kernel,
        [
            shape(ROWS, COLS, CH),
            shape(CH, 4 * CH, dtype=F32),
            shape(HEADS, CH, dtype=F32),
            shape(CH, CH, dtype=F32),
            shape(1, CH, dtype=F32),
        ],
        [pltpu.VMEM((DEVICES * OUT_ROWS, CH), F32), tile_f32],
    )(last.reshape(DEVICES * OUT_ROWS, CH), mid, bias, pair_here, proj_weight, wbt, gain)
    return (d_pair, grad_proj, grad_bias.T, grad_out, grad_gain.reshape(CH))


def solution(mesh):
    cores = Mesh(mesh.devices.reshape(N_CHIP, 2, N_NARROW), BOTH)
    tile = P(("chip", "core"), "narrow", None)
    in_specs = (tile, tile, P(), P(), P(), P(), P())
    out_specs = (tile, P(), P(), P(), P())
    return jax.shard_map(local, mesh=cores, in_specs=in_specs, out_specs=out_specs, check_vma=False)
```

```python
import jax
import jax.numpy as jnp
from jax import lax
from jax.experimental import pallas as pl
from jax.experimental.pallas import tpu as pltpu
from jax.sharding import Mesh, PartitionSpec as P

NORM_EPSILON = 1e-05
MASK_FILL = 1000000000.0
BF = jnp.bfloat16
F32 = jnp.float32
CHIPS = ("chip", "narrow")
BOTH = ("chip", "core", "narrow")

ROWS = 16
COLS = 32
TILE = ROWS * COLS
N_WIDE = 16
N_CHIP = 8
N_NARROW = 8
DEVICES = N_WIDE * N_NARROW
LENGTH = 256
CH = 128
HEADS = 4
DIM = 32
HALF = 8
IN_ROWS = 32
TOGETHER = 8
MID_ROWS = 24
SUM_ROWS = 32
OUT_ROWS = 10

NT = (((1,), (1,)), ((), ()))
NN = (((1,), (0,)), ((), ()))
TN = (((0,), (0,)), ((), ()))


def mm(a, b, dims=NN):
    return lax.dot_general(a, b, dims, preferred_element_type=F32)


def normal(x):
    centered = x - jnp.mean(x, axis=-1, keepdims=True)
    inverse = lax.rsqrt(jnp.mean(centered * centered, axis=-1, keepdims=True) + NORM_EPSILON)
    return centered * inverse, inverse


def lane_group(shape, size=DIM):
    return lax.broadcasted_iota(jnp.int32, shape, 1) // size


def turn(x, lanes):
    lanes %= CH
    return pltpu.roll(x, lanes, 1) if lanes else x


def pre_kernel(
    pair_hbm, cot_hbm, gain_hbm, wbt_hbm, send_ref, normed_ref, pair_v, gain_v, wbt_v,
    cot_v, xs, cs, sems,
):
    copies = [
        pltpu.make_async_copy(src, dst, sems.at[i])
        for i, (src, dst) in enumerate(
            ((pair_hbm, pair_v), (gain_hbm, gain_v), (wbt_hbm, wbt_v), (cot_hbm, cot_v))
        )
    ]
    for copy in copies:
        copy.start()
    for copy in copies:
        copy.wait()
    cs[...] = cot_v[...].astype(F32).reshape(TILE, CH)
    hat, _ = normal(pair_v[...].astype(F32).reshape(TILE, CH))
    normed = (hat * gain_v[...]).astype(BF).astype(F32)
    xs[...] = normed
    groups = normed.reshape(TILE // (2 * HALF), 2, HALF, CH)
    halves = [groups[:, s].reshape(TILE // 2, CH) for s in range(2)]
    split = jnp.concatenate(halves, axis=0).astype(BF)
    normed_ref[...] = split
    bias = mm(wbt_v[...], split, NT)
    chunks = [
        jnp.concatenate(
            [
                bias[h : h + 1, (2 * s + kb) * CH : (2 * s + kb + 1) * CH]
                for h in range(HEADS)
                for kb in range(2)
            ],
            axis=0,
        )
        for s in range(2)
    ]
    for col in range(COLS):
        x = xs[pl.ds(col, ROWS, stride=COLS), :].astype(BF)
        c = cs[pl.ds(col, ROWS, stride=COLS), :]
        for s in range(2):
            send_ref[1 - s, COLS - 1 - col, 0:16, :] = x
            rest = jnp.concatenate([c[s * HALF : (s + 1) * HALF], chunks[s]], axis=0)
            send_ref[1 - s, COLS - 1 - col, 16:32, :] = rest.astype(BF)


def attention_kernel(
    own_ref, other_ref, wall_ref, ow_ref, mask_ref, keep_ref, give_ref,
    bias_s, sum_s, tail_s, kv_s, qg_s, gout_s,
):
    core = lax.axis_index("core")
    side = lax.axis_index("chip") // 4
    scale = DIM**-0.5
    two = [wall_ref[2 * core + hh] for hh in range(2)]
    w_kv = jnp.concatenate([w[DIM : 3 * DIM] for w in two], axis=0)
    w_qg = jnp.concatenate([w[:DIM] for w in two] + [w[3 * DIM :] for w in two], axis=0)
    out_w = ow_ref[pl.ds(pl.multiple_of(core * 2 * DIM, 2 * DIM), 2 * DIM), :]
    zero = jnp.zeros((DIM, CH), BF)

    def rows(n, start):
        place = N_NARROW - 1 - n
        own, other = [
            jnp.stack([ref[m, place, start : start + ROWS, :] for m in reversed(range(N_CHIP))])
            for ref in (own_ref, other_ref)
        ]
        low, high = jnp.where(core == 0, own, other), jnp.where(core == 0, other, own)
        both = jnp.stack([low, high], axis=1).astype(F32).reshape(N_WIDE, 2, HALF, CH)
        return [both[:, i].reshape(N_WIDE * HALF, CH) for i in range(2)]

    group = lane_group((N_WIDE, CH), 16)
    for n in range(N_NARROW):
        tail_s[n * CH : (n + 1) * CH, :] = rows(n, 16)[1]
    for hh in range(2):
        for kb in range(2):
            got = []
            for n in range(N_NARROW):
                at = n * CH + 2 * hh + kb
                first = tail_s[pl.ds(at, N_WIDE, stride=8), :]
                second = tail_s[pl.ds(at + 4, N_WIDE, stride=8), :]
                got.append(jnp.where(core == 0, first, second))
            for kq in range(HALF):
                acc = got[0]
                acc = turn(acc, -kq * 16)
                for n in range(1, N_NARROW):
                    acc = jnp.where(group == n, turn(got[n], (n - kq) * 16), acc)
                bias_s.at[hh][pl.ds(kb * CH + kq, N_WIDE, stride=HALF), :] = acc

    class Unit:
        pass

    def project(n):
        u = Unit()
        u.n = n
        parts = [part.astype(BF) for part in rows(n, 0)]
        u.x = jnp.concatenate(parts, axis=0)
        u.x_own = jnp.where(side == 0, parts[0], parts[1])
        u.cot = rows(n, 16)[0].astype(BF)
        kv_t = mm(w_kv, u.x, NT).astype(BF)
        qg = mm(w_qg, u.x_own, NT)
        og = mm(out_w, u.cot, NT)
        u.pieces = []
        for hh in range(2):
            h = Unit()
            h.n, h.hh = n, hh
            h.kv = mm(u.x, w_kv[2 * hh * DIM : (2 * hh + 2) * DIM], NT).astype(BF)
            h.q = qg[hh * DIM : (hh + 1) * DIM].astype(BF)
            h.gate = jax.nn.sigmoid(qg[(2 + hh) * DIM : (3 + hh) * DIM])
            h.og = og[hh * DIM : (hh + 1) * DIM]
            h.da = (h.og * h.gate).astype(BF)
            h.k, h.v = [kv_t[(2 * hh + t) * DIM : (2 * hh + t + 1) * DIM] for t in range(2)]
            u.pieces.append(h)
        return u

    def score(h):
        right = jnp.concatenate(
            [jnp.concatenate(pair, axis=1) for pair in ((h.q, zero), (zero, h.da))], axis=0
        )
        both = mm(h.kv, right)
        h.logits, h.d_soft = both[:, :CH], both[:, CH:]

    def softmax(h):
        logits = h.logits * scale + bias_s[h.hh] + mask_ref[...]
        top = jnp.max(logits, axis=0, keepdims=True)
        e = jnp.exp(logits - top)
        h.soft = e * (1.0 / jnp.sum(e, axis=0, keepdims=True))
        h.soft_bf = h.soft.astype(BF)

    def attend(h):
        h.att = mm(h.v, h.soft_bf)
        h.delta = jnp.sum(h.da.astype(F32) * h.att, axis=0, keepdims=True)

    def logit_grads(h):
        h.d_log = (h.soft * (h.d_soft - h.delta)).astype(BF)
        if h.n == 0:
            sum_s[h.hh] = h.d_log.astype(F32)
        else:
            sum_s[h.hh] += h.d_log.astype(F32)

    def gradients(h):
        h.dq = mm(h.k, h.d_log) * scale
        h.dk = mm(h.q, h.d_log, NT) * scale
        h.dv = mm(h.da, h.soft_bf, NT)
        h.dg = h.og * h.att * h.gate * (1.0 - h.gate)
        h.gated = (h.gate * h.att).astype(BF)

    def emit(u):
        one, other = u.pieces
        kv_grads = jnp.concatenate([one.dk, one.dv, other.dk, other.dv], axis=0).astype(BF)
        qg_grads = jnp.concatenate([one.dq, other.dq, one.dg, other.dg], axis=0).astype(BF)
        gated = jnp.concatenate([one.gated, other.gated], axis=0)
        sums = (mm(kv_grads, u.x), mm(qg_grads, u.x_own), mm(gated, u.cot))
        for ref, part in zip((kv_s, qg_s, gout_s), sums):
            if u.n == 0:
                ref[...] = part
            else:
                ref[...] += part
        d_normed = mm(kv_grads, w_kv, TN)
        d_own = mm(qg_grads, w_qg, TN)
        both = [
            (d_normed[i * CH : (i + 1) * CH] + jnp.where(side == i, d_own, 0.0)).reshape(
                N_CHIP, 2, HALF, CH
            )
            for i in range(2)
        ]
        put(jnp.concatenate(both, axis=2).astype(BF), u.n, 0, 16)

    def put(value, n, start, stop):
        even, odd = value[:, 0], value[:, 1]
        keep_ref[:, n, start:stop, :] = jnp.where(core == 0, even, odd)
        give_ref[:, n, start:stop, :] = jnp.where(core == 0, odd, even)

    for first in range(0, N_NARROW, TOGETHER):
        units = [project(n) for n in range(first, first + TOGETHER)]
        flat = [h for u in units for h in u.pieces]
        for step in (score, softmax, attend, logit_grads, gradients):
            for h in flat:
                step(h)
        for u in units:
            emit(u)

    for hh in range(2):
        for kb in range(2):
            got = [
                sum_s.at[hh][pl.ds(kb * CH + kq, N_WIDE, stride=HALF), :] for kq in range(HALF)
            ]
            for n in range(N_NARROW):
                acc = turn(got[0], -n * 16)
                for kq in range(1, HALF):
                    acc = jnp.where(group == kq, turn(got[kq], (kq - n) * 16), acc)
                tail_s[pl.ds(n * 8 + 2 * hh + kb, N_WIDE, stride=64), :] = acc
    tail_s[pl.ds(4, DEVICES, stride=8), :] = jnp.transpose(kv_s[...])
    tail_s[pl.ds(5, DEVICES, stride=8), :] = jnp.transpose(qg_s[...])
    for hh in range(2):
        out_part = gout_s[hh * DIM : (hh + 1) * DIM, :]
        for r in range(4):
            tail_s[pl.ds(6 + hh + 8 * r, DIM, stride=32), :] = out_part
    tail = tail_s[...].astype(BF).reshape(N_CHIP, 2, N_NARROW, 8, CH)
    put(tail, slice(None), 16, 24)


def join_kernel(keep_ref, got_ref, send_ref):
    core = lax.axis_index("core")
    total = keep_ref[:, 0:16, :].astype(F32) + got_ref[:, 0:16, :].astype(F32)
    send_ref[:, 0:16, :] = total.astype(BF)
    keep, got = keep_ref[:, 16:24, :], got_ref[:, 16:24, :]
    send_ref[:, 16:24, :] = jnp.where(core == 0, keep, got)
    send_ref[:, 24:32, :] = jnp.where(core == 0, got, keep)


def reduce_kernel(recv_ref, normed_ref, send_ref, bias_ref):
    sums = [
        [
            jnp.sum(recv_ref[s, :, 16 + 8 * c : 24 + 8 * c, :].astype(F32), axis=0)
            for c in range(2)
        ]
        for s in range(2)
    ]
    blocks = []
    for s in range(2):
        for kb in range(2):
            parts = [sums[s][h // 2][h % 2 * 2 + kb :][:1] for h in range(HEADS)]
            blocks.append(jnp.concatenate(parts, axis=0))
    bias = jnp.concatenate(blocks, axis=1)
    bias = jnp.concatenate([bias, jnp.zeros_like(bias)], axis=0).astype(BF)
    bias_ref[...] = bias
    grad_bias = mm(bias, normed_ref[...])[:HEADS]
    total = [sums[0][c] + sums[1][c] for c in range(2)]
    group = lane_group((1, CH))
    rows = []
    for t in range(4):
        row = jnp.zeros((1, CH), F32)
        for h in range(HEADS):
            own = total[h // 2]
            got, place = {
                0: (own[5:6], h % 2),
                1: (own[4:5], h % 2 * 2),
                2: (own[4:5], h % 2 * 2 + 1),
                3: (own[5:6], 2 + h % 2),
            }[t]
            row = jnp.where(group == h, turn(got, (h - place) * DIM), row)
        rows.append(row)
    place = lax.rem(lax.axis_index("narrow"), 4)
    row = jnp.zeros((1, CH), F32)
    for h in range(HEADS):
        shift = lax.rem(h * DIM + CH - place * DIM, CH)
        got = total[h // 2][6 + h % 2 :][:1]
        row = jnp.where(group == h, pltpu.roll(got, shift, 1), row)
    rows += [row, jnp.zeros((1, CH), F32), grad_bias]
    chunk = jnp.concatenate(rows, axis=0)
    block = jnp.concatenate([chunk] * 8, axis=0).astype(BF)
    for i in range(DEVICES // 8):
        send_ref[i * 80 : (i + 1) * 80, :] = block


def pair_grads(recv_ref, bias_ref, pair_ref, gain_ref, wbt_ref, out_ref, ds):
    total = recv_ref[0, :, 0:16, :].astype(F32) + recv_ref[1, :, 0:16, :].astype(F32)
    ds[...] = total.reshape(TILE, CH)
    d_normed = jnp.concatenate([ds[pl.ds(r, COLS, stride=ROWS), :] for r in range(ROWS)], axis=0)
    wbt = wbt_ref[...].astype(F32)
    wbt = jnp.concatenate([wbt, jnp.zeros_like(wbt)], axis=0).astype(BF)
    split = mm(bias_ref[...], wbt, TN).reshape(2, TILE // (2 * HALF), HALF, CH)
    d_normed = d_normed + jnp.stack([split[0], split[1]], axis=1).reshape(TILE, CH)
    hat, inverse = normal(pair_ref[...].astype(F32).reshape(TILE, CH))
    d_hat = d_normed * gain_ref[...]
    d_pair = inverse * (
        d_hat
        - jnp.mean(d_hat, axis=-1, keepdims=True)
        - hat * jnp.mean(d_hat * hat, axis=-1, keepdims=True)
    )
    out_ref[...] = d_pair.astype(BF).reshape(ROWS, COLS, CH)


def final_kernel(
    recv_ref, mid_ref, bias_ref, pair_ref, pw_ref, wbt_ref, gain_ref,
    out_ref, gp_ref, gb_ref, go_ref, gg_ref, vs, ds,
):
    pair_grads(mid_ref, bias_ref, pair_ref, gain_ref, wbt_ref, out_ref, ds)
    vs[...] = recv_ref[...].astype(F32)
    dots = jnp.zeros((CH, CH), F32)
    for t in range(4):
        got = vs[pl.ds(t, CH, stride=OUT_ROWS), :]
        gp_ref[:, t * CH : (t + 1) * CH] = got
        dots = dots + got * pw_ref[:, t * CH : (t + 1) * CH].astype(F32)
    group = lane_group((DIM, CH))
    quarters = [vs[pl.ds(OUT_ROWS * q + 4, DIM, stride=4 * OUT_ROWS), :] for q in range(4)]
    for h in range(HEADS):
        acc = jnp.zeros((DIM, CH), F32)
        for q in range(4):
            shift = (q - h) * COLS % CH
            got = pltpu.roll(quarters[q], shift, 1) if shift else quarters[q]
            acc = jnp.where(group == q, got, acc)
        go_ref[h * DIM : (h + 1) * DIM, :] = acc
    grad_bias = jnp.concatenate(
        [
            jnp.sum(vs[pl.ds(6 + h, DEVICES, stride=OUT_ROWS), :], axis=0, keepdims=True)
            for h in range(HEADS)
        ],
        axis=0,
    )
    gb_ref[...] = grad_bias
    dots_row = jnp.sum(jnp.transpose(dots), axis=0, keepdims=True)
    bias_row = jnp.sum(grad_bias * wbt_ref[...].astype(F32), axis=0, keepdims=True)
    gg_ref[...] = (dots_row + bias_row) / gain_ref[...]


def call(kernel, out_shape, scratch=(), cost=None, hbm=False):
    many = isinstance(out_shape, (list, tuple))
    spec = pl.BlockSpec(memory_space=pltpu.VMEM)
    in_spec = pl.BlockSpec(memory_space=pltpu.HBM) if hbm else spec

    def run(*args):
        return pl.pallas_call(
            kernel,
            out_shape=out_shape,
            in_specs=[in_spec] * len(args),
            out_specs=[spec] * len(out_shape) if many else spec,
            scratch_shapes=list(scratch),
            compiler_params=pltpu.CompilerParams(vmem_limit_bytes=32 * 1024 * 1024),
            cost_estimate=cost,
        )(*args)

    return run


def shape(*dims, dtype=BF):
    return jax.ShapeDtypeStruct(dims, dtype)


def exchange(x, axes, tile):
    count, rows, lanes = x.shape
    x = x.reshape(count, rows // tile, tile, lanes)
    return lax.all_to_all(x, axes, 0, 0, tiled=True).reshape(count, rows, lanes)


def swap(x):
    return lax.ppermute(x, "core", [(0, 1), (1, 0)])


def local(pair_rep, cotangent, norm_gain, proj_weight, bias_weight, out_weight, residue_mask):
    gain = norm_gain.reshape(1, CH)
    wbt = bias_weight.T
    wall = proj_weight.reshape(CH, 4, HEADS, DIM).transpose(2, 1, 3, 0).reshape(HEADS, CH, CH)
    masking = (residue_mask.astype(F32) - 1.0) * MASK_FILL
    masking = masking.reshape(N_WIDE, 2, HALF).transpose(1, 0, 2).reshape(LENGTH)
    masking = jnp.broadcast_to(masking[:, None], (LENGTH, CH))
    tile_f32 = pltpu.VMEM((TILE, CH), F32)
    half = DEVICES // 2

    send, normed, pair_here, gain, wbt = call(
        pre_kernel,
        [
            pltpu.VMEM((2, COLS, IN_ROWS, CH), BF),
            pltpu.VMEM((TILE, CH), BF),
            pltpu.VMEM((ROWS, COLS, CH), BF),
            pltpu.VMEM((1, CH), F32),
            pltpu.VMEM((HEADS, CH), BF),
        ],
        [
            pltpu.VMEM((ROWS, COLS, CH), BF),
            tile_f32,
            tile_f32,
            pltpu.SemaphoreType.DMA((4,)),
        ],
        hbm=True,
    )(*[pltpu.with_memory_space_constraint(a, pltpu.HBM) for a in (pair_rep, cotangent, gain, wbt)])
    own = lax.all_to_all(
        send.reshape(half, IN_ROWS // 4, 4, CH),
        BOTH,
        0,
        0,
        tiled=True,
        axis_index_groups=[
            [
                m * 2 * N_NARROW + core * N_NARROW + n
                for m in reversed(range(N_CHIP))
                for n in reversed(range(N_NARROW))
            ]
            for core in range(2)
        ],
    ).reshape(half, IN_ROWS, CH)
    other = swap(own)
    keep, give = call(
        attention_kernel,
        [pltpu.VMEM((N_CHIP, N_NARROW, MID_ROWS, CH), BF)] * 2,
        [
            pltpu.VMEM((2, LENGTH, CH), F32),
            pltpu.VMEM((2, LENGTH, CH), F32),
            pltpu.VMEM((DEVICES * 8, CH), F32),
            pltpu.VMEM((CH, CH), F32),
            pltpu.VMEM((CH, CH), F32),
            pltpu.VMEM((2 * DIM, CH), F32),
        ],
    )(
        own.reshape(N_CHIP, N_NARROW, IN_ROWS, CH),
        other.reshape(N_CHIP, N_NARROW, IN_ROWS, CH),
        wall,
        out_weight,
        masking,
    )
    got = swap(give)
    mid = call(join_kernel, pltpu.VMEM((half, SUM_ROWS, CH), BF))(
        keep.reshape(half, MID_ROWS, CH), got.reshape(half, MID_ROWS, CH)
    )
    mid = exchange(mid, CHIPS, 8).reshape(2, COLS, SUM_ROWS, CH)
    send, bias = call(reduce_kernel, [pltpu.VMEM((DEVICES * OUT_ROWS, CH), BF), pltpu.VMEM((8, TILE), BF)])(mid, normed)
    last = exchange(send.reshape(DEVICES, OUT_ROWS, CH), BOTH, 2)
    d_pair, grad_proj, grad_bias, grad_out, grad_gain = call(
        final_kernel,
        [
            shape(ROWS, COLS, CH),
            shape(CH, 4 * CH, dtype=F32),
            shape(HEADS, CH, dtype=F32),
            shape(CH, CH, dtype=F32),
            shape(1, CH, dtype=F32),
        ],
        [pltpu.VMEM((DEVICES * OUT_ROWS, CH), F32), tile_f32],
    )(last.reshape(DEVICES * OUT_ROWS, CH), mid, bias, pair_here, proj_weight, wbt, gain)
    return (d_pair, grad_proj, grad_bias.T, grad_out, grad_gain.reshape(CH))


def solution(mesh):
    cores = Mesh(mesh.devices.reshape(N_CHIP, 2, N_NARROW), BOTH)
    tile = P(("chip", "core"), "narrow", None)
    in_specs = (tile, tile, P(), P(), P(), P(), P())
    out_specs = (tile, P(), P(), P(), P())
    return jax.shard_map(local, mesh=cores, in_specs=in_specs, out_specs=out_specs, check_vma=False)
```

```python
import jax
import jax.numpy as jnp
from jax import lax
from jax.experimental import pallas as pl
from jax.experimental.pallas import tpu as pltpu
from jax.sharding import Mesh, PartitionSpec as P

NORM_EPSILON = 1e-05
MASK_FILL = 1000000000.0
BF = jnp.bfloat16
F32 = jnp.float32
BOTH = ("chip", "core", "narrow")

ROWS = 16
COLS = 32
TILE = ROWS * COLS
N_WIDE = 16
N_CHIP = 8
N_NARROW = 8
DEVICES = N_WIDE * N_NARROW
LENGTH = 256
CH = 128
HEADS = 4
DIM = 32
HALF = 8
IN_ROWS = 32
TOGETHER = 8
MID_ROWS = 24
SUM_ROWS = 32
OUT_ROWS = 10

NT = (((1,), (1,)), ((), ()))
NN = (((1,), (0,)), ((), ()))
TN = (((0,), (0,)), ((), ()))


def mm(a, b, dims=NN):
    return lax.dot_general(a, b, dims, preferred_element_type=F32)


def normal(x):
    centered = x - jnp.mean(x, axis=-1, keepdims=True)
    inverse = lax.rsqrt(jnp.mean(centered * centered, axis=-1, keepdims=True) + NORM_EPSILON)
    return centered * inverse, inverse


def lane_group(shape, size=DIM):
    return lax.broadcasted_iota(jnp.int32, shape, 1) // size


def turn(x, lanes):
    lanes %= CH
    return pltpu.roll(x, lanes, 1) if lanes else x


def pre_kernel(
    pair_hbm, cot_hbm, gain_hbm, wbt_hbm, send_ref, normed_ref, pair_v, gain_v, wbt_v,
    cot_v, xs, cs, sems,
):
    copies = [
        pltpu.make_async_copy(src, dst, sems.at[i])
        for i, (src, dst) in enumerate(
            ((pair_hbm, pair_v), (gain_hbm, gain_v), (wbt_hbm, wbt_v), (cot_hbm, cot_v))
        )
    ]
    for copy in copies:
        copy.start()
    for copy in copies:
        copy.wait()
    cs[...] = cot_v[...].astype(F32).reshape(TILE, CH)
    hat, _ = normal(pair_v[...].astype(F32).reshape(TILE, CH))
    normed = (hat * gain_v[...]).astype(BF).astype(F32)
    xs[...] = normed
    groups = normed.reshape(TILE // (2 * HALF), 2, HALF, CH)
    halves = [groups[:, s].reshape(TILE // 2, CH) for s in range(2)]
    split = jnp.concatenate(halves, axis=0).astype(BF)
    normed_ref[...] = split
    bias = mm(wbt_v[...], split, NT)
    chunks = [
        jnp.concatenate(
            [
                bias[h : h + 1, (2 * s + kb) * CH : (2 * s + kb + 1) * CH]
                for h in range(HEADS)
                for kb in range(2)
            ],
            axis=0,
        )
        for s in range(2)
    ]
    for col in range(COLS):
        x = xs[pl.ds(col, ROWS, stride=COLS), :].astype(BF)
        c = cs[pl.ds(col, ROWS, stride=COLS), :]
        for s in range(2):
            send_ref[1 - s, COLS - 1 - col, 0:16, :] = x
            rest = jnp.concatenate([c[s * HALF : (s + 1) * HALF], chunks[s]], axis=0)
            send_ref[1 - s, COLS - 1 - col, 16:32, :] = rest.astype(BF)


def attention_kernel(
    own_ref, other_ref, wall_ref, ow_ref, mask_ref, keep_ref, give_ref,
    bias_s, sum_s, tail_s, kv_s, qg_s, gout_s,
):
    core = lax.axis_index("core")
    side = lax.axis_index("chip") // 4
    scale = DIM**-0.5
    two = [wall_ref[2 * core + hh] for hh in range(2)]
    w_kv = jnp.concatenate([w[DIM : 3 * DIM] for w in two], axis=0)
    w_qg = jnp.concatenate([w[:DIM] for w in two] + [w[3 * DIM :] for w in two], axis=0)
    out_w = ow_ref[pl.ds(pl.multiple_of(core * 2 * DIM, 2 * DIM), 2 * DIM), :]
    zero = jnp.zeros((DIM, CH), BF)

    def rows(n, start):
        place = N_NARROW - 1 - n
        own, other = [
            jnp.stack([ref[m, place, start : start + ROWS, :] for m in reversed(range(N_CHIP))])
            for ref in (own_ref, other_ref)
        ]
        low, high = jnp.where(core == 0, own, other), jnp.where(core == 0, other, own)
        both = jnp.stack([low, high], axis=1).astype(F32).reshape(N_WIDE, 2, HALF, CH)
        return [both[:, i].reshape(N_WIDE * HALF, CH) for i in range(2)]

    group = lane_group((N_WIDE, CH), 16)
    for n in range(N_NARROW):
        tail_s[n * CH : (n + 1) * CH, :] = rows(n, 16)[1]
    for hh in range(2):
        for kb in range(2):
            got = []
            for n in range(N_NARROW):
                at = n * CH + 2 * hh + kb
                first = tail_s[pl.ds(at, N_WIDE, stride=8), :]
                second = tail_s[pl.ds(at + 4, N_WIDE, stride=8), :]
                got.append(jnp.where(core == 0, first, second))
            for kq in range(HALF):
                acc = got[0]
                acc = turn(acc, -kq * 16)
                for n in range(1, N_NARROW):
                    acc = jnp.where(group == n, turn(got[n], (n - kq) * 16), acc)
                bias_s.at[hh][pl.ds(kb * CH + kq, N_WIDE, stride=HALF), :] = acc

    class Unit:
        pass

    def project(n):
        u = Unit()
        u.n = n
        parts = [part.astype(BF) for part in rows(n, 0)]
        u.x = jnp.concatenate(parts, axis=0)
        u.x_own = jnp.where(side == 0, parts[0], parts[1])
        u.cot = rows(n, 16)[0].astype(BF)
        kv_t = mm(w_kv, u.x, NT).astype(BF)
        qg = mm(w_qg, u.x_own, NT)
        og = mm(out_w, u.cot, NT)
        u.pieces = []
        for hh in range(2):
            h = Unit()
            h.n, h.hh = n, hh
            h.kv = mm(u.x, w_kv[2 * hh * DIM : (2 * hh + 2) * DIM], NT).astype(BF)
            h.q = qg[hh * DIM : (hh + 1) * DIM].astype(BF)
            h.gate = jax.nn.sigmoid(qg[(2 + hh) * DIM : (3 + hh) * DIM])
            h.og = og[hh * DIM : (hh + 1) * DIM]
            h.da = (h.og * h.gate).astype(BF)
            h.k, h.v = [kv_t[(2 * hh + t) * DIM : (2 * hh + t + 1) * DIM] for t in range(2)]
            u.pieces.append(h)
        return u

    def score(h):
        right = jnp.concatenate(
            [jnp.concatenate(pair, axis=1) for pair in ((h.q, zero), (zero, h.da))], axis=0
        )
        both = mm(h.kv, right)
        h.logits, h.d_soft = both[:, :CH], both[:, CH:]

    def softmax(h):
        logits = h.logits * scale + bias_s[h.hh] + mask_ref[...]
        top = jnp.max(logits, axis=0, keepdims=True)
        e = jnp.exp(logits - top)
        h.soft = e * (1.0 / jnp.sum(e, axis=0, keepdims=True))
        h.soft_bf = h.soft.astype(BF)

    def attend(h):
        h.att = mm(h.v, h.soft_bf)
        h.delta = jnp.sum(h.da.astype(F32) * h.att, axis=0, keepdims=True)

    def logit_grads(h):
        h.d_log = (h.soft * (h.d_soft - h.delta)).astype(BF)
        if h.n == 0:
            sum_s[h.hh] = h.d_log.astype(F32)
        else:
            sum_s[h.hh] += h.d_log.astype(F32)

    def gradients(h):
        h.dq = mm(h.k, h.d_log) * scale
        h.dk = mm(h.q, h.d_log, NT) * scale
        h.dv = mm(h.da, h.soft_bf, NT)
        h.dg = h.og * h.att * h.gate * (1.0 - h.gate)
        h.gated = (h.gate * h.att).astype(BF)

    def emit(u):
        one, other = u.pieces
        kv_grads = jnp.concatenate([one.dk, one.dv, other.dk, other.dv], axis=0).astype(BF)
        qg_grads = jnp.concatenate([one.dq, other.dq, one.dg, other.dg], axis=0).astype(BF)
        gated = jnp.concatenate([one.gated, other.gated], axis=0)
        sums = (mm(kv_grads, u.x), mm(qg_grads, u.x_own), mm(gated, u.cot))
        for ref, part in zip((kv_s, qg_s, gout_s), sums):
            if u.n == 0:
                ref[...] = part
            else:
                ref[...] += part
        d_normed = mm(kv_grads, w_kv, TN)
        d_own = mm(qg_grads, w_qg, TN)
        both = [
            (d_normed[i * CH : (i + 1) * CH] + jnp.where(side == i, d_own, 0.0)).reshape(
                N_CHIP, 2, HALF, CH
            )
            for i in range(2)
        ]
        put(jnp.concatenate(both, axis=2).astype(BF), u.n, 0, 16)

    def put(value, n, start, stop):
        even, odd = value[:, 0], value[:, 1]
        keep_ref[:, n, start:stop, :] = jnp.where(core == 0, even, odd)
        give_ref[:, n, start:stop, :] = jnp.where(core == 0, odd, even)

    for first in range(0, N_NARROW, TOGETHER):
        units = [project(n) for n in range(first, first + TOGETHER)]
        flat = [h for u in units for h in u.pieces]
        for step in (score, softmax, attend, logit_grads, gradients):
            for h in flat:
                step(h)
        for u in units:
            emit(u)

    for hh in range(2):
        for kb in range(2):
            got = [
                sum_s.at[hh][pl.ds(kb * CH + kq, N_WIDE, stride=HALF), :] for kq in range(HALF)
            ]
            for n in range(N_NARROW):
                acc = turn(got[0], -n * 16)
                for kq in range(1, HALF):
                    acc = jnp.where(group == kq, turn(got[kq], (kq - n) * 16), acc)
                tail_s[pl.ds(n * 8 + 2 * hh + kb, N_WIDE, stride=64), :] = acc
    tail_s[pl.ds(4, DEVICES, stride=8), :] = jnp.transpose(kv_s[...])
    tail_s[pl.ds(5, DEVICES, stride=8), :] = jnp.transpose(qg_s[...])
    for hh in range(2):
        out_part = gout_s[hh * DIM : (hh + 1) * DIM, :]
        for r in range(4):
            tail_s[pl.ds(6 + hh + 8 * r, DIM, stride=32), :] = out_part
    tail = tail_s[...].astype(BF).reshape(N_CHIP, 2, N_NARROW, 8, CH)
    put(tail, slice(None), 16, 24)


def reverse(x):
    return jnp.stack([x[i] for i in reversed(range(x.shape[0]))])


def join_kernel(keep_ref, got_ref, send_ref):
    core = lax.axis_index("core")
    total = keep_ref[:, 0:16, :].astype(F32) + got_ref[:, 0:16, :].astype(F32)
    send_ref[:, 0:16, :] = reverse(total.astype(BF))
    tails = [ref[:, 16:24, :].astype(F32) for ref in (keep_ref, got_ref)]
    first = lax.broadcasted_iota(jnp.int32, tails[0].shape, 1) < 4
    keep, got = [jnp.where(first, reverse(t), t).astype(BF) for t in tails]
    send_ref[:, 16:24, :] = jnp.where(core == 0, keep, got)
    send_ref[:, 24:32, :] = jnp.where(core == 0, got, keep)


def reduce_kernel(recv_ref, normed_ref, send_ref, bias_ref):
    sums = [
        [
            jnp.sum(recv_ref[1 - s, :, 16 + 8 * c : 24 + 8 * c, :].astype(F32), axis=0)
            for c in range(2)
        ]
        for s in range(2)
    ]
    blocks = []
    for s in range(2):
        for kb in range(2):
            parts = [sums[s][h // 2][h % 2 * 2 + kb :][:1] for h in range(HEADS)]
            blocks.append(jnp.concatenate(parts, axis=0))
    bias = jnp.concatenate(blocks, axis=1)
    bias = jnp.concatenate([bias, jnp.zeros_like(bias)], axis=0).astype(BF)
    bias_ref[...] = bias
    grad_bias = mm(bias, normed_ref[...])[:HEADS]
    total = [sums[0][c] + sums[1][c] for c in range(2)]
    group = lane_group((1, CH))
    rows = []
    for t in range(4):
        row = jnp.zeros((1, CH), F32)
        for h in range(HEADS):
            own = total[h // 2]
            got, place = {
                0: (own[5:6], h % 2),
                1: (own[4:5], h % 2 * 2),
                2: (own[4:5], h % 2 * 2 + 1),
                3: (own[5:6], 2 + h % 2),
            }[t]
            row = jnp.where(group == h, turn(got, (h - place) * DIM), row)
        rows.append(row)
    place = lax.rem(N_NARROW - 1 - lax.axis_index("narrow"), 4)
    row = jnp.zeros((1, CH), F32)
    for h in range(HEADS):
        shift = lax.rem(h * DIM + CH - place * DIM, CH)
        got = total[h // 2][6 + h % 2 :][:1]
        row = jnp.where(group == h, pltpu.roll(got, shift, 1), row)
    rows += [row, jnp.zeros((1, CH), F32), grad_bias]
    chunk = jnp.concatenate(rows, axis=0)
    block = jnp.concatenate([chunk] * 8, axis=0).astype(BF)
    for i in range(DEVICES // 8):
        send_ref[i * 80 : (i + 1) * 80, :] = block


def pair_grads(recv_ref, bias_ref, pair_ref, gain_ref, wbt_ref, out_ref, ds):
    total = recv_ref[0, :, 0:16, :].astype(F32) + recv_ref[1, :, 0:16, :].astype(F32)
    ds[...] = reverse(total).reshape(TILE, CH)
    d_normed = jnp.concatenate([ds[pl.ds(r, COLS, stride=ROWS), :] for r in range(ROWS)], axis=0)
    wbt = wbt_ref[...].astype(F32)
    wbt = jnp.concatenate([wbt, jnp.zeros_like(wbt)], axis=0).astype(BF)
    split = mm(bias_ref[...], wbt, TN).reshape(2, TILE // (2 * HALF), HALF, CH)
    d_normed = d_normed + jnp.stack([split[0], split[1]], axis=1).reshape(TILE, CH)
    hat, inverse = normal(pair_ref[...].astype(F32).reshape(TILE, CH))
    d_hat = d_normed * gain_ref[...]
    d_pair = inverse * (
        d_hat
        - jnp.mean(d_hat, axis=-1, keepdims=True)
        - hat * jnp.mean(d_hat * hat, axis=-1, keepdims=True)
    )
    out_ref[...] = d_pair.astype(BF).reshape(ROWS, COLS, CH)


def final_kernel(
    recv_ref, mid_ref, bias_ref, pair_ref, pw_ref, wbt_ref, gain_ref,
    out_ref, gp_ref, gb_ref, go_ref, gg_ref, vs, ds,
):
    pair_grads(mid_ref, bias_ref, pair_ref, gain_ref, wbt_ref, out_ref, ds)
    vs[...] = recv_ref[...].astype(F32)
    dots = jnp.zeros((CH, CH), F32)
    for t in range(4):
        got = vs[pl.ds(t, CH, stride=OUT_ROWS), :]
        gp_ref[:, t * CH : (t + 1) * CH] = got
        dots = dots + got * pw_ref[:, t * CH : (t + 1) * CH].astype(F32)
    group = lane_group((DIM, CH))
    quarters = [vs[pl.ds(OUT_ROWS * q + 4, DIM, stride=4 * OUT_ROWS), :] for q in range(4)]
    for h in range(HEADS):
        acc = jnp.zeros((DIM, CH), F32)
        for q in range(4):
            shift = (q - h) * COLS % CH
            got = pltpu.roll(quarters[q], shift, 1) if shift else quarters[q]
            acc = jnp.where(group == q, got, acc)
        go_ref[h * DIM : (h + 1) * DIM, :] = acc
    grad_bias = jnp.concatenate(
        [
            jnp.sum(vs[pl.ds(6 + h, DEVICES, stride=OUT_ROWS), :], axis=0, keepdims=True)
            for h in range(HEADS)
        ],
        axis=0,
    )
    gb_ref[...] = grad_bias
    dots_row = jnp.sum(jnp.transpose(dots), axis=0, keepdims=True)
    bias_row = jnp.sum(grad_bias * wbt_ref[...].astype(F32), axis=0, keepdims=True)
    gg_ref[...] = (dots_row + bias_row) / gain_ref[...]


def call(kernel, out_shape, scratch=(), cost=None, hbm=False):
    many = isinstance(out_shape, (list, tuple))
    spec = pl.BlockSpec(memory_space=pltpu.VMEM)
    in_spec = pl.BlockSpec(memory_space=pltpu.HBM) if hbm else spec

    def run(*args):
        return pl.pallas_call(
            kernel,
            out_shape=out_shape,
            in_specs=[in_spec] * len(args),
            out_specs=[spec] * len(out_shape) if many else spec,
            scratch_shapes=list(scratch),
            compiler_params=pltpu.CompilerParams(vmem_limit_bytes=32 * 1024 * 1024),
            cost_estimate=cost,
        )(*args)

    return run


def shape(*dims, dtype=BF):
    return jax.ShapeDtypeStruct(dims, dtype)


def backward(x, tile, cores=((0,), (1,))):
    count, rows, lanes = x.shape
    groups = [
        [
            (m * 2 + core) * N_NARROW + n
            for m in reversed(range(N_CHIP))
            for core in group
            for n in reversed(range(N_NARROW))
        ]
        for group in cores
    ]
    x = x.reshape(count, rows // tile, tile, lanes)
    x = lax.all_to_all(x, BOTH, 0, 0, tiled=True, axis_index_groups=groups)
    return x.reshape(count, rows, lanes)


def swap(x):
    return lax.ppermute(x, "core", [(0, 1), (1, 0)])


def local(pair_rep, cotangent, norm_gain, proj_weight, bias_weight, out_weight, residue_mask):
    gain = norm_gain.reshape(1, CH)
    wbt = bias_weight.T
    wall = proj_weight.reshape(CH, 4, HEADS, DIM).transpose(2, 1, 3, 0).reshape(HEADS, CH, CH)
    masking = (residue_mask.astype(F32) - 1.0) * MASK_FILL
    masking = masking.reshape(N_WIDE, 2, HALF).transpose(1, 0, 2).reshape(LENGTH)
    masking = jnp.broadcast_to(masking[:, None], (LENGTH, CH))
    tile_f32 = pltpu.VMEM((TILE, CH), F32)
    half = DEVICES // 2

    send, normed, pair_here, gain, wbt = call(
        pre_kernel,
        [
            pltpu.VMEM((2, COLS, IN_ROWS, CH), BF),
            pltpu.VMEM((TILE, CH), BF),
            pltpu.VMEM((ROWS, COLS, CH), BF),
            pltpu.VMEM((1, CH), F32),
            pltpu.VMEM((HEADS, CH), BF),
        ],
        [
            pltpu.VMEM((ROWS, COLS, CH), BF),
            tile_f32,
            tile_f32,
            pltpu.SemaphoreType.DMA((4,)),
        ],
        hbm=True,
    )(*[pltpu.with_memory_space_constraint(a, pltpu.HBM) for a in (pair_rep, cotangent, gain, wbt)])
    own = backward(send.reshape(half, IN_ROWS, CH), 4)
    other = swap(own)
    keep, give = call(
        attention_kernel,
        [pltpu.VMEM((N_CHIP, N_NARROW, MID_ROWS, CH), BF)] * 2,
        [
            pltpu.VMEM((2, LENGTH, CH), F32),
            pltpu.VMEM((2, LENGTH, CH), F32),
            pltpu.VMEM((DEVICES * 8, CH), F32),
            pltpu.VMEM((CH, CH), F32),
            pltpu.VMEM((CH, CH), F32),
            pltpu.VMEM((2 * DIM, CH), F32),
        ],
    )(
        own.reshape(N_CHIP, N_NARROW, IN_ROWS, CH),
        other.reshape(N_CHIP, N_NARROW, IN_ROWS, CH),
        wall,
        out_weight,
        masking,
    )
    got = swap(give)
    mid = call(join_kernel, pltpu.VMEM((half, SUM_ROWS, CH), BF))(
        keep.reshape(half, MID_ROWS, CH), got.reshape(half, MID_ROWS, CH)
    )
    mid = backward(mid, 8).reshape(2, COLS, SUM_ROWS, CH)
    send, bias = call(reduce_kernel, [pltpu.VMEM((DEVICES * OUT_ROWS, CH), BF), pltpu.VMEM((8, TILE), BF)])(mid, normed)
    last = backward(send.reshape(DEVICES, OUT_ROWS, CH), 2, [(0, 1)])
    d_pair, grad_proj, grad_bias, grad_out, grad_gain = call(
        final_kernel,
        [
            shape(ROWS, COLS, CH),
            shape(CH, 4 * CH, dtype=F32),
            shape(HEADS, CH, dtype=F32),
            shape(CH, CH, dtype=F32),
            shape(1, CH, dtype=F32),
        ],
        [pltpu.VMEM((DEVICES * OUT_ROWS, CH), F32), tile_f32],
    )(last.reshape(DEVICES * OUT_ROWS, CH), mid, bias, pair_here, proj_weight, wbt, gain)
    return (d_pair, grad_proj, grad_bias.T, grad_out, grad_gain.reshape(CH))


def solution(mesh):
    cores = Mesh(mesh.devices.reshape(N_CHIP, 2, N_NARROW), BOTH)
    tile = P(("chip", "core"), "narrow", None)
    in_specs = (tile, tile, P(), P(), P(), P(), P())
    out_specs = (tile, P(), P(), P(), P())
    return jax.shard_map(local, mesh=cores, in_specs=in_specs, out_specs=out_specs, check_vma=False)
```
